32 devices in a mesh: ka: 4 (over y, x), ea: 8 (over z, core).
Axes of the slice: x: 2, y: 2, z: 4, core: 2. Of those that a mesh axis runs over, the one named last changes fastest.
Arguments:
- lesser_in: float32 [4, 8, 2, 2, 128, 128], P('ka', 'ea'), may hold values from -6 to 6
- greater_in: float32 [4, 8, 2, 2, 128, 128], P('ka', 'ea'), may hold values from -6 to 6
- h_diag: float32 [4, 2, 2, 128, 128], P('ka'), may hold values from -0.035 to 0.45, as said below
- coupling: float32 [4, 1, 2, 128, 128], P('ka'), may hold values from -0.024 to 0.024
- contact: float32 [4, 8, 2, 2, 128, 128], P('ka', 'ea'), may hold values from -0.6 to 0.6
- coulomb: float32 [2, 128, 128], replicated, may hold values from 0.5 to 1.5
- tiles: int32 [16], replicated, may hold values from 0 to 31, as said below
Outputs:
- lesser_out: float32 [4, 8, 2, 2, 128, 128], P('ka', 'ea')
- greater_out: float32 [4, 8, 2, 2, 128, 128], P('ka', 'ea')
The draws below stay inside these ranges and needn't reach their ends.
Inputs may be any that keep to these rules, and one draw needn't show every extreme that they name: The first 8 entries are the diagonal tiles 16 * b + 5 * r (r = 0 to 3) of each block b in order; then 4 distinct pairs, each an off-diagonal tile 16 * b + 4 * r + c with r < c followed by its transpose 16 * b + 4 * c + r. `h_diag`: every block is Hermitian: its real part is symmetric and its imaginary part antisymmetric.
All inputs are finite; a program needn't handle non-finite values.
Results may differ from the reference program's by a relative error of at most 0.0001.
Values sent between devices are 32-bit elements; how exact they have to be, the bound alone decides.
A program may use at most 128 MiB of HBM per device.

```python
import math
import jax
import jax.numpy as jnp
import numpy as np
from jax import lax

BS = 128
NB = 2
NPAIR = 4
NSTEPS = 2
NE = 8
NK = 4


def draw_h_diag(key, part):
    key = jax.random.fold_in(key, 11)
    key_list = jax.random.split(key, 3)
    dims_all = (NK, NB, BS, BS)
    raw_real = jax.random.normal(key_list[0], dims_all, jnp.float32)
    raw_imag = jax.random.normal(key_list[1], dims_all, jnp.float32)
    symmetric = jnp.clip((raw_real + jnp.swapaxes(raw_real, -1, -2)) * 0.70710678, -6.0, 6.0) * 0.0057
    antisym = jnp.clip((raw_imag - jnp.swapaxes(raw_imag, -1, -2)) * 0.70710678, -6.0, 6.0) * 0.0057
    onsite = jax.random.uniform(key_list[2], (NK, NB, BS), jnp.float32, 0.35, 0.45)
    identity = jnp.eye(BS, dtype=jnp.float32)
    real_part = symmetric * (1.0 - identity) + onsite[..., None] * identity
    return jnp.stack([real_part, antisym], axis=2).astype(jnp.float32)


def draw_tiles(key, part):
    key = jax.random.fold_in(key, 7)
    upper_list = []
    lower_list = []
    for blk_no in range(NB):
        for row_pos in range(4):
            for col_pos in range(row_pos + 1, 4):
                upper_list.append(16 * blk_no + 4 * row_pos + col_pos)
                lower_list.append(16 * blk_no + 4 * col_pos + row_pos)
    diag_list = [16 * blk_no + 5 * row_pos for blk_no in range(NB) for row_pos in range(4)]
    chosen = jax.random.permutation(key, len(upper_list))[:NPAIR]
    uppers = jnp.asarray(np.array(upper_list, np.int32))[chosen]
    lowers = jnp.asarray(np.array(lower_list, np.int32))[chosen]
    paired = jnp.stack([uppers, lowers], axis=1).reshape(-1)
    return jnp.concatenate([jnp.asarray(np.array(diag_list, np.int32)), paired]).astype(jnp.int32)


def level_of(key, shape, cuts, smallest, top_value):
    def one(axis_at, blocks):
        heights = jax.random.uniform(jax.random.fold_in(jax.random.fold_in(key, 6), axis_at), (blocks,), jnp.float32, smallest / len(cuts), top_value / len(cuts))
        return jnp.repeat(jnp.exp(heights), shape[axis_at] // blocks).reshape((-1,) + (1,) * (len(shape) - axis_at - 1))

    factor_of = one(*cuts[0])
    for cut in cuts[1:]:
        factor_of = factor_of * one(*cut)
    return factor_of


def scatter_about(key, shape, width, bound, cuts=(), kind=jnp.bfloat16):
    drawn = jax.random.normal(key, shape, jnp.float32) * width
    if len(cuts) > 0:
        drawn = level_of(key, shape, cuts, -0.22, 0.18) * drawn
    return jnp.clip(drawn, min=-bound, max=bound).astype(kind)


def setup_inputs(seed: int = 0) -> dict:
    seeds = jax.random.split(jax.random.key(seed), 8)
    lesser_in = scatter_about(seeds[0], (NK, NE, NB, 2, BS, BS), 1.0, 6.0, ((0, 4), (1, 8)), jnp.float32)
    greater_in = scatter_about(seeds[1], (NK, NE, NB, 2, BS, BS), 1.0, 6.0, ((0, 4), (1, 8)), jnp.float32)
    h_diag = draw_h_diag(jax.random.fold_in(seeds[7], 71), 0)
    coupling = scatter_about(seeds[3], (NK, NB - 1, 2, BS, BS), 0.004, 0.024, ((0, 4),), jnp.float32)
    contact = scatter_about(seeds[4], (NK, NE, 2, 2, BS, BS), 0.1, 0.6, ((0, 4), (1, 8)), jnp.float32)
    coulomb = jnp.clip(jnp.exp(jax.random.uniform(seeds[5], (NB, BS, BS), jnp.float32, math.log(0.5), math.log(1.5))), 0.5, 1.5)
    tiles = draw_tiles(jax.random.fold_in(seeds[7], 71), 0)
    return {"lesser_in": lesser_in, "greater_in": greater_in, "h_diag": h_diag, "coupling": coupling, "contact": contact, "coulomb": coulomb, "tiles": tiles}


BROADEN = 0.3
SPREAD = 0.05
SIGMA_SCALE = 0.01
PRECISE = lax.Precision.HIGHEST

def tiles_of(blocks):
    leading = blocks.shape[:-3]
    lead_rank = len(leading)
    block_count = blocks.shape[-3]
    tile_order = blocks.shape[-1] // 4
    viewed = blocks.reshape(leading + (block_count, 4, tile_order, 4, tile_order))
    viewed = jnp.moveaxis(viewed, lead_rank + 3, lead_rank + 2)
    return viewed.reshape(leading + (block_count * 16, tile_order, tile_order))

def blocks_of(pieces, block_count):
    leading = pieces.shape[:-3]
    lead_rank = len(leading)
    tile_order = pieces.shape[-1]
    viewed = pieces.reshape(leading + (block_count, 4, 4, tile_order, tile_order))
    viewed = jnp.moveaxis(viewed, lead_rank + 2, lead_rank + 3)
    return viewed.reshape(leading + (block_count, 4 * tile_order, 4 * tile_order))

def product(first, second):
    return jnp.matmul(first, second, precision=PRECISE)

def dagger(matrix):
    return jnp.conj(jnp.swapaxes(matrix, -1, -2))

def invert(matrix):
    identity = jnp.eye(matrix.shape[-1], dtype=matrix.dtype)
    approx = jnp.diag(1.0 / jnp.diagonal(matrix))
    for step_no in range(NSTEPS):
        approx = product(approx, 2.0 * identity - product(matrix, approx))
    return approx

def sweep(energy, diagonal, couple, sigma_ret, sigma_less):
    identity = jnp.eye(diagonal.shape[-1], dtype=diagonal.dtype)
    shifted = (energy + 1j * BROADEN) * identity
    forward_r = []
    forward_l = []
    for blk_no in range(NB):
        system = shifted - diagonal[blk_no] - sigma_ret[blk_no]
        source = sigma_less[blk_no]
        if blk_no > 0:
            link = couple[blk_no - 1]
            system = system - product(dagger(link), product(forward_r[-1], link))
            source = source + product(dagger(link), product(forward_l[-1], link))
        green_r = invert(system)
        forward_r.append(green_r)
        forward_l.append(product(product(green_r, source), dagger(green_r)))
    retarded_list = [forward_r[-1]]
    lesser_list = [forward_l[-1]]
    for blk_no in range(NB - 2, -1, -1):
        green_r = forward_r[blk_no]
        green_l = forward_l[blk_no]
        link = couple[blk_no]
        right_op = product(green_r, link)
        middle = product(right_op, retarded_list[0])
        new_r = green_r + product(middle, product(dagger(link), green_r))
        cross = product(middle, product(dagger(link), green_l))
        new_l = green_l + product(product(right_op, lesser_list[0]), dagger(right_op)) - cross - dagger(cross)
        retarded_list.insert(0, new_r)
        lesser_list.insert(0, new_l)
    retarded = jnp.stack(retarded_list)
    lesser = jnp.stack(lesser_list)
    return (lesser, lesser + retarded - dagger(retarded))

def reflect(spectrum):
    return jnp.concatenate([spectrum[:1], jnp.flip(spectrum[1:], axis=0)], axis=0)

def reference(lesser_in, greater_in, h_diag, coupling, contact, coulomb, tiles):
    length = 2 * NE
    scale_p = 1.0 / math.sqrt(NE)
    lesser_c = lesser_in[:, :, :, 0] + 1j * lesser_in[:, :, :, 1]
    greater_c = greater_in[:, :, :, 0] + 1j * greater_in[:, :, :, 1]

    def select(blocks):
        return jnp.take(tiles_of(blocks), tiles, axis=-3).reshape(blocks.shape[:-3] + (-1,))
    lesser_x = select(lesser_c)
    greater_x = select(greater_c)
    lesser_t = select(jnp.swapaxes(lesser_c, -1, -2))
    greater_t = select(jnp.swapaxes(greater_c, -1, -2))
    weight = select(coulomb) ** 2
    total_l = jnp.zeros((length, lesser_x.shape[-1]), dtype=lesser_x.dtype)
    total_g = jnp.zeros((length, lesser_x.shape[-1]), dtype=lesser_x.dtype)
    for k_index in range(NK):
        spec_l = jnp.fft.fft(lesser_x[k_index], n=length, axis=0)
        spec_g = jnp.fft.fft(greater_x[k_index], n=length, axis=0)
        spec_lt = jnp.fft.fft(lesser_t[k_index], n=length, axis=0)
        spec_gt = jnp.fft.fft(greater_t[k_index], n=length, axis=0)
        total_l = total_l + jnp.fft.ifft(spec_l * reflect(spec_gt), axis=0)
        total_g = total_g + jnp.fft.ifft(spec_g * reflect(spec_lt), axis=0)
    screened_l = weight * (-1j * scale_p) * total_l / NK
    screened_g = weight * (-1j * scale_p) * total_g / NK
    spec_wl = jnp.fft.fft(screened_l, axis=0)
    spec_wg = jnp.fft.fft(screened_g, axis=0)
    sigma_l_list = []
    sigma_g_list = []
    for k_index in range(NK):
        spec_l = jnp.fft.fft(lesser_x[k_index], n=length, axis=0)
        spec_g = jnp.fft.fft(greater_x[k_index], n=length, axis=0)
        sigma_l_list.append(1j * SIGMA_SCALE * scale_p * jnp.fft.ifft(spec_l * spec_wl, axis=0)[:NE])
        sigma_g_list.append(1j * SIGMA_SCALE * scale_p * jnp.fft.ifft(spec_g * spec_wg, axis=0)[:NE])
    tile_order = BS // 4

    def place(values):
        pieces = values.reshape((NK, NE, tiles.shape[0], tile_order, tile_order))
        empty = jnp.zeros((NK, NE, NB * 16, tile_order, tile_order), dtype=values.dtype)
        return blocks_of(empty.at[:, :, tiles, :, :].set(pieces), NB)
    sigma_less = place(jnp.stack(sigma_l_list))
    sigma_more = place(jnp.stack(sigma_g_list))
    sigma_ret = 0.5 * (sigma_more - sigma_less)
    contact_c = contact[:, :, :, 0] + 1j * contact[:, :, :, 1]
    sigma_less = sigma_less.at[:, :, 0].add(contact_c[:, :, 0])
    sigma_less = sigma_less.at[:, :, NB - 1].add(contact_c[:, :, 1])
    h_c = h_diag[:, :, 0] + 1j * h_diag[:, :, 1]
    couple_c = coupling[:, :, 0] + 1j * coupling[:, :, 1]
    energies = -SPREAD + 2.0 * SPREAD * (jnp.arange(NE, dtype=jnp.float32) + 0.5) / NE

    def per_momentum(inputs):
        diagonal, couple, sig_r, sig_l = inputs
        return jax.vmap(sweep, in_axes=(0, None, None, 0, 0))(energies, diagonal, couple, sig_r, sig_l)
    lesser, greater = lax.map(per_momentum, (h_c, couple_c, sigma_ret, sigma_less))
    lesser_out = jnp.stack([jnp.real(lesser), jnp.imag(lesser)], axis=3)
    greater_out = jnp.stack([jnp.real(greater), jnp.imag(greater)], axis=3)
    return (lesser_out, greater_out)
```

```python
import math
from functools import partial

import jax
import jax.numpy as jnp
import numpy as np
from jax import lax
from jax.experimental import pallas as pl
from jax.experimental.pallas import tpu as pltpu
from jax.sharding import PartitionSpec as P

BROADEN = 0.3
SPREAD = 0.05
SIGMA_SCALE = 0.01
PRECISE = lax.Precision.HIGHEST


def tiles_of(blocks):
    leading = blocks.shape[:-3]
    lead_rank = len(leading)
    block_count = blocks.shape[-3]
    tile_order = blocks.shape[-1] // 4
    viewed = blocks.reshape(leading + (block_count, 4, tile_order, 4, tile_order))
    viewed = jnp.moveaxis(viewed, lead_rank + 3, lead_rank + 2)
    return viewed.reshape(leading + (block_count * 16, tile_order, tile_order))


def blocks_of(pieces, block_count):
    leading = pieces.shape[:-3]
    lead_rank = len(leading)
    tile_order = pieces.shape[-1]
    viewed = pieces.reshape(leading + (block_count, 4, 4, tile_order, tile_order))
    viewed = jnp.moveaxis(viewed, lead_rank + 2, lead_rank + 3)
    return viewed.reshape(leading + (block_count, 4 * tile_order, 4 * tile_order))


def diag_order(tile_order):
    listing = [row_pos * tile_order + row_pos for row_pos in range(tile_order)]
    for row_pos in range(tile_order):
        for col_pos in range(row_pos + 1, tile_order):
            listing.append(row_pos * tile_order + col_pos)
            listing.append(col_pos * tile_order + row_pos)
    forward = np.array(listing, np.int32)
    return (forward, np.argsort(forward).astype(np.int32))


def arrange(pieces, diag_count):
    leading = pieces.shape[:-3]
    tile_order = pieces.shape[-1]
    forward = diag_order(tile_order)[0]
    diagonal = pieces[..., :diag_count, :, :].reshape(
        leading + (diag_count, tile_order * tile_order)
    )
    diagonal = jnp.take(diagonal, forward, axis=-1).reshape(leading + (-1,))
    paired = pieces[..., diag_count:, :, :].reshape(leading + (-1, 2, tile_order, tile_order))
    paired = jnp.stack([paired[..., 0, :, :], jnp.swapaxes(paired[..., 1, :, :], -1, -2)], axis=-1)
    return jnp.concatenate([diagonal, paired.reshape(leading + (-1,))], axis=-1)


def unarrange(flattened, diag_count, tile_order):
    leading = flattened.shape[:-1]
    square = tile_order * tile_order
    inverse = diag_order(tile_order)[1]
    diagonal = flattened[..., : diag_count * square].reshape(leading + (diag_count, square))
    diagonal = jnp.take(diagonal, inverse, axis=-1).reshape(
        leading + (diag_count, tile_order, tile_order)
    )
    paired = flattened[..., diag_count * square :].reshape(
        leading + (-1, tile_order, tile_order, 2)
    )
    paired = jnp.stack([paired[..., 0], jnp.swapaxes(paired[..., 1], -1, -2)], axis=-3)
    paired = paired.reshape(leading + (-1, tile_order, tile_order))
    return jnp.concatenate([diagonal, paired], axis=-3)


def partner(flattened, diag_count, tile_order):
    size_last = flattened.shape[-1]
    square = tile_order * tile_order
    flipped = flattened.reshape(flattened.shape[:-1] + (size_last // 2, 2))[..., ::-1].reshape(
        flattened.shape
    )
    position = jnp.arange(size_last, dtype=jnp.int32)
    itself = (position < diag_count * square) & (position % square < tile_order)
    return jnp.where(itself, flattened, flipped)


def tables(rows_count, cols_count, length):
    phases = (
        jnp.arange(rows_count, dtype=jnp.int32)[:, None]
        * jnp.arange(cols_count, dtype=jnp.int32)[None, :]
        % length
    )
    angles = phases.astype(jnp.float32) * (2.0 * math.pi / length)
    return (jnp.cos(angles), jnp.sin(angles))


def apply_table(coeffs, values):
    return jnp.einsum("fe,keal->kfal", coeffs, values, precision=PRECISE)


def transform(series, cosine, sine, sign, factor):
    real_in = series[..., 0, :]
    imag_in = series[..., 1, :]
    real_out = apply_table(cosine, real_in) + sign * apply_table(sine, imag_in)
    imag_out = apply_table(cosine, imag_in) - sign * apply_table(sine, real_in)
    return jnp.stack([real_out, imag_out], axis=-2) * factor


def pair_prod(first, second):
    first_re = first[..., 0, :]
    first_im = first[..., 1, :]
    second_re = second[..., 0, :]
    second_im = second[..., 1, :]
    return jnp.stack(
        [first_re * second_re - first_im * second_im, first_re * second_im + first_im * second_re],
        axis=-2,
    )


def pair_mul(first, second):
    products = jnp.einsum("bsij,btjk->bstik", first, second, precision=PRECISE)
    return jnp.stack(
        [products[:, 0, 0] - products[:, 1, 1], products[:, 0, 1] + products[:, 1, 0]], axis=1
    )


def dagger(matrix):
    swapped = jnp.swapaxes(matrix, -1, -2)
    return jnp.stack([swapped[:, 0], -swapped[:, 1]], axis=1)


def newton(system, twice_eye):
    real_d = jnp.diagonal(system[:, 0], axis1=-2, axis2=-1)
    imag_d = jnp.diagonal(system[:, 1], axis1=-2, axis2=-1)
    denominator = real_d * real_d + imag_d * imag_d
    inverse_re = real_d / denominator
    inverse_im = -imag_d / denominator
    scaled_re = system[:, 0] * inverse_re[:, None, :] - system[:, 1] * inverse_im[:, None, :]
    scaled_im = system[:, 0] * inverse_im[:, None, :] + system[:, 1] * inverse_re[:, None, :]
    inner_re = twice_eye[:, 0] - scaled_re
    inner_im = -scaled_im
    approx = jnp.stack(
        [
            inverse_re[:, :, None] * inner_re - inverse_im[:, :, None] * inner_im,
            inverse_re[:, :, None] * inner_im + inverse_im[:, :, None] * inner_re,
        ],
        axis=1,
    )
    approx = pair_mul(approx, twice_eye - pair_mul(system, approx))
    return approx


def polar_terms(direct, mirrored, scale_p):
    reflected = jnp.concatenate([mirrored[:, :1], jnp.flip(mirrored[:, 1:], axis=1)], axis=1)
    correlated = pair_prod(direct, reflected[:, :, ::-1])
    return jnp.stack([correlated[..., 1, :], -correlated[..., 0, :]], axis=-2) * scale_p


def self_energy(direct, screened, out_cos, out_sin, length, scale_p):
    convolved = transform(pair_prod(direct, screened), out_cos, out_sin, -1.0, 1.0 / length)
    return jnp.stack([-convolved[..., 1, :], convolved[..., 0, :]], axis=-2) * (
        SIGMA_SCALE * scale_p
    )


def on_device(lesser_in, greater_in, h_diag, coupling, contact, coulomb, tiles):
    k_local = lesser_in.shape[0]
    e_local = lesser_in.shape[1]
    block_count = lesser_in.shape[2]
    order_n = lesser_in.shape[-1]
    tile_order = order_n // 4
    diag_count = 4 * block_count
    devices_e = lax.axis_size("ea")
    devices_k = lax.axis_size("ka")
    e_total = e_local * devices_e
    length = 2 * e_total
    ret_local = tiles.shape[0] * tile_order * tile_order // devices_e
    offset = lax.axis_index("ea") * ret_local
    k_total = k_local * devices_k
    scale_p = 1.0 / math.sqrt(e_total)

    def layout(blocks):
        return arrange(jnp.take(tiles_of(jnp.moveaxis(blocks, 3, 2)), tiles, axis=-3), diag_count)

    greens = jnp.stack([layout(lesser_in), layout(greater_in)], axis=2)
    fwd_cos, fwd_sin = tables(length, e_total, length)
    full_cos, full_sin = tables(length, length, length)
    out_cos, out_sin = tables(e_total, length, length)
    coulomb_flat = arrange(jnp.take(tiles_of(coulomb), tiles, axis=-3), diag_count)
    outgoing = jnp.concatenate([greens, partner(greens, diag_count, tile_order)], axis=2)
    spectra = transform(
        lax.all_to_all(outgoing, "ea", split_axis=4, concat_axis=1, tiled=True),
        fwd_cos,
        fwd_sin,
        1.0,
        1.0,
    )
    direct = spectra[:, :, :2]
    mirrored = spectra[:, :, 2:]
    turned = polar_terms(direct, mirrored, scale_p)
    weight = lax.dynamic_slice_in_dim(coulomb_flat, offset, ret_local) ** 2
    lags = transform(jnp.sum(turned, axis=0, keepdims=True), full_cos, full_sin, -1.0, 1.0 / length)
    summed = lax.psum(lags, "ka")
    screened = transform(summed * (weight / k_total), full_cos, full_sin, 1.0, 1.0)
    sigma = self_energy(direct, screened, out_cos, out_sin, length, scale_p)
    returned = lax.all_to_all(sigma, "ea", split_axis=1, concat_axis=4, tiled=True)
    pieces = unarrange(returned, diag_count, tile_order)
    empty = jnp.zeros(pieces.shape[:-3] + (block_count * 16, tile_order, tile_order), jnp.float32)
    sigma_blocks = blocks_of(empty.at[..., tiles, :, :].set(pieces), block_count)
    sigma_ret = 0.5 * (sigma_blocks[:, :, 1] - sigma_blocks[:, :, 0])
    sigma_less = sigma_blocks[:, :, 0]
    batch = k_local * e_local
    identity = jnp.eye(order_n, dtype=jnp.float32)
    energy_idx = lax.axis_index("ea") * e_local + jnp.arange(e_local, dtype=jnp.int32)
    energies = -SPREAD + 2.0 * SPREAD * (energy_idx.astype(jnp.float32) + 0.5) / e_total
    energies = energies[None, :].reshape(batch)
    shifted = jnp.stack(
        [
            energies[:, None, None] * identity,
            jnp.broadcast_to(BROADEN * identity, (batch, order_n, order_n)),
        ],
        axis=1,
    )
    twice_eye = jnp.broadcast_to(
        jnp.stack([2.0 * identity, 0.0 * identity]), (batch, 2, order_n, order_n)
    )

    def per_energy(array_k):
        return array_k[:, None].reshape((batch,) + array_k.shape[1:])

    forward_r = []
    forward_l = []
    for blk_no in range(block_count):
        system = (
            shifted
            - per_energy(h_diag[:, blk_no])
            - sigma_ret[:, :, :, blk_no].reshape(batch, 2, order_n, order_n)
        )
        source = sigma_less[:, :, :, blk_no].reshape(batch, 2, order_n, order_n)
        if blk_no == 0:
            source = source + contact[:, :, 0].reshape(batch, 2, order_n, order_n)
        if blk_no == block_count - 1:
            source = source + contact[:, :, 1].reshape(batch, 2, order_n, order_n)
        if blk_no > 0:
            link = per_energy(coupling[:, blk_no - 1])
            system = system - pair_mul(dagger(link), pair_mul(forward_r[-1], link))
            source = source + pair_mul(dagger(link), pair_mul(forward_l[-1], link))
        green_r = newton(system, twice_eye)
        forward_r.append(green_r)
        forward_l.append(pair_mul(pair_mul(green_r, source), dagger(green_r)))
    retarded_list = [forward_r[-1]]
    lesser_list = [forward_l[-1]]
    blk_no = 0
    green_r = forward_r[blk_no]
    green_l = forward_l[blk_no]
    link = per_energy(coupling[:, blk_no])
    right_op = pair_mul(green_r, link)
    middle = pair_mul(right_op, retarded_list[0])
    new_r = green_r + pair_mul(middle, pair_mul(dagger(link), green_r))
    cross = pair_mul(middle, pair_mul(dagger(link), green_l))
    new_l = (
        green_l
        + pair_mul(pair_mul(right_op, lesser_list[0]), dagger(right_op))
        - cross
        - dagger(cross)
    )
    retarded_list.insert(0, new_r)
    lesser_list.insert(0, new_l)
    lesser = jnp.stack(lesser_list, axis=1)
    greater = jnp.stack(
        [
            lesser_list[blk_no] + retarded_list[blk_no] - dagger(retarded_list[blk_no])
            for blk_no in range(block_count)
        ],
        axis=1,
    )
    out_shape = (k_local, e_local, block_count, 2, order_n, order_n)
    return (lesser.reshape(out_shape), greater.reshape(out_shape))


MESH = pl.DeviceIdType.MESH
VMEM = pl.BlockSpec(memory_space=pltpu.VMEM)
SMEM = pl.BlockSpec(memory_space=pltpu.SMEM)


def half_swap(rows):
    return pltpu.roll(rows, 4, rows.ndim - 2)


def upper_half(shape):
    return lax.broadcasted_iota(jnp.int32, shape, len(shape) - 2) % 8 < 4


def tile_place(tiles_ref, slot):
    tile = tiles_ref[slot]
    return tile // 16, tile % 16 // 4, tile % 4


def pack_tiles(tiles_ref, load):
    group = lax.broadcasted_iota(jnp.int32, (32, 128), 1) // 32
    parts = []
    for blk in range(2):
        part = load(blk, 0)
        for pos in range(1, 4):
            part = jnp.where(group == pos, load(blk, 32 * pos), part)
        parts.append(part)
    for half in range(2):
        part = None
        for pos in range(4):
            blk, row, col = tile_place(tiles_ref, 8 + 4 * half + pos)
            slab = load(blk, pl.multiple_of(32 * row, 32))
            slab = pltpu.roll(slab, (pos + 4 - col) % 4 * 32, 1)
            part = slab if part is None else jnp.where(group == pos, slab, part)
        parts.append(part)
    return jnp.concatenate(parts, axis=0).reshape(16, 8, 128)


def pack_kernel(tiles_ref, l_ref, g_ref, c_ref, out_ref, weight_ref, gt_ref, ct_ref):
    top = upper_half((16, 8, 128))
    for blk in range(2):
        ct_ref[blk] = c_ref[blk].T
        for part in range(2):
            gt_ref[blk, part] = g_ref[blk, part].T
    for kind, ref in ((0, l_ref), (1, gt_ref)):
        real = pack_tiles(tiles_ref, lambda blk, row: ref[blk, 0, pl.ds(row, 32), :])
        imag = pack_tiles(tiles_ref, lambda blk, row: ref[blk, 1, pl.ds(row, 32), :])
        out_ref[:, 0, kind] = jnp.where(top, real, half_swap(imag))
        out_ref[:, 1, kind] = jnp.where(top, half_swap(real), imag)
    for kind, ref in ((0, c_ref), (1, ct_ref)):
        bare = pack_tiles(tiles_ref, lambda blk, row: ref[blk, pl.ds(row, 32), :])
        bare = bare * bare
        weight_ref[:, 0, kind] = jnp.where(top, bare, half_swap(bare))
        weight_ref[:, 1, kind] = jnp.where(top, half_swap(bare), bare)


def exchange_kernel(
    n_k, n_e, send_ref, weight_ref, out_ref, held, sigma, back, send_a, recv_a, send_b, recv_b
):
    count = n_k * n_e
    me = lax.axis_index("ka") * n_e + lax.axis_index("ea")

    def place(other):
        return {"ka": other // n_e, "ea": other % n_e}

    def forward(other):
        return pltpu.make_async_remote_copy(
            src_ref=send_ref.at[other],
            dst_ref=held.at[me],
            send_sem=send_a.at[other],
            recv_sem=recv_a.at[me],
            device_id=place(other),
            device_id_type=MESH,
        )

    def arrival(other):
        return pltpu.make_async_remote_copy(
            src_ref=send_ref.at[other],
            dst_ref=held.at[other],
            send_sem=send_a.at[other],
            recv_sem=recv_a.at[other],
            device_id=place(other),
            device_id_type=MESH,
        )

    def backward(other):
        return pltpu.make_async_remote_copy(
            src_ref=sigma.at[other],
            dst_ref=back.at[me],
            send_sem=send_b.at[other],
            recv_sem=recv_b.at[me],
            device_id=place(other),
            device_id_type=MESH,
        )

    def returned(other):
        return pltpu.make_async_remote_copy(
            src_ref=sigma.at[other],
            dst_ref=back.at[other],
            send_sem=send_b.at[other],
            recv_sem=recv_b.at[other],
            device_id=place(other),
            device_id_type=MESH,
        )

    def others(body):
        def step(index, carry):
            body((me + index) % count)
            return carry

        lax.fori_loop(1, count, step, 0)

    barrier = pltpu.get_barrier_semaphore()
    others(
        lambda other: pl.semaphore_signal(
            barrier, inc=1, device_id=place(other), device_id_type=MESH
        )
    )
    pl.semaphore_wait(barrier, count - 1)
    others(lambda other: forward(other).start())
    held[me] = send_ref[me]
    others(lambda other: arrival(other).wait_recv())

    lags = 2 * n_e - 1

    def correlate(k_index, sums):
        plain, crossed = list(sums[0]), list(sums[1])
        lesser = [held[k_index * n_e + e, 0] for e in range(n_e)]
        greater = [held[k_index * n_e + e, 1] for e in range(n_e)]
        for e_two in range(n_e):
            swapped = half_swap(greater[e_two])
            for e_one in range(n_e):
                lag = e_one - e_two + n_e - 1
                plain[lag] = plain[lag] + lesser[e_one] * greater[e_two]
                crossed[lag] = crossed[lag] + lesser[e_one] * swapped
        return tuple(plain), tuple(crossed)

    zero = jnp.zeros((8, 128), jnp.float32)
    plain, crossed = lax.fori_loop(0, n_k, correlate, ((zero,) * lags, (zero,) * lags))
    sign = jnp.where(upper_half((8, 128)), 1.0, -1.0)
    scale = SIGMA_SCALE / (n_e * n_k)
    weight_l = weight_ref[me, 0] * scale
    weight_g = weight_ref[me, 1] * scale
    real = [sign * (total - half_swap(total)) for total in plain]
    imag = [-sign * (total + half_swap(total)) for total in crossed]

    def convolve(k_index, carry):
        first = k_index * n_e
        for kind, weight in ((0, weight_l), (1, weight_g)):
            green = [held[first + e, kind] for e in range(n_e)]
            swapped = [half_swap(piece) for piece in green]
            for e_out in range(n_e):
                total = None
                for e_in in range(n_e):
                    lag = e_out - e_in if kind == 0 else e_in - e_out
                    lag = lag + n_e - 1
                    term = green[e_in] * real[lag] + swapped[e_in] * imag[lag]
                    total = term if total is None else total + term
                sigma[first + e_out, kind] = total * weight

        def send(e_out, inner):
            @pl.when(first + e_out != me)
            def _():
                backward(first + e_out).start()

            return inner

        lax.fori_loop(0, n_e, send, 0)
        return carry

    lax.fori_loop(0, n_k, convolve, 0)
    back[me] = sigma[me]
    others(lambda other: returned(other).wait_recv())
    out_ref[...] = back[...]
    others(lambda other: forward(other).wait_send())
    others(lambda other: backward(other).wait_send())


def split(value):
    high = value.astype(jnp.bfloat16)
    return high, (value - high.astype(jnp.float32)).astype(jnp.bfloat16)


def square_form(rows):
    real, imag = rows[:, :128], rows[:, 128:]
    return split(jnp.concatenate([rows, jnp.concatenate([-imag, real], axis=1)], axis=0))


def times(first, second, contract=0):
    dims = (((1,), (contract,)), ((), ()))

    def dot(left, right):
        return lax.dot_general(left, right, dims, preferred_element_type=jnp.float32)

    high, low = first
    return dot(high, second[0]) + (dot(high, second[1]) + dot(low, second[0]))


def adjoint(rows):
    return jnp.concatenate([rows[:, :128].T, -rows[:, 128:].T], axis=1)


def invert_rows(system, eye):
    real_m, imag_m = system[:, :128], system[:, 128:]
    only_re = jnp.where(eye, real_m, 0.0)
    only_im = jnp.where(eye, imag_m, 0.0)

    def reciprocal(axis):
        real_d = jnp.sum(only_re, axis=axis, keepdims=True)
        imag_d = jnp.sum(only_im, axis=axis, keepdims=True)
        denominator = real_d * real_d + imag_d * imag_d
        return real_d / denominator, -imag_d / denominator

    row_re, row_im = reciprocal(0)
    col_re, col_im = reciprocal(1)
    twice = jnp.where(eye, 2.0, 0.0)
    inner_re = twice - (real_m * row_re - imag_m * row_im)
    inner_im = -(real_m * row_im + imag_m * row_re)
    approx = jnp.concatenate(
        [col_re * inner_re - col_im * inner_im, col_re * inner_im + col_im * inner_re], axis=1
    )
    product = times(split(system), square_form(approx))
    rest = jnp.concatenate([twice - product[:, :128], -product[:, 128:]], axis=1)
    return times(split(approx), square_form(rest))


def sweep_kernel(
    tiles_ref, energy_ref, sigma_ref, h_ref, link_ref, contact_ref, lesser_ref, greater_ref, blocks
):
    top = upper_half((16, 8, 128))
    group = lax.broadcasted_iota(jnp.int32, (32, 128), 1) // 32
    for kind in range(2):
        first, second = sigma_ref[:, 0, kind], sigma_ref[:, 1, kind]
        parts = (
            jnp.where(top, first, half_swap(second)),
            jnp.where(top, half_swap(first), second),
        )
        for part in range(2):
            packed = parts[part].reshape(128, 128)
            for blk in range(2):
                for pos in range(4):
                    blocks[kind, part, blk, 32 * pos : 32 * pos + 32, :] = jnp.where(
                        group == pos, packed[32 * blk : 32 * blk + 32], 0.0
                    )
            for slot in range(8):
                blk, row, col = tile_place(tiles_ref, 8 + slot)
                start = 64 + 32 * (slot // 4)
                slab = pltpu.roll(packed[start : start + 32], (col + 4 - slot % 4) % 4 * 32, 1)
                rows = pl.ds(pl.multiple_of(32 * row, 32), 32)
                blocks[kind, part, blk, rows, :] = jnp.where(
                    group == col, slab, blocks[kind, part, blk, rows, :]
                )

    eye = lax.broadcasted_iota(jnp.int32, (128, 128), 0) == lax.broadcasted_iota(
        jnp.int32, (128, 128), 1
    )
    shift = jnp.concatenate(
        [jnp.where(eye, energy_ref[0], 0.0), jnp.where(eye, BROADEN, 0.0)], axis=1
    )

    def rows_of(ref, *index):
        return jnp.concatenate([ref[*index, 0], ref[*index, 1]], axis=1)

    def system_source(blk):
        less = jnp.concatenate([blocks[0, 0, blk], blocks[0, 1, blk]], axis=1)
        more = jnp.concatenate([blocks[1, 0, blk].T, blocks[1, 1, blk].T], axis=1)
        system = shift - rows_of(h_ref, blk) - 0.5 * (more - less)
        return system, less + rows_of(contact_ref, blk)

    link = rows_of(link_ref, 0)
    link_square = square_form(link)
    link_adjoint = split(adjoint(link))

    system_0, source_0 = system_source(0)
    system_1, source_1 = system_source(1)
    gr_0 = invert_rows(system_0, eye)
    gr_0_rows, gr_0_square = split(gr_0), square_form(gr_0)
    right_op = times(gr_0_rows, link_square)
    right_square = square_form(right_op)
    system_1 = system_1 - times(link_adjoint, right_square)
    gr_1 = invert_rows(system_1, eye)
    gl_0 = times(split(times(gr_0_rows, square_form(source_0))), gr_0_square, 1)
    left_l = times(link_adjoint, square_form(gl_0))
    source_1 = source_1 + times(split(left_l), link_square)
    gr_1_square = square_form(gr_1)
    gl_1 = times(split(times(split(gr_1), square_form(source_1))), gr_1_square, 1)
    left_r = times(link_adjoint, gr_0_square)
    right_rows = split(right_op)
    middle = split(times(right_rows, gr_1_square))
    full_r = gr_0 + times(middle, square_form(left_r))
    cross = times(middle, square_form(left_l))
    inner = times(split(times(right_rows, square_form(gl_1))), right_square, 1)
    full_l = gl_0 + inner - cross - adjoint(cross)
    for blk, retarded, lesser in ((0, full_r, full_l), (1, gr_1, gl_1)):
        greater = lesser + retarded - adjoint(retarded)
        for part in range(2):
            lesser_ref[blk, part] = lesser[:, 128 * part : 128 * part + 128]
            greater_ref[blk, part] = greater[:, 128 * part : 128 * part + 128]


def small_device(n_k, n_e, lesser_in, greater_in, h_diag, coupling, contact, coulomb, tiles):
    count = n_k * n_e
    f32 = jnp.float32
    limit = pltpu.CompilerParams(vmem_limit_bytes=32 * 1024 * 1024)
    packed, weight = pl.pallas_call(
        pack_kernel,
        out_shape=(jax.ShapeDtypeStruct((16, 2, 2, 8, 128), f32),) * 2,
        in_specs=[SMEM, VMEM, VMEM, VMEM],
        out_specs=(VMEM, VMEM),
        scratch_shapes=[pltpu.VMEM((2, 2, 128, 128), f32), pltpu.VMEM((2, 128, 128), f32)],
        compiler_params=limit,
        name="pack",
    )(tiles, lesser_in[0, 0], greater_in[0, 0], coulomb)
    slots = (count, 2, 8, 128)
    sigma = pl.pallas_call(
        partial(exchange_kernel, n_k, n_e),
        out_shape=jax.ShapeDtypeStruct(slots, f32),
        in_specs=[VMEM, VMEM],
        out_specs=VMEM,
        scratch_shapes=[pltpu.VMEM(slots, f32)] * 3 + [pltpu.SemaphoreType.DMA((count,))] * 4,
        compiler_params=pltpu.CompilerParams(
            collective_id=0, has_side_effects=True, vmem_limit_bytes=32 * 1024 * 1024
        ),
        name="exchange",
    )(packed.reshape(slots), weight.reshape(slots))
    energy = -SPREAD + 2.0 * SPREAD * (lax.axis_index("ea").astype(f32) + 0.5) / n_e
    lesser, greater = pl.pallas_call(
        sweep_kernel,
        out_shape=(jax.ShapeDtypeStruct((2, 2, 128, 128), f32),) * 2,
        in_specs=[SMEM, SMEM, VMEM, VMEM, VMEM, VMEM],
        out_specs=(VMEM, VMEM),
        scratch_shapes=[pltpu.VMEM((2, 2, 2, 128, 128), f32)],
        compiler_params=limit,
        name="sweep",
    )(
        tiles,
        energy.reshape(1),
        sigma.reshape(16, 2, 2, 8, 128),
        h_diag[0],
        coupling[0],
        contact[0, 0],
    )
    return lesser[None, None], greater[None, None]


def per_device(mesh, lesser_in, *rest):
    n_k, n_e = mesh.shape["ka"], mesh.shape["ea"]
    fits = n_k * n_e == 32 and lesser_in.shape == (1, 1, 2, 2, 128, 128) and rest[-1].shape == (16,)
    if fits:
        return small_device(n_k, n_e, lesser_in, *rest)
    return on_device(lesser_in, *rest)


def solution(mesh):
    in_specs = (
        P("ka", "ea", None, None, None, None),
        P("ka", "ea", None, None, None, None),
        P("ka", None, None, None, None),
        P("ka", None, None, None, None),
        P("ka", "ea", None, None, None, None),
        P(),
        P(),
    )
    out_specs = (P("ka", "ea", None, None, None, None), P("ka", "ea", None, None, None, None))
    return jax.shard_map(
        partial(per_device, mesh), mesh=mesh, in_specs=in_specs, out_specs=out_specs, check_vma=False
    )
```

```python
import math
from functools import partial

import jax
import jax.numpy as jnp
import numpy as np
from jax import lax
from jax.experimental import pallas as pl
from jax.experimental.pallas import tpu as pltpu
from jax.sharding import PartitionSpec as P

BROADEN = 0.3
SPREAD = 0.05
SIGMA_SCALE = 0.01
PRECISE = lax.Precision.HIGHEST


def tiles_of(blocks):
    leading = blocks.shape[:-3]
    lead_rank = len(leading)
    block_count = blocks.shape[-3]
    tile_order = blocks.shape[-1] // 4
    viewed = blocks.reshape(leading + (block_count, 4, tile_order, 4, tile_order))
    viewed = jnp.moveaxis(viewed, lead_rank + 3, lead_rank + 2)
    return viewed.reshape(leading + (block_count * 16, tile_order, tile_order))


def blocks_of(pieces, block_count):
    leading = pieces.shape[:-3]
    lead_rank = len(leading)
    tile_order = pieces.shape[-1]
    viewed = pieces.reshape(leading + (block_count, 4, 4, tile_order, tile_order))
    viewed = jnp.moveaxis(viewed, lead_rank + 2, lead_rank + 3)
    return viewed.reshape(leading + (block_count, 4 * tile_order, 4 * tile_order))


def diag_order(tile_order):
    listing = [row_pos * tile_order + row_pos for row_pos in range(tile_order)]
    for row_pos in range(tile_order):
        for col_pos in range(row_pos + 1, tile_order):
            listing.append(row_pos * tile_order + col_pos)
            listing.append(col_pos * tile_order + row_pos)
    forward = np.array(listing, np.int32)
    return (forward, np.argsort(forward).astype(np.int32))


def arrange(pieces, diag_count):
    leading = pieces.shape[:-3]
    tile_order = pieces.shape[-1]
    forward = diag_order(tile_order)[0]
    diagonal = pieces[..., :diag_count, :, :].reshape(
        leading + (diag_count, tile_order * tile_order)
    )
    diagonal = jnp.take(diagonal, forward, axis=-1).reshape(leading + (-1,))
    paired = pieces[..., diag_count:, :, :].reshape(leading + (-1, 2, tile_order, tile_order))
    paired = jnp.stack([paired[..., 0, :, :], jnp.swapaxes(paired[..., 1, :, :], -1, -2)], axis=-1)
    return jnp.concatenate([diagonal, paired.reshape(leading + (-1,))], axis=-1)


def unarrange(flattened, diag_count, tile_order):
    leading = flattened.shape[:-1]
    square = tile_order * tile_order
    inverse = diag_order(tile_order)[1]
    diagonal = flattened[..., : diag_count * square].reshape(leading + (diag_count, square))
    diagonal = jnp.take(diagonal, inverse, axis=-1).reshape(
        leading + (diag_count, tile_order, tile_order)
    )
    paired = flattened[..., diag_count * square :].reshape(
        leading + (-1, tile_order, tile_order, 2)
    )
    paired = jnp.stack([paired[..., 0], jnp.swapaxes(paired[..., 1], -1, -2)], axis=-3)
    paired = paired.reshape(leading + (-1, tile_order, tile_order))
    return jnp.concatenate([diagonal, paired], axis=-3)


def partner(flattened, diag_count, tile_order):
    size_last = flattened.shape[-1]
    square = tile_order * tile_order
    flipped = flattened.reshape(flattened.shape[:-1] + (size_last // 2, 2))[..., ::-1].reshape(
        flattened.shape
    )
    position = jnp.arange(size_last, dtype=jnp.int32)
    itself = (position < diag_count * square) & (position % square < tile_order)
    return jnp.where(itself, flattened, flipped)


def tables(rows_count, cols_count, length):
    phases = (
        jnp.arange(rows_count, dtype=jnp.int32)[:, None]
        * jnp.arange(cols_count, dtype=jnp.int32)[None, :]
        % length
    )
    angles = phases.astype(jnp.float32) * (2.0 * math.pi / length)
    return (jnp.cos(angles), jnp.sin(angles))


def apply_table(coeffs, values):
    return jnp.einsum("fe,keal->kfal", coeffs, values, precision=PRECISE)


def transform(series, cosine, sine, sign, factor):
    real_in = series[..., 0, :]
    imag_in = series[..., 1, :]
    real_out = apply_table(cosine, real_in) + sign * apply_table(sine, imag_in)
    imag_out = apply_table(cosine, imag_in) - sign * apply_table(sine, real_in)
    return jnp.stack([real_out, imag_out], axis=-2) * factor


def pair_prod(first, second):
    first_re = first[..., 0, :]
    first_im = first[..., 1, :]
    second_re = second[..., 0, :]
    second_im = second[..., 1, :]
    return jnp.stack(
        [first_re * second_re - first_im * second_im, first_re * second_im + first_im * second_re],
        axis=-2,
    )


def pair_mul(first, second):
    products = jnp.einsum("bsij,btjk->bstik", first, second, precision=PRECISE)
    return jnp.stack(
        [products[:, 0, 0] - products[:, 1, 1], products[:, 0, 1] + products[:, 1, 0]], axis=1
    )


def dagger(matrix):
    swapped = jnp.swapaxes(matrix, -1, -2)
    return jnp.stack([swapped[:, 0], -swapped[:, 1]], axis=1)


def newton(system, twice_eye):
    real_d = jnp.diagonal(system[:, 0], axis1=-2, axis2=-1)
    imag_d = jnp.diagonal(system[:, 1], axis1=-2, axis2=-1)
    denominator = real_d * real_d + imag_d * imag_d
    inverse_re = real_d / denominator
    inverse_im = -imag_d / denominator
    scaled_re = system[:, 0] * inverse_re[:, None, :] - system[:, 1] * inverse_im[:, None, :]
    scaled_im = system[:, 0] * inverse_im[:, None, :] + system[:, 1] * inverse_re[:, None, :]
    inner_re = twice_eye[:, 0] - scaled_re
    inner_im = -scaled_im
    approx = jnp.stack(
        [
            inverse_re[:, :, None] * inner_re - inverse_im[:, :, None] * inner_im,
            inverse_re[:, :, None] * inner_im + inverse_im[:, :, None] * inner_re,
        ],
        axis=1,
    )
    approx = pair_mul(approx, twice_eye - pair_mul(system, approx))
    return approx


def polar_terms(direct, mirrored, scale_p):
    reflected = jnp.concatenate([mirrored[:, :1], jnp.flip(mirrored[:, 1:], axis=1)], axis=1)
    correlated = pair_prod(direct, reflected[:, :, ::-1])
    return jnp.stack([correlated[..., 1, :], -correlated[..., 0, :]], axis=-2) * scale_p


def self_energy(direct, screened, out_cos, out_sin, length, scale_p):
    convolved = transform(pair_prod(direct, screened), out_cos, out_sin, -1.0, 1.0 / length)
    return jnp.stack([-convolved[..., 1, :], convolved[..., 0, :]], axis=-2) * (
        SIGMA_SCALE * scale_p
    )


def on_device(lesser_in, greater_in, h_diag, coupling, contact, coulomb, tiles):
    k_local = lesser_in.shape[0]
    e_local = lesser_in.shape[1]
    block_count = lesser_in.shape[2]
    order_n = lesser_in.shape[-1]
    tile_order = order_n // 4
    diag_count = 4 * block_count
    devices_e = lax.axis_size("ea")
    devices_k = lax.axis_size("ka")
    e_total = e_local * devices_e
    length = 2 * e_total
    ret_local = tiles.shape[0] * tile_order * tile_order // devices_e
    offset = lax.axis_index("ea") * ret_local
    k_total = k_local * devices_k
    scale_p = 1.0 / math.sqrt(e_total)

    def layout(blocks):
        return arrange(jnp.take(tiles_of(jnp.moveaxis(blocks, 3, 2)), tiles, axis=-3), diag_count)

    greens = jnp.stack([layout(lesser_in), layout(greater_in)], axis=2)
    fwd_cos, fwd_sin = tables(length, e_total, length)
    full_cos, full_sin = tables(length, length, length)
    out_cos, out_sin = tables(e_total, length, length)
    coulomb_flat = arrange(jnp.take(tiles_of(coulomb), tiles, axis=-3), diag_count)
    outgoing = jnp.concatenate([greens, partner(greens, diag_count, tile_order)], axis=2)
    spectra = transform(
        lax.all_to_all(outgoing, "ea", split_axis=4, concat_axis=1, tiled=True),
        fwd_cos,
        fwd_sin,
        1.0,
        1.0,
    )
    direct = spectra[:, :, :2]
    mirrored = spectra[:, :, 2:]
    turned = polar_terms(direct, mirrored, scale_p)
    weight = lax.dynamic_slice_in_dim(coulomb_flat, offset, ret_local) ** 2
    lags = transform(jnp.sum(turned, axis=0, keepdims=True), full_cos, full_sin, -1.0, 1.0 / length)
    summed = lax.psum(lags, "ka")
    screened = transform(summed * (weight / k_total), full_cos, full_sin, 1.0, 1.0)
    sigma = self_energy(direct, screened, out_cos, out_sin, length, scale_p)
    returned = lax.all_to_all(sigma, "ea", split_axis=1, concat_axis=4, tiled=True)
    pieces = unarrange(returned, diag_count, tile_order)
    empty = jnp.zeros(pieces.shape[:-3] + (block_count * 16, tile_order, tile_order), jnp.float32)
    sigma_blocks = blocks_of(empty.at[..., tiles, :, :].set(pieces), block_count)
    sigma_ret = 0.5 * (sigma_blocks[:, :, 1] - sigma_blocks[:, :, 0])
    sigma_less = sigma_blocks[:, :, 0]
    batch = k_local * e_local
    identity = jnp.eye(order_n, dtype=jnp.float32)
    energy_idx = lax.axis_index("ea") * e_local + jnp.arange(e_local, dtype=jnp.int32)
    energies = -SPREAD + 2.0 * SPREAD * (energy_idx.astype(jnp.float32) + 0.5) / e_total
    energies = energies[None, :].reshape(batch)
    shifted = jnp.stack(
        [
            energies[:, None, None] * identity,
            jnp.broadcast_to(BROADEN * identity, (batch, order_n, order_n)),
        ],
        axis=1,
    )
    twice_eye = jnp.broadcast_to(
        jnp.stack([2.0 * identity, 0.0 * identity]), (batch, 2, order_n, order_n)
    )

    def per_energy(array_k):
        return array_k[:, None].reshape((batch,) + array_k.shape[1:])

    forward_r = []
    forward_l = []
    for blk_no in range(block_count):
        system = (
            shifted
            - per_energy(h_diag[:, blk_no])
            - sigma_ret[:, :, :, blk_no].reshape(batch, 2, order_n, order_n)
        )
        source = sigma_less[:, :, :, blk_no].reshape(batch, 2, order_n, order_n)
        if blk_no == 0:
            source = source + contact[:, :, 0].reshape(batch, 2, order_n, order_n)
        if blk_no == block_count - 1:
            source = source + contact[:, :, 1].reshape(batch, 2, order_n, order_n)
        if blk_no > 0:
            link = per_energy(coupling[:, blk_no - 1])
            system = system - pair_mul(dagger(link), pair_mul(forward_r[-1], link))
            source = source + pair_mul(dagger(link), pair_mul(forward_l[-1], link))
        green_r = newton(system, twice_eye)
        forward_r.append(green_r)
        forward_l.append(pair_mul(pair_mul(green_r, source), dagger(green_r)))
    retarded_list = [forward_r[-1]]
    lesser_list = [forward_l[-1]]
    blk_no = 0
    green_r = forward_r[blk_no]
    green_l = forward_l[blk_no]
    link = per_energy(coupling[:, blk_no])
    right_op = pair_mul(green_r, link)
    middle = pair_mul(right_op, retarded_list[0])
    new_r = green_r + pair_mul(middle, pair_mul(dagger(link), green_r))
    cross = pair_mul(middle, pair_mul(dagger(link), green_l))
    new_l = (
        green_l
        + pair_mul(pair_mul(right_op, lesser_list[0]), dagger(right_op))
        - cross
        - dagger(cross)
    )
    retarded_list.insert(0, new_r)
    lesser_list.insert(0, new_l)
    lesser = jnp.stack(lesser_list, axis=1)
    greater = jnp.stack(
        [
            lesser_list[blk_no] + retarded_list[blk_no] - dagger(retarded_list[blk_no])
            for blk_no in range(block_count)
        ],
        axis=1,
    )
    out_shape = (k_local, e_local, block_count, 2, order_n, order_n)
    return (lesser.reshape(out_shape), greater.reshape(out_shape))


MESH = pl.DeviceIdType.MESH
VMEM = pl.BlockSpec(memory_space=pltpu.VMEM)
SMEM = pl.BlockSpec(memory_space=pltpu.SMEM)
HBM = pl.BlockSpec(memory_space=pltpu.HBM)


def half_swap(rows):
    return pltpu.roll(rows, 4, rows.ndim - 2)


def upper_half(shape):
    return lax.broadcasted_iota(jnp.int32, shape, len(shape) - 2) % 8 < 4


def tile_place(tiles_ref, slot):
    tile = tiles_ref[slot]
    return tile // 16, tile % 16 // 4, tile % 4


def pack_tiles(tiles_ref, load):
    group = lax.broadcasted_iota(jnp.int32, (32, 128), 1) // 32
    slabs = [[load(blk, 32 * pos) for pos in range(4)] for blk in range(2)]
    parts = []
    for blk in range(2):
        part = slabs[blk][0]
        for pos in range(1, 4):
            part = jnp.where(group == pos, slabs[blk][pos], part)
        parts.append(part)
    for half in range(2):
        part = None
        for pos in range(4):
            blk, row, col = tile_place(tiles_ref, 8 + 4 * half + pos)
            slab = slabs[0][0]
            for index in range(1, 8):
                found = blk * 4 + row == index
                slab = jnp.where(found, slabs[index // 4][index % 4], slab)
            turn = (pos + 4 - col) % 4
            slab = jnp.where(turn % 2 == 1, pltpu.roll(slab, 32, 1), slab)
            slab = jnp.where(turn >= 2, pltpu.roll(slab, 64, 1), slab)
            part = slab if part is None else jnp.where(group == pos, slab, part)
        parts.append(part)
    return jnp.concatenate(parts, axis=0).reshape(16, 8, 128)


def exchange_kernel(
    n_k,
    n_e,
    tiles_hbm,
    l_hbm,
    g_hbm,
    c_hbm,
    out_ref,
    tiles_ref,
    l_ref,
    g_ref,
    c_ref,
    gt_ref,
    ct_ref,
    packed,
    weight_ref,
    held,
    sigma,
    back,
    load_sem,
    send_a,
    recv_a,
    send_b,
    recv_b,
):
    count = n_k * n_e
    half = n_e // 2
    my_k = lax.axis_index("ka")
    my_e = lax.axis_index("ea")
    me = my_k * n_e + my_e
    side = my_e // half

    loads = [
        pltpu.make_async_copy(source, target, load_sem.at[index])
        for index, (source, target) in enumerate(
            ((tiles_hbm, tiles_ref), (g_hbm, g_ref), (l_hbm, l_ref), (c_hbm, c_ref))
        )
    ]
    for load in loads:
        load.start()

    def place(other):
        return {"ka": other // n_e, "ea": other % n_e}

    def remote(source, slot, send_sem, recv_sem, other):
        return pltpu.make_async_remote_copy(
            src_ref=source,
            dst_ref=slot,
            send_sem=send_sem,
            recv_sem=recv_sem,
            device_id=place(other),
            device_id_type=MESH,
        )

    def forward(other):
        source = packed.at[other // 2, other % 2]
        return remote(source, held.at[me], send_a.at[other], recv_a.at[me], other)

    def arrival(other):
        source = packed.at[other // 2, other % 2]
        return remote(source, held.at[other], send_a.at[other], recv_a.at[other], other)

    def backward(other):
        return remote(sigma.at[other], back.at[me], send_b.at[other], recv_b.at[me], other)

    def returned(other):
        return remote(sigma.at[other], back.at[other], send_b.at[other], recv_b.at[other], other)

    def others(body):
        def step(index, carry):
            turn = (side + 1 + index // (n_k * half)) % 2
            rest = index % (n_k * half)
            energy = turn * half + (my_e + rest) % half
            body((my_k + rest // half) % n_k * n_e + energy)
            return carry

        lax.fori_loop(0, n_k * half, step, 0)
        lax.fori_loop(n_k * half + 1, count, step, 0)

    barrier = pltpu.get_barrier_semaphore()
    others(
        lambda other: pl.semaphore_signal(
            barrier, inc=1, device_id=place(other), device_id_type=MESH
        )
    )

    top = upper_half((16, 8, 128))

    def pack(kind, ref):
        real = pack_tiles(tiles_ref, lambda blk, row: ref[blk, 0, pl.ds(row, 32), :])
        imag = pack_tiles(tiles_ref, lambda blk, row: ref[blk, 1, pl.ds(row, 32), :])
        packed[:, 0, kind] = jnp.where(top, real, half_swap(imag))
        packed[:, 1, kind] = jnp.where(top, half_swap(real), imag)

    loads[0].wait()
    loads[1].wait()
    for blk in range(2):
        for part in range(2):
            gt_ref[blk, part] = g_ref[blk, part].T
    pack(1, gt_ref)
    loads[2].wait()
    pack(0, l_ref)
    pl.semaphore_wait(barrier, count - 1)
    others(lambda other: forward(other).start())

    held[me] = packed[me // 2, me % 2]
    loads[3].wait()
    for blk in range(2):
        ct_ref[blk] = c_ref[blk].T
    for kind, ref in ((0, c_ref), (1, ct_ref)):
        bare = pack_tiles(tiles_ref, lambda blk, row: ref[blk, pl.ds(row, 32), :])
        bare = bare * bare
        weight_ref[:, 0, kind] = jnp.where(top, bare, half_swap(bare))
        weight_ref[:, 1, kind] = jnp.where(top, half_swap(bare), bare)
    scale = SIGMA_SCALE / (n_e * n_k)
    weight_l = weight_ref[me // 2, me % 2, 0] * scale
    weight_g = weight_ref[me // 2, me % 2, 1] * scale

    lags = 2 * n_e - 1

    def correlate(turn, sums):
        first = (my_k + turn) % n_k * n_e

        def arrive(e, carry):
            @pl.when(first + e != me)
            def _():
                arrival(first + e).wait_recv()

            return carry

        lax.fori_loop(0, n_e, arrive, 0)
        plain, crossed = list(sums[0]), list(sums[1])
        lesser = [held[first + e, 0] for e in range(n_e)]
        greater = [held[first + e, 1] for e in range(n_e)]
        for e_two in range(n_e):
            swapped = half_swap(greater[e_two])
            for e_one in range(n_e):
                lag = e_one - e_two + n_e - 1
                plain[lag] = plain[lag] + lesser[e_one] * greater[e_two]
                crossed[lag] = crossed[lag] + lesser[e_one] * swapped
        return tuple(plain), tuple(crossed)

    zero = jnp.zeros((8, 128), jnp.float32)
    plain, crossed = lax.fori_loop(0, n_k, correlate, ((zero,) * lags, (zero,) * lags))
    sign = jnp.where(upper_half((8, 128)), 1.0, -1.0)
    real = [sign * (total - half_swap(total)) for total in plain]
    imag = [-sign * (total + half_swap(total)) for total in crossed]

    def convolve(turn, carry):
        first = (my_k + turn) % n_k * n_e
        for kind, weight in ((0, weight_l), (1, weight_g)):
            green = [held[first + e, kind] for e in range(n_e)]
            swapped = [half_swap(piece) for piece in green]
            for e_out in range(n_e):
                total = None
                for e_in in range(n_e):
                    lag = e_out - e_in if kind == 0 else e_in - e_out
                    lag = lag + n_e - 1
                    term = green[e_in] * real[lag] + swapped[e_in] * imag[lag]
                    total = term if total is None else total + term
                sigma[first + e_out, kind] = total * weight

        def send(index, inner):
            other = first + (side + 1 + index // half) % 2 * half + (my_e + index) % half

            @pl.when(other != me)
            def _():
                backward(other).start()

            return inner

        lax.fori_loop(0, n_e, send, 0)
        return carry

    lax.fori_loop(0, n_k, convolve, 0)
    back[me] = sigma[me]
    others(lambda other: forward(other).wait_send())
    others(lambda other: backward(other).wait_send())
    others(lambda other: returned(other).wait_recv())
    out_ref[...] = back[...]


def split(value):
    high = value.astype(jnp.bfloat16)
    return high, (value - high.astype(jnp.float32)).astype(jnp.bfloat16)


def square_form(rows):
    real, imag = rows[:, :128], rows[:, 128:]
    return split(jnp.concatenate([rows, jnp.concatenate([-imag, real], axis=1)], axis=0))


def times(first, second, contract=0):
    dims = (((1,), (contract,)), ((), ()))

    def dot(left, right):
        return lax.dot_general(left, right, dims, preferred_element_type=jnp.float32)

    high, low = first
    both = dot(jnp.concatenate([high, low], axis=0), second[0])
    return both[:128] + (dot(high, second[1]) + both[128:])


def adjoint(rows):
    return jnp.concatenate([rows[:, :128].T, -rows[:, 128:].T], axis=1)


def invert_rows(system, eye):
    real_m, imag_m = system[:, :128], system[:, 128:]
    only_re = jnp.where(eye, real_m, 0.0)
    only_im = jnp.where(eye, imag_m, 0.0)

    def reciprocal(axis):
        real_d = jnp.sum(only_re, axis=axis, keepdims=True)
        imag_d = jnp.sum(only_im, axis=axis, keepdims=True)
        denominator = real_d * real_d + imag_d * imag_d
        return real_d / denominator, -imag_d / denominator

    row_re, row_im = reciprocal(0)
    col_re, col_im = reciprocal(1)
    twice = jnp.where(eye, 2.0, 0.0)
    inner_re = twice - (real_m * row_re - imag_m * row_im)
    inner_im = -(real_m * row_im + imag_m * row_re)
    approx = jnp.concatenate(
        [col_re * inner_re - col_im * inner_im, col_re * inner_im + col_im * inner_re], axis=1
    )
    product = times(split(system), square_form(approx))
    rest = jnp.concatenate([twice - product[:, :128], -product[:, 128:]], axis=1)
    return times(split(approx), square_form(rest))


def sweep_kernel(
    tiles_hbm,
    energy_ref,
    sigma_ref,
    h_ref,
    link_ref,
    contact_ref,
    lesser_ref,
    greater_ref,
    blocks,
    tiles_ref,
    load_sem,
):
    load = pltpu.make_async_copy(tiles_hbm, tiles_ref, load_sem)
    load.start()
    top = upper_half((16, 8, 128))
    group = lax.broadcasted_iota(jnp.int32, (32, 128), 1) // 32
    pieces = []
    for kind in range(2):
        first, second = sigma_ref[:, 0, kind], sigma_ref[:, 1, kind]
        parts = (
            jnp.where(top, first, half_swap(second)),
            jnp.where(top, half_swap(first), second),
        )
        for part in range(2):
            packed = parts[part].reshape(128, 128)
            pieces.append((kind, part, packed[64:]))
            for blk in range(2):
                for pos in range(4):
                    blocks[kind, part, blk, 32 * pos : 32 * pos + 32, :] = jnp.where(
                        group == pos, packed[32 * blk : 32 * blk + 32], 0.0
                    )
    load.wait()
    for slot in range(8):
        blk, row, col = tile_place(tiles_ref, 8 + slot)
        start = 32 * (slot // 4)
        rows = pl.ds(pl.multiple_of(32 * row, 32), 32)
        for kind, part, packed in pieces:
            slab = pltpu.roll(packed[start : start + 32], (col + 4 - slot % 4) % 4 * 32, 1)
            blocks[kind, part, blk, rows, :] = jnp.where(
                group == col, slab, blocks[kind, part, blk, rows, :]
            )

    eye = lax.broadcasted_iota(jnp.int32, (128, 128), 0) == lax.broadcasted_iota(
        jnp.int32, (128, 128), 1
    )
    shift = jnp.concatenate(
        [jnp.where(eye, energy_ref[0], 0.0), jnp.where(eye, BROADEN, 0.0)], axis=1
    )

    def rows_of(ref, *index):
        return jnp.concatenate([ref[*index, 0], ref[*index, 1]], axis=1)

    def system_source(blk):
        less = jnp.concatenate([blocks[0, 0, blk], blocks[0, 1, blk]], axis=1)
        more = jnp.concatenate([blocks[1, 0, blk].T, blocks[1, 1, blk].T], axis=1)
        system = shift - rows_of(h_ref, blk) - 0.5 * (more - less)
        return system, less + rows_of(contact_ref, blk)

    link = rows_of(link_ref, 0)
    link_square = square_form(link)
    link_adjoint = split(adjoint(link))

    system_0, source_0 = system_source(0)
    system_1, source_1 = system_source(1)
    gr_0 = invert_rows(system_0, eye)
    gr_0_rows, gr_0_square = split(gr_0), square_form(gr_0)
    right_op = times(gr_0_rows, link_square)
    right_square = square_form(right_op)
    system_1 = system_1 - times(link_adjoint, right_square)
    gr_1 = invert_rows(system_1, eye)
    gl_0 = times(split(times(gr_0_rows, square_form(source_0))), gr_0_square, 1)
    left_l = times(link_adjoint, square_form(gl_0))
    source_1 = source_1 + times(split(left_l), link_square)
    gr_1_square = square_form(gr_1)
    gl_1 = times(split(times(split(gr_1), square_form(source_1))), gr_1_square, 1)
    left_r = times(link_adjoint, gr_0_square)
    right_rows = split(right_op)
    middle = split(times(right_rows, gr_1_square))
    full_r = gr_0 + times(middle, square_form(left_r))
    cross = times(middle, square_form(left_l))
    inner = times(split(times(right_rows, square_form(gl_1))), right_square, 1)
    full_l = gl_0 + inner - cross - adjoint(cross)
    for blk, retarded, lesser in ((0, full_r, full_l), (1, gr_1, gl_1)):
        greater = lesser + retarded - adjoint(retarded)
        for part in range(2):
            lesser_ref[blk, part] = lesser[:, 128 * part : 128 * part + 128]
            greater_ref[blk, part] = greater[:, 128 * part : 128 * part + 128]


def in_hbm(array):
    return pltpu.with_memory_space_constraint(array, pltpu.HBM)


def small_device(n_k, n_e, lesser_in, greater_in, h_diag, coupling, contact, coulomb, tiles):
    count = n_k * n_e
    f32 = jnp.float32
    limit = pltpu.CompilerParams(vmem_limit_bytes=32 * 1024 * 1024)
    slots = (count, 2, 8, 128)
    blocks = pltpu.VMEM((2, 2, 128, 128), f32)
    plane = pltpu.VMEM((2, 128, 128), f32)
    sigma = pl.pallas_call(
        partial(exchange_kernel, n_k, n_e),
        out_shape=jax.ShapeDtypeStruct(slots, f32),
        in_specs=[HBM] * 4,
        out_specs=VMEM,
        scratch_shapes=[pltpu.SMEM((16,), jnp.int32), blocks, blocks, plane, blocks, plane]
        + [pltpu.VMEM((16, 2, 2, 8, 128), f32)] * 2
        + [pltpu.VMEM(slots, f32)] * 3
        + [pltpu.SemaphoreType.DMA((4,))]
        + [pltpu.SemaphoreType.DMA((count,))] * 4,
        compiler_params=pltpu.CompilerParams(
            collective_id=0, has_side_effects=True, vmem_limit_bytes=32 * 1024 * 1024
        ),
        name="exchange",
    )(*(in_hbm(array) for array in (tiles, lesser_in[0, 0], greater_in[0, 0], coulomb)))
    energy = -SPREAD + 2.0 * SPREAD * (lax.axis_index("ea").astype(f32) + 0.5) / n_e
    lesser, greater = pl.pallas_call(
        sweep_kernel,
        out_shape=(jax.ShapeDtypeStruct((2, 2, 128, 128), f32),) * 2,
        in_specs=[HBM, SMEM, VMEM, VMEM, VMEM, VMEM],
        out_specs=(VMEM, VMEM),
        scratch_shapes=[
            pltpu.VMEM((2, 2, 2, 128, 128), f32),
            pltpu.SMEM((16,), jnp.int32),
            pltpu.SemaphoreType.DMA,
        ],
        compiler_params=limit,
        name="sweep",
    )(
        in_hbm(tiles),
        energy.reshape(1),
        sigma.reshape(16, 2, 2, 8, 128),
        h_diag[0],
        coupling[0],
        contact[0, 0],
    )
    return lesser[None, None], greater[None, None]


def per_device(mesh, lesser_in, *rest):
    n_k, n_e = mesh.shape["ka"], mesh.shape["ea"]
    fits = n_k * n_e == 32 and lesser_in.shape == (1, 1, 2, 2, 128, 128) and rest[-1].shape == (16,)
    if fits:
        return small_device(n_k, n_e, lesser_in, *rest)
    return on_device(lesser_in, *rest)


def solution(mesh):
    in_specs = (
        P("ka", "ea", None, None, None, None),
        P("ka", "ea", None, None, None, None),
        P("ka", None, None, None, None),
        P("ka", None, None, None, None),
        P("ka", "ea", None, None, None, None),
        P(),
        P(),
    )
    out_specs = (P("ka", "ea", None, None, None, None), P("ka", "ea", None, None, None, None))
    return jax.shard_map(
        partial(per_device, mesh), mesh=mesh, in_specs=in_specs, out_specs=out_specs, check_vma=False
    )
```

```python
import math
from functools import partial

import jax
import jax.numpy as jnp
import numpy as np
from jax import lax
from jax.experimental import pallas as pl
from jax.experimental.pallas import tpu as pltpu
from jax.sharding import PartitionSpec as P

BROADEN = 0.3
SPREAD = 0.05
SIGMA_SCALE = 0.01
PRECISE = lax.Precision.HIGHEST


def tiles_of(blocks):
    leading = blocks.shape[:-3]
    lead_rank = len(leading)
    block_count = blocks.shape[-3]
    tile_order = blocks.shape[-1] // 4
    viewed = blocks.reshape(leading + (block_count, 4, tile_order, 4, tile_order))
    viewed = jnp.moveaxis(viewed, lead_rank + 3, lead_rank + 2)
    return viewed.reshape(leading + (block_count * 16, tile_order, tile_order))


def blocks_of(pieces, block_count):
    leading = pieces.shape[:-3]
    lead_rank = len(leading)
    tile_order = pieces.shape[-1]
    viewed = pieces.reshape(leading + (block_count, 4, 4, tile_order, tile_order))
    viewed = jnp.moveaxis(viewed, lead_rank + 2, lead_rank + 3)
    return viewed.reshape(leading + (block_count, 4 * tile_order, 4 * tile_order))


def diag_order(tile_order):
    listing = [row_pos * tile_order + row_pos for row_pos in range(tile_order)]
    for row_pos in range(tile_order):
        for col_pos in range(row_pos + 1, tile_order):
            listing.append(row_pos * tile_order + col_pos)
            listing.append(col_pos * tile_order + row_pos)
    forward = np.array(listing, np.int32)
    return (forward, np.argsort(forward).astype(np.int32))


def arrange(pieces, diag_count):
    leading = pieces.shape[:-3]
    tile_order = pieces.shape[-1]
    forward = diag_order(tile_order)[0]
    diagonal = pieces[..., :diag_count, :, :].reshape(
        leading + (diag_count, tile_order * tile_order)
    )
    diagonal = jnp.take(diagonal, forward, axis=-1).reshape(leading + (-1,))
    paired = pieces[..., diag_count:, :, :].reshape(leading + (-1, 2, tile_order, tile_order))
    paired = jnp.stack([paired[..., 0, :, :], jnp.swapaxes(paired[..., 1, :, :], -1, -2)], axis=-1)
    return jnp.concatenate([diagonal, paired.reshape(leading + (-1,))], axis=-1)


def unarrange(flattened, diag_count, tile_order):
    leading = flattened.shape[:-1]
    square = tile_order * tile_order
    inverse = diag_order(tile_order)[1]
    diagonal = flattened[..., : diag_count * square].reshape(leading + (diag_count, square))
    diagonal = jnp.take(diagonal, inverse, axis=-1).reshape(
        leading + (diag_count, tile_order, tile_order)
    )
    paired = flattened[..., diag_count * square :].reshape(
        leading + (-1, tile_order, tile_order, 2)
    )
    paired = jnp.stack([paired[..., 0], jnp.swapaxes(paired[..., 1], -1, -2)], axis=-3)
    paired = paired.reshape(leading + (-1, tile_order, tile_order))
    return jnp.concatenate([diagonal, paired], axis=-3)


def partner(flattened, diag_count, tile_order):
    size_last = flattened.shape[-1]
    square = tile_order * tile_order
    flipped = flattened.reshape(flattened.shape[:-1] + (size_last // 2, 2))[..., ::-1].reshape(
        flattened.shape
    )
    position = jnp.arange(size_last, dtype=jnp.int32)
    itself = (position < diag_count * square) & (position % square < tile_order)
    return jnp.where(itself, flattened, flipped)


def tables(rows_count, cols_count, length):
    phases = (
        jnp.arange(rows_count, dtype=jnp.int32)[:, None]
        * jnp.arange(cols_count, dtype=jnp.int32)[None, :]
        % length
    )
    angles = phases.astype(jnp.float32) * (2.0 * math.pi / length)
    return (jnp.cos(angles), jnp.sin(angles))


def apply_table(coeffs, values):
    return jnp.einsum("fe,keal->kfal", coeffs, values, precision=PRECISE)


def transform(series, cosine, sine, sign, factor):
    real_in = series[..., 0, :]
    imag_in = series[..., 1, :]
    real_out = apply_table(cosine, real_in) + sign * apply_table(sine, imag_in)
    imag_out = apply_table(cosine, imag_in) - sign * apply_table(sine, real_in)
    return jnp.stack([real_out, imag_out], axis=-2) * factor


def pair_prod(first, second):
    first_re = first[..., 0, :]
    first_im = first[..., 1, :]
    second_re = second[..., 0, :]
    second_im = second[..., 1, :]
    return jnp.stack(
        [first_re * second_re - first_im * second_im, first_re * second_im + first_im * second_re],
        axis=-2,
    )


def pair_mul(first, second):
    products = jnp.einsum("bsij,btjk->bstik", first, second, precision=PRECISE)
    return jnp.stack(
        [products[:, 0, 0] - products[:, 1, 1], products[:, 0, 1] + products[:, 1, 0]], axis=1
    )


def dagger(matrix):
    swapped = jnp.swapaxes(matrix, -1, -2)
    return jnp.stack([swapped[:, 0], -swapped[:, 1]], axis=1)


def newton(system, twice_eye):
    real_d = jnp.diagonal(system[:, 0], axis1=-2, axis2=-1)
    imag_d = jnp.diagonal(system[:, 1], axis1=-2, axis2=-1)
    denominator = real_d * real_d + imag_d * imag_d
    inverse_re = real_d / denominator
    inverse_im = -imag_d / denominator
    scaled_re = system[:, 0] * inverse_re[:, None, :] - system[:, 1] * inverse_im[:, None, :]
    scaled_im = system[:, 0] * inverse_im[:, None, :] + system[:, 1] * inverse_re[:, None, :]
    inner_re = twice_eye[:, 0] - scaled_re
    inner_im = -scaled_im
    approx = jnp.stack(
        [
            inverse_re[:, :, None] * inner_re - inverse_im[:, :, None] * inner_im,
            inverse_re[:, :, None] * inner_im + inverse_im[:, :, None] * inner_re,
        ],
        axis=1,
    )
    approx = pair_mul(approx, twice_eye - pair_mul(system, approx))
    return approx


def polar_terms(direct, mirrored, scale_p):
    reflected = jnp.concatenate([mirrored[:, :1], jnp.flip(mirrored[:, 1:], axis=1)], axis=1)
    correlated = pair_prod(direct, reflected[:, :, ::-1])
    return jnp.stack([correlated[..., 1, :], -correlated[..., 0, :]], axis=-2) * scale_p


def self_energy(direct, screened, out_cos, out_sin, length, scale_p):
    convolved = transform(pair_prod(direct, screened), out_cos, out_sin, -1.0, 1.0 / length)
    return jnp.stack([-convolved[..., 1, :], convolved[..., 0, :]], axis=-2) * (
        SIGMA_SCALE * scale_p
    )


def on_device(lesser_in, greater_in, h_diag, coupling, contact, coulomb, tiles):
    k_local = lesser_in.shape[0]
    e_local = lesser_in.shape[1]
    block_count = lesser_in.shape[2]
    order_n = lesser_in.shape[-1]
    tile_order = order_n // 4
    diag_count = 4 * block_count
    devices_e = lax.axis_size("ea")
    devices_k = lax.axis_size("ka")
    e_total = e_local * devices_e
    length = 2 * e_total
    ret_local = tiles.shape[0] * tile_order * tile_order // devices_e
    offset = lax.axis_index("ea") * ret_local
    k_total = k_local * devices_k
    scale_p = 1.0 / math.sqrt(e_total)

    def layout(blocks):
        return arrange(jnp.take(tiles_of(jnp.moveaxis(blocks, 3, 2)), tiles, axis=-3), diag_count)

    greens = jnp.stack([layout(lesser_in), layout(greater_in)], axis=2)
    fwd_cos, fwd_sin = tables(length, e_total, length)
    full_cos, full_sin = tables(length, length, length)
    out_cos, out_sin = tables(e_total, length, length)
    coulomb_flat = arrange(jnp.take(tiles_of(coulomb), tiles, axis=-3), diag_count)
    outgoing = jnp.concatenate([greens, partner(greens, diag_count, tile_order)], axis=2)
    spectra = transform(
        lax.all_to_all(outgoing, "ea", split_axis=4, concat_axis=1, tiled=True),
        fwd_cos,
        fwd_sin,
        1.0,
        1.0,
    )
    direct = spectra[:, :, :2]
    mirrored = spectra[:, :, 2:]
    turned = polar_terms(direct, mirrored, scale_p)
    weight = lax.dynamic_slice_in_dim(coulomb_flat, offset, ret_local) ** 2
    lags = transform(jnp.sum(turned, axis=0, keepdims=True), full_cos, full_sin, -1.0, 1.0 / length)
    summed = lax.psum(lags, "ka")
    screened = transform(summed * (weight / k_total), full_cos, full_sin, 1.0, 1.0)
    sigma = self_energy(direct, screened, out_cos, out_sin, length, scale_p)
    returned = lax.all_to_all(sigma, "ea", split_axis=1, concat_axis=4, tiled=True)
    pieces = unarrange(returned, diag_count, tile_order)
    empty = jnp.zeros(pieces.shape[:-3] + (block_count * 16, tile_order, tile_order), jnp.float32)
    sigma_blocks = blocks_of(empty.at[..., tiles, :, :].set(pieces), block_count)
    sigma_ret = 0.5 * (sigma_blocks[:, :, 1] - sigma_blocks[:, :, 0])
    sigma_less = sigma_blocks[:, :, 0]
    batch = k_local * e_local
    identity = jnp.eye(order_n, dtype=jnp.float32)
    energy_idx = lax.axis_index("ea") * e_local + jnp.arange(e_local, dtype=jnp.int32)
    energies = -SPREAD + 2.0 * SPREAD * (energy_idx.astype(jnp.float32) + 0.5) / e_total
    energies = energies[None, :].reshape(batch)
    shifted = jnp.stack(
        [
            energies[:, None, None] * identity,
            jnp.broadcast_to(BROADEN * identity, (batch, order_n, order_n)),
        ],
        axis=1,
    )
    twice_eye = jnp.broadcast_to(
        jnp.stack([2.0 * identity, 0.0 * identity]), (batch, 2, order_n, order_n)
    )

    def per_energy(array_k):
        return array_k[:, None].reshape((batch,) + array_k.shape[1:])

    forward_r = []
    forward_l = []
    for blk_no in range(block_count):
        system = (
            shifted
            - per_energy(h_diag[:, blk_no])
            - sigma_ret[:, :, :, blk_no].reshape(batch, 2, order_n, order_n)
        )
        source = sigma_less[:, :, :, blk_no].reshape(batch, 2, order_n, order_n)
        if blk_no == 0:
            source = source + contact[:, :, 0].reshape(batch, 2, order_n, order_n)
        if blk_no == block_count - 1:
            source = source + contact[:, :, 1].reshape(batch, 2, order_n, order_n)
        if blk_no > 0:
            link = per_energy(coupling[:, blk_no - 1])
            system = system - pair_mul(dagger(link), pair_mul(forward_r[-1], link))
            source = source + pair_mul(dagger(link), pair_mul(forward_l[-1], link))
        green_r = newton(system, twice_eye)
        forward_r.append(green_r)
        forward_l.append(pair_mul(pair_mul(green_r, source), dagger(green_r)))
    retarded_list = [forward_r[-1]]
    lesser_list = [forward_l[-1]]
    blk_no = 0
    green_r = forward_r[blk_no]
    green_l = forward_l[blk_no]
    link = per_energy(coupling[:, blk_no])
    right_op = pair_mul(green_r, link)
    middle = pair_mul(right_op, retarded_list[0])
    new_r = green_r + pair_mul(middle, pair_mul(dagger(link), green_r))
    cross = pair_mul(middle, pair_mul(dagger(link), green_l))
    new_l = (
        green_l
        + pair_mul(pair_mul(right_op, lesser_list[0]), dagger(right_op))
        - cross
        - dagger(cross)
    )
    retarded_list.insert(0, new_r)
    lesser_list.insert(0, new_l)
    lesser = jnp.stack(lesser_list, axis=1)
    greater = jnp.stack(
        [
            lesser_list[blk_no] + retarded_list[blk_no] - dagger(retarded_list[blk_no])
            for blk_no in range(block_count)
        ],
        axis=1,
    )
    out_shape = (k_local, e_local, block_count, 2, order_n, order_n)
    return (lesser.reshape(out_shape), greater.reshape(out_shape))


MESH = pl.DeviceIdType.MESH
VMEM = pl.BlockSpec(memory_space=pltpu.VMEM)
SMEM = pl.BlockSpec(memory_space=pltpu.SMEM)
HBM = pl.BlockSpec(memory_space=pltpu.HBM)


def half_swap(rows):
    return pltpu.roll(rows, 4, rows.ndim - 2)


def upper_half(shape):
    return lax.broadcasted_iota(jnp.int32, shape, len(shape) - 2) % 8 < 4


def tile_place(tiles_ref, slot):
    tile = tiles_ref[slot]
    return tile // 16, tile % 16 // 4, tile % 4


def pack_tiles(tiles_ref, load):
    group = lax.broadcasted_iota(jnp.int32, (32, 128), 1) // 32
    slabs = [[load(blk, 32 * pos) for pos in range(4)] for blk in range(2)]
    parts = []
    for blk in range(2):
        part = slabs[blk][0]
        for pos in range(1, 4):
            part = jnp.where(group == pos, slabs[blk][pos], part)
        parts.append(part)
    for half in range(2):
        part = None
        for pos in range(4):
            blk, row, col = tile_place(tiles_ref, 8 + 4 * half + pos)
            slab = slabs[0][0]
            for index in range(1, 8):
                found = blk * 4 + row == index
                slab = jnp.where(found, slabs[index // 4][index % 4], slab)
            turn = (pos + 4 - col) % 4
            slab = jnp.where(turn % 2 == 1, pltpu.roll(slab, 32, 1), slab)
            slab = jnp.where(turn >= 2, pltpu.roll(slab, 64, 1), slab)
            part = slab if part is None else jnp.where(group == pos, slab, part)
        parts.append(part)
    return jnp.concatenate(parts, axis=0).reshape(16, 8, 128)


def exchange_kernel(
    n_k,
    n_e,
    tiles_hbm,
    l_hbm,
    g_hbm,
    c_hbm,
    out_ref,
    tiles_ref,
    l_ref,
    g_ref,
    c_ref,
    gt_ref,
    ct_ref,
    packed,
    weight_ref,
    held,
    sigma,
    back,
    load_sem,
    send_a,
    recv_a,
    send_b,
    recv_b,
):
    count = n_k * n_e
    half = n_e // 2
    my_k = lax.axis_index("ka")
    my_e = lax.axis_index("ea")
    me = my_k * n_e + my_e
    side = my_e // half

    loads = [
        pltpu.make_async_copy(source, target, load_sem.at[index])
        for index, (source, target) in enumerate(
            ((tiles_hbm, tiles_ref), (g_hbm, g_ref), (l_hbm, l_ref), (c_hbm, c_ref))
        )
    ]
    for load in loads:
        load.start()

    k_list = [(my_k + step) % n_k for step in range(n_k)]
    near = [side * half + (my_e + step) % half for step in range(half)]
    far = [(1 - side) * half + (my_e + step) % half for step in range(half)]
    others = [(k, e) for k in k_list for e in far]
    others += [(k, e) for k in k_list for e in near][1:]

    def remote(source, target, send_sem, recv_sem, k, e):
        return pltpu.make_async_remote_copy(
            src_ref=source,
            dst_ref=target,
            send_sem=send_sem,
            recv_sem=recv_sem,
            device_id={"ka": k, "ea": e},
            device_id_type=MESH,
        )

    def all_of(ref, send_sem, recv_sem):
        every = ref.at[pl.ds(0, count - 1)]
        return remote(every, every, send_sem, recv_sem, *others[0])

    barrier = pltpu.get_barrier_semaphore()
    for k, e in others:
        pl.semaphore_signal(barrier, inc=1, device_id={"ka": k, "ea": e}, device_id_type=MESH)

    top = upper_half((16, 8, 128))

    def pack(kind, ref):
        real = pack_tiles(tiles_ref, lambda blk, row: ref[blk, 0, pl.ds(row, 32), :])
        imag = pack_tiles(tiles_ref, lambda blk, row: ref[blk, 1, pl.ds(row, 32), :])
        packed[:16, kind] = jnp.where(top, real, half_swap(imag))
        packed[16:, kind] = jnp.where(top, half_swap(real), imag)

    loads[0].wait()
    loads[1].wait()
    for blk in range(2):
        for part in range(2):
            gt_ref[blk, part] = g_ref[blk, part].T
    pack(1, gt_ref)
    loads[2].wait()
    pack(0, l_ref)
    pl.semaphore_wait(barrier, count - 1)
    for k, e in others:
        other = k * n_e + e
        remote(packed.at[other], held.at[me], send_a, recv_a, k, e).start()

    held[me] = packed[me]
    loads[3].wait()
    for blk in range(2):
        ct_ref[blk] = c_ref[blk].T
    for kind, ref in ((0, c_ref), (1, ct_ref)):
        bare = pack_tiles(tiles_ref, lambda blk, row: ref[blk, pl.ds(row, 32), :])
        bare = bare * bare
        weight_ref[:16, kind] = jnp.where(top, bare, half_swap(bare))
        weight_ref[16:, kind] = jnp.where(top, half_swap(bare), bare)
    scale = SIGMA_SCALE / (n_e * n_k)
    weight_l = weight_ref[me, 0] * scale
    weight_g = weight_ref[me, 1] * scale

    lags = 2 * n_e - 1

    def correlate(k_index, sums):
        first = k_index * n_e
        plain, crossed = list(sums[0]), list(sums[1])
        lesser = [held[first + e, 0] for e in range(n_e)]
        greater = [held[first + e, 1] for e in range(n_e)]
        for e_two in range(n_e):
            swapped = half_swap(greater[e_two])
            for e_one in range(n_e):
                lag = e_one - e_two + n_e - 1
                plain[lag] = plain[lag] + lesser[e_one] * greater[e_two]
                crossed[lag] = crossed[lag] + lesser[e_one] * swapped
        return tuple(plain), tuple(crossed)

    all_of(held, send_a, recv_a).wait_recv()
    zero = jnp.zeros((8, 128), jnp.float32)
    plain, crossed = lax.fori_loop(0, n_k, correlate, ((zero,) * lags, (zero,) * lags))
    sign = jnp.where(upper_half((8, 128)), 1.0, -1.0)
    real = [sign * (total - half_swap(total)) for total in plain]
    imag = [-sign * (total + half_swap(total)) for total in crossed]

    def convolve(turn, carry):
        k_index = (my_k + turn) % n_k
        first = k_index * n_e
        for kind, weight in ((0, weight_l), (1, weight_g)):
            green = [held[first + e, kind] for e in range(n_e)]
            swapped = [half_swap(piece) for piece in green]
            for e_out in range(n_e):
                total = None
                for e_in in range(n_e):
                    lag = e_out - e_in if kind == 0 else e_in - e_out
                    lag = lag + n_e - 1
                    term = green[e_in] * real[lag] + swapped[e_in] * imag[lag]
                    total = term if total is None else total + term
                sigma[first + e_out, kind] = total * weight

        def send(e):
            source = sigma.at[first + e]
            remote(source, back.at[me], send_b, recv_b, k_index, e).start()

        for e in far + near[1:]:
            send(e)

        @pl.when(turn > 0)
        def _():
            send(my_e)

        return carry

    lax.fori_loop(0, n_k, convolve, 0)
    back[me] = sigma[me]
    all_of(held, send_a, recv_a).wait_send()
    all_of(back, send_b, recv_b).wait_send()
    all_of(back, send_b, recv_b).wait_recv()
    out_ref[...] = back[...]


def split(value):
    high = value.astype(jnp.bfloat16)
    return high, (value - high.astype(jnp.float32)).astype(jnp.bfloat16)


def square_form(rows):
    real, imag = rows[:, :128], rows[:, 128:]
    return split(jnp.concatenate([rows, jnp.concatenate([-imag, real], axis=1)], axis=0))


def times(first, second, contract=0):
    dims = (((1,), (contract,)), ((), ()))

    def dot(left, right):
        return lax.dot_general(left, right, dims, preferred_element_type=jnp.float32)

    high, low = first
    both = dot(jnp.concatenate([high, low], axis=0), second[0])
    return both[:128] + (dot(high, second[1]) + both[128:])


def adjoint(rows):
    return jnp.concatenate([rows[:, :128].T, -rows[:, 128:].T], axis=1)


def invert_rows(system, eye):
    real_m, imag_m = system[:, :128], system[:, 128:]
    only_re = jnp.where(eye, real_m, 0.0)
    only_im = jnp.where(eye, imag_m, 0.0)

    def reciprocal(axis):
        real_d = jnp.sum(only_re, axis=axis, keepdims=True)
        imag_d = jnp.sum(only_im, axis=axis, keepdims=True)
        denominator = real_d * real_d + imag_d * imag_d
        return real_d / denominator, -imag_d / denominator

    row_re, row_im = reciprocal(0)
    col_re, col_im = reciprocal(1)
    twice = jnp.where(eye, 2.0, 0.0)
    inner_re = twice - (real_m * row_re - imag_m * row_im)
    inner_im = -(real_m * row_im + imag_m * row_re)
    approx = jnp.concatenate(
        [col_re * inner_re - col_im * inner_im, col_re * inner_im + col_im * inner_re], axis=1
    )
    product = times(split(system), square_form(approx))
    rest = jnp.concatenate([twice - product[:, :128], -product[:, 128:]], axis=1)
    return times(split(approx), square_form(rest))


def sweep_kernel(
    tiles_hbm,
    energy_ref,
    sigma_ref,
    h_ref,
    link_ref,
    contact_ref,
    lesser_ref,
    greater_ref,
    blocks,
    tiles_ref,
    load_sem,
):
    load = pltpu.make_async_copy(tiles_hbm, tiles_ref, load_sem)
    load.start()
    top = upper_half((16, 8, 128))
    group = lax.broadcasted_iota(jnp.int32, (32, 128), 1) // 32
    pieces = []
    for kind in range(2):
        first, second = sigma_ref[:16, kind], sigma_ref[16:, kind]
        parts = (
            jnp.where(top, first, half_swap(second)),
            jnp.where(top, half_swap(first), second),
        )
        for part in range(2):
            packed = parts[part].reshape(128, 128)
            pieces.append((kind, part, packed[64:]))
            for blk in range(2):
                for pos in range(4):
                    blocks[kind, part, blk, 32 * pos : 32 * pos + 32, :] = jnp.where(
                        group == pos, packed[32 * blk : 32 * blk + 32], 0.0
                    )
    load.wait()
    for slot in range(8):
        blk, row, col = tile_place(tiles_ref, 8 + slot)
        start = 32 * (slot // 4)
        rows = pl.ds(pl.multiple_of(32 * row, 32), 32)
        for kind, part, packed in pieces:
            slab = pltpu.roll(packed[start : start + 32], (col + 4 - slot % 4) % 4 * 32, 1)
            blocks[kind, part, blk, rows, :] = jnp.where(
                group == col, slab, blocks[kind, part, blk, rows, :]
            )

    eye = lax.broadcasted_iota(jnp.int32, (128, 128), 0) == lax.broadcasted_iota(
        jnp.int32, (128, 128), 1
    )
    shift = jnp.concatenate(
        [jnp.where(eye, energy_ref[0], 0.0), jnp.where(eye, BROADEN, 0.0)], axis=1
    )

    def rows_of(ref, *index):
        return jnp.concatenate([ref[*index, 0], ref[*index, 1]], axis=1)

    def system_source(blk):
        less = jnp.concatenate([blocks[0, 0, blk], blocks[0, 1, blk]], axis=1)
        more = jnp.concatenate([blocks[1, 0, blk].T, blocks[1, 1, blk].T], axis=1)
        system = shift - rows_of(h_ref, blk) - 0.5 * (more - less)
        return system, less + rows_of(contact_ref, blk)

    link = rows_of(link_ref, 0)
    link_square = square_form(link)
    link_adjoint = split(adjoint(link))

    system_0, source_0 = system_source(0)
    system_1, source_1 = system_source(1)
    gr_0 = invert_rows(system_0, eye)
    gr_0_rows, gr_0_square = split(gr_0), square_form(gr_0)
    right_op = times(gr_0_rows, link_square)
    right_square = square_form(right_op)
    system_1 = system_1 - times(link_adjoint, right_square)
    gr_1 = invert_rows(system_1, eye)
    gl_0 = times(split(times(gr_0_rows, square_form(source_0))), gr_0_square, 1)
    left_l = times(link_adjoint, square_form(gl_0))
    source_1 = source_1 + times(split(left_l), link_square)
    gr_1_square = square_form(gr_1)
    gl_1 = times(split(times(split(gr_1), square_form(source_1))), gr_1_square, 1)
    left_r = times(link_adjoint, gr_0_square)
    right_rows = split(right_op)
    middle = split(times(right_rows, gr_1_square))
    full_r = gr_0 + times(middle, square_form(left_r))
    cross = times(middle, square_form(left_l))
    inner = times(split(times(right_rows, square_form(gl_1))), right_square, 1)
    full_l = gl_0 + inner - cross - adjoint(cross)
    for blk, retarded, lesser in ((0, full_r, full_l), (1, gr_1, gl_1)):
        greater = lesser + retarded - adjoint(retarded)
        for part in range(2):
            lesser_ref[blk, part] = lesser[:, 128 * part : 128 * part + 128]
            greater_ref[blk, part] = greater[:, 128 * part : 128 * part + 128]


def in_hbm(array):
    return pltpu.with_memory_space_constraint(array, pltpu.HBM)


def small_device(n_k, n_e, lesser_in, greater_in, h_diag, coupling, contact, coulomb, tiles):
    count = n_k * n_e
    f32 = jnp.float32
    limit = pltpu.CompilerParams(vmem_limit_bytes=32 * 1024 * 1024)
    slots = (count, 2, 8, 128)
    blocks = pltpu.VMEM((2, 2, 128, 128), f32)
    plane = pltpu.VMEM((2, 128, 128), f32)
    sigma = pl.pallas_call(
        partial(exchange_kernel, n_k, n_e),
        out_shape=jax.ShapeDtypeStruct(slots, f32),
        in_specs=[HBM] * 4,
        out_specs=VMEM,
        scratch_shapes=[pltpu.SMEM((16,), jnp.int32), blocks, blocks, plane, blocks, plane]
        + [pltpu.VMEM(slots, f32)] * 5
        + [pltpu.SemaphoreType.DMA((4,))]
        + [pltpu.SemaphoreType.DMA] * 4,
        compiler_params=pltpu.CompilerParams(
            collective_id=0, has_side_effects=True, vmem_limit_bytes=32 * 1024 * 1024
        ),
        name="exchange",
    )(*(in_hbm(array) for array in (tiles, lesser_in[0, 0], greater_in[0, 0], coulomb)))
    energy = -SPREAD + 2.0 * SPREAD * (lax.axis_index("ea").astype(f32) + 0.5) / n_e
    lesser, greater = pl.pallas_call(
        sweep_kernel,
        out_shape=(jax.ShapeDtypeStruct((2, 2, 128, 128), f32),) * 2,
        in_specs=[HBM, SMEM, VMEM, VMEM, VMEM, VMEM],
        out_specs=(VMEM, VMEM),
        scratch_shapes=[
            pltpu.VMEM((2, 2, 2, 128, 128), f32),
            pltpu.SMEM((16,), jnp.int32),
            pltpu.SemaphoreType.DMA,
        ],
        compiler_params=limit,
        name="sweep",
    )(
        in_hbm(tiles),
        energy.reshape(1),
        sigma,
        h_diag[0],
        coupling[0],
        contact[0, 0],
    )
    return lesser[None, None], greater[None, None]


def per_device(mesh, lesser_in, *rest):
    n_k, n_e = mesh.shape["ka"], mesh.shape["ea"]
    fits = n_k * n_e == 32 and lesser_in.shape == (1, 1, 2, 2, 128, 128) and rest[-1].shape == (16,)
    if fits:
        return small_device(n_k, n_e, lesser_in, *rest)
    return on_device(lesser_in, *rest)


def solution(mesh):
    in_specs = (
        P("ka", "ea", None, None, None, None),
        P("ka", "ea", None, None, None, None),
        P("ka", None, None, None, None),
        P("ka", None, None, None, None),
        P("ka", "ea", None, None, None, None),
        P(),
        P(),
    )
    out_specs = (P("ka", "ea", None, None, None, None), P("ka", "ea", None, None, None, None))
    return jax.shard_map(
        partial(per_device, mesh), mesh=mesh, in_specs=in_specs, out_specs=out_specs, check_vma=False
    )
```

```python
import math
from functools import partial

import jax
import jax.numpy as jnp
import numpy as np
from jax import lax
from jax.experimental import pallas as pl
from jax.experimental.pallas import tpu as pltpu
from jax.sharding import PartitionSpec as P

BROADEN = 0.3
SPREAD = 0.05
SIGMA_SCALE = 0.01
PRECISE = lax.Precision.HIGHEST


def tiles_of(blocks):
    leading = blocks.shape[:-3]
    lead_rank = len(leading)
    block_count = blocks.shape[-3]
    tile_order = blocks.shape[-1] // 4
    viewed = blocks.reshape(leading + (block_count, 4, tile_order, 4, tile_order))
    viewed = jnp.moveaxis(viewed, lead_rank + 3, lead_rank + 2)
    return viewed.reshape(leading + (block_count * 16, tile_order, tile_order))


def blocks_of(pieces, block_count):
    leading = pieces.shape[:-3]
    lead_rank = len(leading)
    tile_order = pieces.shape[-1]
    viewed = pieces.reshape(leading + (block_count, 4, 4, tile_order, tile_order))
    viewed = jnp.moveaxis(viewed, lead_rank + 2, lead_rank + 3)
    return viewed.reshape(leading + (block_count, 4 * tile_order, 4 * tile_order))


def diag_order(tile_order):
    listing = [row_pos * tile_order + row_pos for row_pos in range(tile_order)]
    for row_pos in range(tile_order):
        for col_pos in range(row_pos + 1, tile_order):
            listing.append(row_pos * tile_order + col_pos)
            listing.append(col_pos * tile_order + row_pos)
    forward = np.array(listing, np.int32)
    return (forward, np.argsort(forward).astype(np.int32))


def arrange(pieces, diag_count):
    leading = pieces.shape[:-3]
    tile_order = pieces.shape[-1]
    forward = diag_order(tile_order)[0]
    diagonal = pieces[..., :diag_count, :, :].reshape(
        leading + (diag_count, tile_order * tile_order)
    )
    diagonal = jnp.take(diagonal, forward, axis=-1).reshape(leading + (-1,))
    paired = pieces[..., diag_count:, :, :].reshape(leading + (-1, 2, tile_order, tile_order))
    paired = jnp.stack([paired[..., 0, :, :], jnp.swapaxes(paired[..., 1, :, :], -1, -2)], axis=-1)
    return jnp.concatenate([diagonal, paired.reshape(leading + (-1,))], axis=-1)


def unarrange(flattened, diag_count, tile_order):
    leading = flattened.shape[:-1]
    square = tile_order * tile_order
    inverse = diag_order(tile_order)[1]
    diagonal = flattened[..., : diag_count * square].reshape(leading + (diag_count, square))
    diagonal = jnp.take(diagonal, inverse, axis=-1).reshape(
        leading + (diag_count, tile_order, tile_order)
    )
    paired = flattened[..., diag_count * square :].reshape(
        leading + (-1, tile_order, tile_order, 2)
    )
    paired = jnp.stack([paired[..., 0], jnp.swapaxes(paired[..., 1], -1, -2)], axis=-3)
    paired = paired.reshape(leading + (-1, tile_order, tile_order))
    return jnp.concatenate([diagonal, paired], axis=-3)


def partner(flattened, diag_count, tile_order):
    size_last = flattened.shape[-1]
    square = tile_order * tile_order
    flipped = flattened.reshape(flattened.shape[:-1] + (size_last // 2, 2))[..., ::-1].reshape(
        flattened.shape
    )
    position = jnp.arange(size_last, dtype=jnp.int32)
    itself = (position < diag_count * square) & (position % square < tile_order)
    return jnp.where(itself, flattened, flipped)


def tables(rows_count, cols_count, length):
    phases = (
        jnp.arange(rows_count, dtype=jnp.int32)[:, None]
        * jnp.arange(cols_count, dtype=jnp.int32)[None, :]
        % length
    )
    angles = phases.astype(jnp.float32) * (2.0 * math.pi / length)
    return (jnp.cos(angles), jnp.sin(angles))


def apply_table(coeffs, values):
    return jnp.einsum("fe,keal->kfal", coeffs, values, precision=PRECISE)


def transform(series, cosine, sine, sign, factor):
    real_in = series[..., 0, :]
    imag_in = series[..., 1, :]
    real_out = apply_table(cosine, real_in) + sign * apply_table(sine, imag_in)
    imag_out = apply_table(cosine, imag_in) - sign * apply_table(sine, real_in)
    return jnp.stack([real_out, imag_out], axis=-2) * factor


def pair_prod(first, second):
    first_re = first[..., 0, :]
    first_im = first[..., 1, :]
    second_re = second[..., 0, :]
    second_im = second[..., 1, :]
    return jnp.stack(
        [first_re * second_re - first_im * second_im, first_re * second_im + first_im * second_re],
        axis=-2,
    )


def pair_mul(first, second):
    products = jnp.einsum("bsij,btjk->bstik", first, second, precision=PRECISE)
    return jnp.stack(
        [products[:, 0, 0] - products[:, 1, 1], products[:, 0, 1] + products[:, 1, 0]], axis=1
    )


def dagger(matrix):
    swapped = jnp.swapaxes(matrix, -1, -2)
    return jnp.stack([swapped[:, 0], -swapped[:, 1]], axis=1)


def newton(system, twice_eye):
    real_d = jnp.diagonal(system[:, 0], axis1=-2, axis2=-1)
    imag_d = jnp.diagonal(system[:, 1], axis1=-2, axis2=-1)
    denominator = real_d * real_d + imag_d * imag_d
    inverse_re = real_d / denominator
    inverse_im = -imag_d / denominator
    scaled_re = system[:, 0] * inverse_re[:, None, :] - system[:, 1] * inverse_im[:, None, :]
    scaled_im = system[:, 0] * inverse_im[:, None, :] + system[:, 1] * inverse_re[:, None, :]
    inner_re = twice_eye[:, 0] - scaled_re
    inner_im = -scaled_im
    approx = jnp.stack(
        [
            inverse_re[:, :, None] * inner_re - inverse_im[:, :, None] * inner_im,
            inverse_re[:, :, None] * inner_im + inverse_im[:, :, None] * inner_re,
        ],
        axis=1,
    )
    approx = pair_mul(approx, twice_eye - pair_mul(system, approx))
    return approx


def polar_terms(direct, mirrored, scale_p):
    reflected = jnp.concatenate([mirrored[:, :1], jnp.flip(mirrored[:, 1:], axis=1)], axis=1)
    correlated = pair_prod(direct, reflected[:, :, ::-1])
    return jnp.stack([correlated[..., 1, :], -correlated[..., 0, :]], axis=-2) * scale_p


def self_energy(direct, screened, out_cos, out_sin, length, scale_p):
    convolved = transform(pair_prod(direct, screened), out_cos, out_sin, -1.0, 1.0 / length)
    return jnp.stack([-convolved[..., 1, :], convolved[..., 0, :]], axis=-2) * (
        SIGMA_SCALE * scale_p
    )


def on_device(lesser_in, greater_in, h_diag, coupling, contact, coulomb, tiles):
    k_local = lesser_in.shape[0]
    e_local = lesser_in.shape[1]
    block_count = lesser_in.shape[2]
    order_n = lesser_in.shape[-1]
    tile_order = order_n // 4
    diag_count = 4 * block_count
    devices_e = lax.axis_size("ea")
    devices_k = lax.axis_size("ka")
    e_total = e_local * devices_e
    length = 2 * e_total
    ret_local = tiles.shape[0] * tile_order * tile_order // devices_e
    offset = lax.axis_index("ea") * ret_local
    k_total = k_local * devices_k
    scale_p = 1.0 / math.sqrt(e_total)

    def layout(blocks):
        return arrange(jnp.take(tiles_of(jnp.moveaxis(blocks, 3, 2)), tiles, axis=-3), diag_count)

    greens = jnp.stack([layout(lesser_in), layout(greater_in)], axis=2)
    fwd_cos, fwd_sin = tables(length, e_total, length)
    full_cos, full_sin = tables(length, length, length)
    out_cos, out_sin = tables(e_total, length, length)
    coulomb_flat = arrange(jnp.take(tiles_of(coulomb), tiles, axis=-3), diag_count)
    outgoing = jnp.concatenate([greens, partner(greens, diag_count, tile_order)], axis=2)
    spectra = transform(
        lax.all_to_all(outgoing, "ea", split_axis=4, concat_axis=1, tiled=True),
        fwd_cos,
        fwd_sin,
        1.0,
        1.0,
    )
    direct = spectra[:, :, :2]
    mirrored = spectra[:, :, 2:]
    turned = polar_terms(direct, mirrored, scale_p)
    weight = lax.dynamic_slice_in_dim(coulomb_flat, offset, ret_local) ** 2
    lags = transform(jnp.sum(turned, axis=0, keepdims=True), full_cos, full_sin, -1.0, 1.0 / length)
    summed = lax.psum(lags, "ka")
    screened = transform(summed * (weight / k_total), full_cos, full_sin, 1.0, 1.0)
    sigma = self_energy(direct, screened, out_cos, out_sin, length, scale_p)
    returned = lax.all_to_all(sigma, "ea", split_axis=1, concat_axis=4, tiled=True)
    pieces = unarrange(returned, diag_count, tile_order)
    empty = jnp.zeros(pieces.shape[:-3] + (block_count * 16, tile_order, tile_order), jnp.float32)
    sigma_blocks = blocks_of(empty.at[..., tiles, :, :].set(pieces), block_count)
    sigma_ret = 0.5 * (sigma_blocks[:, :, 1] - sigma_blocks[:, :, 0])
    sigma_less = sigma_blocks[:, :, 0]
    batch = k_local * e_local
    identity = jnp.eye(order_n, dtype=jnp.float32)
    energy_idx = lax.axis_index("ea") * e_local + jnp.arange(e_local, dtype=jnp.int32)
    energies = -SPREAD + 2.0 * SPREAD * (energy_idx.astype(jnp.float32) + 0.5) / e_total
    energies = energies[None, :].reshape(batch)
    shifted = jnp.stack(
        [
            energies[:, None, None] * identity,
            jnp.broadcast_to(BROADEN * identity, (batch, order_n, order_n)),
        ],
        axis=1,
    )
    twice_eye = jnp.broadcast_to(
        jnp.stack([2.0 * identity, 0.0 * identity]), (batch, 2, order_n, order_n)
    )

    def per_energy(array_k):
        return array_k[:, None].reshape((batch,) + array_k.shape[1:])

    forward_r = []
    forward_l = []
    for blk_no in range(block_count):
        system = (
            shifted
            - per_energy(h_diag[:, blk_no])
            - sigma_ret[:, :, :, blk_no].reshape(batch, 2, order_n, order_n)
        )
        source = sigma_less[:, :, :, blk_no].reshape(batch, 2, order_n, order_n)
        if blk_no == 0:
            source = source + contact[:, :, 0].reshape(batch, 2, order_n, order_n)
        if blk_no == block_count - 1:
            source = source + contact[:, :, 1].reshape(batch, 2, order_n, order_n)
        if blk_no > 0:
            link = per_energy(coupling[:, blk_no - 1])
            system = system - pair_mul(dagger(link), pair_mul(forward_r[-1], link))
            source = source + pair_mul(dagger(link), pair_mul(forward_l[-1], link))
        green_r = newton(system, twice_eye)
        forward_r.append(green_r)
        forward_l.append(pair_mul(pair_mul(green_r, source), dagger(green_r)))
    retarded_list = [forward_r[-1]]
    lesser_list = [forward_l[-1]]
    blk_no = 0
    green_r = forward_r[blk_no]
    green_l = forward_l[blk_no]
    link = per_energy(coupling[:, blk_no])
    right_op = pair_mul(green_r, link)
    middle = pair_mul(right_op, retarded_list[0])
    new_r = green_r + pair_mul(middle, pair_mul(dagger(link), green_r))
    cross = pair_mul(middle, pair_mul(dagger(link), green_l))
    new_l = (
        green_l
        + pair_mul(pair_mul(right_op, lesser_list[0]), dagger(right_op))
        - cross
        - dagger(cross)
    )
    retarded_list.insert(0, new_r)
    lesser_list.insert(0, new_l)
    lesser = jnp.stack(lesser_list, axis=1)
    greater = jnp.stack(
        [
            lesser_list[blk_no] + retarded_list[blk_no] - dagger(retarded_list[blk_no])
            for blk_no in range(block_count)
        ],
        axis=1,
    )
    out_shape = (k_local, e_local, block_count, 2, order_n, order_n)
    return (lesser.reshape(out_shape), greater.reshape(out_shape))


MESH = pl.DeviceIdType.MESH
VMEM = pl.BlockSpec(memory_space=pltpu.VMEM)
SMEM = pl.BlockSpec(memory_space=pltpu.SMEM)
HBM = pl.BlockSpec(memory_space=pltpu.HBM)


def rolled(rows, shift):
    return pltpu.roll(rows, shift, rows.ndim - 2)


def sublane(shape):
    return lax.broadcasted_iota(jnp.int32, shape, len(shape) - 2) % 8


def crossed_rows(four):
    row = sublane(four[0].shape)
    top, first = row < 4, row % 4 < 2
    a, b, c, d = four
    out = []
    for left, right in (
        (jnp.where(top, a, rolled(c, 4)), jnp.where(top, b, rolled(d, 4))),
        (jnp.where(top, rolled(a, 4), c), jnp.where(top, rolled(b, 4), d)),
    ):
        out.append(jnp.where(first, left, rolled(right, 2)))
        out.append(jnp.where(first, rolled(left, 6), right))
    return out


def tile_place(tiles_ref, slot):
    tile = tiles_ref[slot]
    return tile // 16, tile % 16 // 4, tile % 4


def pack_tiles(tiles_ref, load):
    group = lax.broadcasted_iota(jnp.int32, (32, 128), 1) // 32
    slabs = [[load(blk, 32 * pos) for pos in range(4)] for blk in range(2)]
    parts = []
    for blk in range(2):
        part = slabs[blk][0]
        for pos in range(1, 4):
            part = jnp.where(group == pos, slabs[blk][pos], part)
        parts.append(part)
    for half in range(2):
        part = None
        for pos in range(4):
            blk, row, col = tile_place(tiles_ref, 8 + 4 * half + pos)
            slab = slabs[0][0]
            for index in range(1, 8):
                found = blk * 4 + row == index
                slab = jnp.where(found, slabs[index // 4][index % 4], slab)
            turn = (pos + 4 - col) % 4
            slab = jnp.where(turn % 2 == 1, pltpu.roll(slab, 32, 1), slab)
            slab = jnp.where(turn >= 2, pltpu.roll(slab, 64, 1), slab)
            part = slab if part is None else jnp.where(group == pos, slab, part)
        parts.append(part)
    return jnp.concatenate(parts, axis=0).reshape(16, 8, 128)


def exchange_kernel(
    n_k,
    n_e,
    tiles_hbm,
    l_hbm,
    g_hbm,
    c_hbm,
    out_ref,
    tiles_ref,
    l_ref,
    g_ref,
    c_ref,
    gt_ref,
    ct_ref,
    packed,
    weight_ref,
    held,
    sigma,
    back,
    load_sem,
    send_a,
    recv_a,
    send_b,
    recv_b,
):
    count = n_k * n_e
    half = n_e // 2
    my_k = lax.axis_index("ka")
    my_e = lax.axis_index("ea")
    me = my_k * n_e + my_e
    side = my_e // half

    loads = [
        pltpu.make_async_copy(source, target, load_sem.at[index])
        for index, (source, target) in enumerate(
            ((tiles_hbm, tiles_ref), (g_hbm, g_ref), (l_hbm, l_ref), (c_hbm, c_ref))
        )
    ]
    for load in loads:
        load.start()

    k_list = [(my_k + step) % n_k for step in range(n_k)]
    near = [side * half + (my_e + step) % half for step in range(half)]
    far = [(1 - side) * half + (my_e + step) % half for step in range(half)]
    others = [(k, e) for k in k_list for e in far]
    others += [(k, e) for k in k_list for e in near][1:]

    def remote(source, target, send_sem, recv_sem, k, e):
        return pltpu.make_async_remote_copy(
            src_ref=source,
            dst_ref=target,
            send_sem=send_sem,
            recv_sem=recv_sem,
            device_id={"ka": k, "ea": e},
            device_id_type=MESH,
        )

    def all_of(ref, send_sem, recv_sem):
        every = ref.at[pl.ds(0, count - 1)]
        return remote(every, every, send_sem, recv_sem, *others[0])

    barrier = pltpu.get_barrier_semaphore()
    for k, e in others:
        pl.semaphore_signal(barrier, inc=1, device_id={"ka": k, "ea": e}, device_id_type=MESH)

    def spread(ref, pieces):
        for index, piece in enumerate(crossed_rows(pieces)):
            start = index % 2 * 16
            ref[index // 2, start : start + 16] = piece

    def pack(ref):
        return [
            pack_tiles(tiles_ref, lambda blk, row: ref[blk, part, pl.ds(row, 32), :])
            for part in range(2)
        ]

    loads[0].wait()
    loads[1].wait()
    for blk in range(2):
        for part in range(2):
            gt_ref[blk, part] = g_ref[blk, part].T
    greater_rows = pack(gt_ref)
    loads[2].wait()
    spread(packed, pack(l_ref) + greater_rows)
    pl.semaphore_wait(barrier, count - 1)
    for chunk in range(2):
        for k, e in others:
            source = packed.at[chunk, k * n_e + e]
            target = held.at[chunk, me]
            remote(source, target, send_a.at[chunk], recv_a.at[chunk], k, e).start()

    held[0, me] = packed[0, me]
    held[1, me] = packed[1, me]
    loads[3].wait()
    for blk in range(2):
        ct_ref[blk] = c_ref[blk].T
    for kind, ref in ((0, c_ref), (1, ct_ref)):
        bare = pack_tiles(tiles_ref, lambda blk, row: ref[blk, pl.ds(row, 32), :])
        spread(weight_ref.at[kind], [bare * bare * (SIGMA_SCALE / (n_e * n_k))] * 4)

    lags = 2 * n_e - 1
    row = sublane((8, 128))
    top, first_pair = row < 4, row % 4 < 2
    sign = jnp.where(first_pair, 1.0, -1.0)

    def swap(rows):
        return jnp.where(first_pair, rolled(rows, 6), rolled(rows, 2))

    def greens(chunk, pair):
        both = []
        for e in range(n_e):
            one = held[chunk, 2 * pair * n_e + e]
            two = held[chunk, (2 * pair + 1) * n_e + e]
            lesser = jnp.where(top, one, rolled(two, 4))
            both.append((lesser, jnp.where(top, rolled(one, 4), two)))
        return [piece[0] for piece in both], [piece[1] for piece in both]

    def work(chunk, carry):
        all_of(held.at[chunk], send_a.at[chunk], recv_a.at[chunk]).wait_recv()

        def correlate(pair, sums):
            plain, crossed = list(sums[0]), list(sums[1])
            lesser, greater = greens(chunk, pair)
            for e_two in range(n_e):
                swapped = swap(greater[e_two])
                for e_one in range(n_e):
                    lag = e_one - e_two + n_e - 1
                    plain[lag] = plain[lag] + lesser[e_one] * greater[e_two]
                    crossed[lag] = crossed[lag] + lesser[e_one] * swapped
            return tuple(plain), tuple(crossed)

        zero = jnp.zeros((8, 128), jnp.float32)
        plain, crossed = lax.fori_loop(
            0, n_k // 2, correlate, ((zero,) * lags, (zero,) * lags)
        )
        plain = [total + rolled(total, 4) for total in plain]
        crossed = [total + rolled(total, 4) for total in crossed]
        real = [sign * (total - rolled(total, 2)) for total in plain]
        imag = [-sign * (total + rolled(total, 2)) for total in crossed]
        weights = weight_ref[0, chunk, me], weight_ref[1, chunk, me]

        def convolve(turn, inner):
            pair = (my_k // 2 + turn) % (n_k // 2)
            results = []
            for kind, green in enumerate(greens(chunk, pair)):
                swapped = [swap(piece) for piece in green]
                for e_out in range(n_e):
                    total = None
                    for e_in in range(n_e):
                        lag = e_out - e_in if kind == 0 else e_in - e_out
                        lag = lag + n_e - 1
                        term = green[e_in] * real[lag] + swapped[e_in] * imag[lag]
                        total = term if total is None else total + term
                    results.append(total * weights[kind])
            for e in range(n_e):
                less, more = results[e], results[n_e + e]
                sigma[chunk, 2 * pair * n_e + e] = jnp.where(top, less, rolled(more, 4))
                sigma[chunk, (2 * pair + 1) * n_e + e] = jnp.where(top, rolled(less, 4), more)

            def send(k, e):
                source = sigma.at[chunk, k * n_e + e]
                target = back.at[chunk, me]
                remote(source, target, send_b.at[chunk], recv_b.at[chunk], k, e).start()

            for e in far + near[1:]:
                for k in (2 * pair, 2 * pair + 1):
                    send(k, e)
            for k in (2 * pair, 2 * pair + 1):

                @pl.when(k != my_k)
                def _():
                    send(k, my_e)

            return inner

        lax.fori_loop(0, n_k // 2, convolve, 0)
        back[chunk, me] = sigma[chunk, me]
        return carry

    lax.fori_loop(0, 2, work, 0)
    for chunk in range(2):
        all_of(held.at[chunk], send_a.at[chunk], recv_a.at[chunk]).wait_send()
        all_of(back.at[chunk], send_b.at[chunk], recv_b.at[chunk]).wait_send()
        all_of(back.at[chunk], send_b.at[chunk], recv_b.at[chunk]).wait_recv()
    out_ref[...] = back[...]


def split(value):
    high = value.astype(jnp.bfloat16)
    return high, (value - high.astype(jnp.float32)).astype(jnp.bfloat16)


def square_form(rows):
    real, imag = rows[:, :128], rows[:, 128:]
    return split(jnp.concatenate([rows, jnp.concatenate([-imag, real], axis=1)], axis=0))


def times(first, second, contract=0):
    dims = (((1,), (contract,)), ((), ()))

    def dot(left, right):
        return lax.dot_general(left, right, dims, preferred_element_type=jnp.float32)

    high, low = first
    both = dot(jnp.concatenate([high, low], axis=0), second[0])
    return both[:128] + (dot(high, second[1]) + both[128:])


def adjoint(rows):
    return jnp.concatenate([rows[:, :128].T, -rows[:, 128:].T], axis=1)


def invert_rows(system, eye):
    real_m, imag_m = system[:, :128], system[:, 128:]
    only_re = jnp.where(eye, real_m, 0.0)
    only_im = jnp.where(eye, imag_m, 0.0)

    def reciprocal(axis):
        real_d = jnp.sum(only_re, axis=axis, keepdims=True)
        imag_d = jnp.sum(only_im, axis=axis, keepdims=True)
        denominator = real_d * real_d + imag_d * imag_d
        return real_d / denominator, -imag_d / denominator

    row_re, row_im = reciprocal(0)
    col_re, col_im = reciprocal(1)
    twice = jnp.where(eye, 2.0, 0.0)
    inner_re = twice - (real_m * row_re - imag_m * row_im)
    inner_im = -(real_m * row_im + imag_m * row_re)
    approx = jnp.concatenate(
        [col_re * inner_re - col_im * inner_im, col_re * inner_im + col_im * inner_re], axis=1
    )
    product = times(split(system), square_form(approx))
    rest = jnp.concatenate([twice - product[:, :128], -product[:, 128:]], axis=1)
    return times(split(approx), square_form(rest))


def sweep_kernel(
    tiles_hbm,
    energy_ref,
    sigma_ref,
    h_ref,
    link_ref,
    contact_ref,
    lesser_ref,
    greater_ref,
    blocks,
    tiles_ref,
    load_sem,
):
    load = pltpu.make_async_copy(tiles_hbm, tiles_ref, load_sem)
    load.start()
    group = lax.broadcasted_iota(jnp.int32, (32, 128), 1) // 32
    pieces = []
    parts = crossed_rows(
        [sigma_ref[index // 2, index % 2 * 16 : index % 2 * 16 + 16] for index in range(4)]
    )
    for kind in range(2):
        for part in range(2):
            packed = parts[2 * kind + part].reshape(128, 128)
            pieces.append((kind, part, packed[64:]))
            for blk in range(2):
                for pos in range(4):
                    blocks[kind, part, blk, 32 * pos : 32 * pos + 32, :] = jnp.where(
                        group == pos, packed[32 * blk : 32 * blk + 32], 0.0
                    )
    load.wait()
    for slot in range(8):
        blk, row, col = tile_place(tiles_ref, 8 + slot)
        start = 32 * (slot // 4)
        rows = pl.ds(pl.multiple_of(32 * row, 32), 32)
        for kind, part, packed in pieces:
            slab = pltpu.roll(packed[start : start + 32], (col + 4 - slot % 4) % 4 * 32, 1)
            blocks[kind, part, blk, rows, :] = jnp.where(
                group == col, slab, blocks[kind, part, blk, rows, :]
            )

    eye = lax.broadcasted_iota(jnp.int32, (128, 128), 0) == lax.broadcasted_iota(
        jnp.int32, (128, 128), 1
    )
    shift = jnp.concatenate(
        [jnp.where(eye, energy_ref[0], 0.0), jnp.where(eye, BROADEN, 0.0)], axis=1
    )

    def rows_of(ref, *index):
        return jnp.concatenate([ref[*index, 0], ref[*index, 1]], axis=1)

    def system_source(blk):
        less = jnp.concatenate([blocks[0, 0, blk], blocks[0, 1, blk]], axis=1)
        more = jnp.concatenate([blocks[1, 0, blk].T, blocks[1, 1, blk].T], axis=1)
        system = shift - rows_of(h_ref, blk) - 0.5 * (more - less)
        return system, less + rows_of(contact_ref, blk)

    link = rows_of(link_ref, 0)
    link_square = square_form(link)
    link_adjoint = split(adjoint(link))

    system_0, source_0 = system_source(0)
    system_1, source_1 = system_source(1)
    gr_0 = invert_rows(system_0, eye)
    gr_0_rows, gr_0_square = split(gr_0), square_form(gr_0)
    right_op = times(gr_0_rows, link_square)
    right_square = square_form(right_op)
    system_1 = system_1 - times(link_adjoint, right_square)
    gr_1 = invert_rows(system_1, eye)
    gl_0 = times(split(times(gr_0_rows, square_form(source_0))), gr_0_square, 1)
    left_l = times(link_adjoint, square_form(gl_0))
    source_1 = source_1 + times(split(left_l), link_square)
    gr_1_square = square_form(gr_1)
    gl_1 = times(split(times(split(gr_1), square_form(source_1))), gr_1_square, 1)
    left_r = times(link_adjoint, gr_0_square)
    right_rows = split(right_op)
    middle = split(times(right_rows, gr_1_square))
    full_r = gr_0 + times(middle, square_form(left_r))
    cross = times(middle, square_form(left_l))
    inner = times(split(times(right_rows, square_form(gl_1))), right_square, 1)
    full_l = gl_0 + inner - cross - adjoint(cross)
    for blk, retarded, lesser in ((0, full_r, full_l), (1, gr_1, gl_1)):
        greater = lesser + retarded - adjoint(retarded)
        for part in range(2):
            lesser_ref[blk, part] = lesser[:, 128 * part : 128 * part + 128]
            greater_ref[blk, part] = greater[:, 128 * part : 128 * part + 128]


def in_hbm(array):
    return pltpu.with_memory_space_constraint(array, pltpu.HBM)


def small_device(n_k, n_e, lesser_in, greater_in, h_diag, coupling, contact, coulomb, tiles):
    count = n_k * n_e
    f32 = jnp.float32
    limit = pltpu.CompilerParams(vmem_limit_bytes=32 * 1024 * 1024)
    slots = (2, count, 8, 128)
    blocks = pltpu.VMEM((2, 2, 128, 128), f32)
    plane = pltpu.VMEM((2, 128, 128), f32)
    sigma = pl.pallas_call(
        partial(exchange_kernel, n_k, n_e),
        out_shape=jax.ShapeDtypeStruct(slots, f32),
        in_specs=[HBM] * 4,
        out_specs=VMEM,
        scratch_shapes=[pltpu.SMEM((16,), jnp.int32), blocks, blocks, plane, blocks, plane]
        + [pltpu.VMEM(slots, f32), pltpu.VMEM((2,) + slots, f32)]
        + [pltpu.VMEM(slots, f32)] * 3
        + [pltpu.SemaphoreType.DMA((4,))]
        + [pltpu.SemaphoreType.DMA((2,))] * 4,
        compiler_params=pltpu.CompilerParams(
            collective_id=0, has_side_effects=True, vmem_limit_bytes=32 * 1024 * 1024
        ),
        name="exchange",
    )(*(in_hbm(array) for array in (tiles, lesser_in[0, 0], greater_in[0, 0], coulomb)))
    energy = -SPREAD + 2.0 * SPREAD * (lax.axis_index("ea").astype(f32) + 0.5) / n_e
    lesser, greater = pl.pallas_call(
        sweep_kernel,
        out_shape=(jax.ShapeDtypeStruct((2, 2, 128, 128), f32),) * 2,
        in_specs=[HBM, SMEM, VMEM, VMEM, VMEM, VMEM],
        out_specs=(VMEM, VMEM),
        scratch_shapes=[
            pltpu.VMEM((2, 2, 2, 128, 128), f32),
            pltpu.SMEM((16,), jnp.int32),
            pltpu.SemaphoreType.DMA,
        ],
        compiler_params=limit,
        name="sweep",
    )(
        in_hbm(tiles),
        energy.reshape(1),
        sigma,
        h_diag[0],
        coupling[0],
        contact[0, 0],
    )
    return lesser[None, None], greater[None, None]


def per_device(mesh, lesser_in, *rest):
    n_k, n_e = mesh.shape["ka"], mesh.shape["ea"]
    fits = n_k * n_e == 32 and lesser_in.shape == (1, 1, 2, 2, 128, 128) and rest[-1].shape == (16,)
    if fits:
        return small_device(n_k, n_e, lesser_in, *rest)
    return on_device(lesser_in, *rest)


def solution(mesh):
    in_specs = (
        P("ka", "ea", None, None, None, None),
        P("ka", "ea", None, None, None, None),
        P("ka", None, None, None, None),
        P("ka", None, None, None, None),
        P("ka", "ea", None, None, None, None),
        P(),
        P(),
    )
    out_specs = (P("ka", "ea", None, None, None, None), P("ka", "ea", None, None, None, None))
    return jax.shard_map(
        partial(per_device, mesh), mesh=mesh, in_specs=in_specs, out_specs=out_specs, check_vma=False
    )
```

```python
import math
from functools import partial

import jax
import jax.numpy as jnp
import numpy as np
from jax import lax
from jax.experimental import pallas as pl
from jax.experimental.pallas import tpu as pltpu
from jax.sharding import PartitionSpec as P

BROADEN = 0.3
SPREAD = 0.05
SIGMA_SCALE = 0.01
PRECISE = lax.Precision.HIGHEST


def tiles_of(blocks):
    leading = blocks.shape[:-3]
    lead_rank = len(leading)
    block_count = blocks.shape[-3]
    tile_order = blocks.shape[-1] // 4
    viewed = blocks.reshape(leading + (block_count, 4, tile_order, 4, tile_order))
    viewed = jnp.moveaxis(viewed, lead_rank + 3, lead_rank + 2)
    return viewed.reshape(leading + (block_count * 16, tile_order, tile_order))


def blocks_of(pieces, block_count):
    leading = pieces.shape[:-3]
    lead_rank = len(leading)
    tile_order = pieces.shape[-1]
    viewed = pieces.reshape(leading + (block_count, 4, 4, tile_order, tile_order))
    viewed = jnp.moveaxis(viewed, lead_rank + 2, lead_rank + 3)
    return viewed.reshape(leading + (block_count, 4 * tile_order, 4 * tile_order))


def diag_order(tile_order):
    listing = [row_pos * tile_order + row_pos for row_pos in range(tile_order)]
    for row_pos in range(tile_order):
        for col_pos in range(row_pos + 1, tile_order):
            listing.append(row_pos * tile_order + col_pos)
            listing.append(col_pos * tile_order + row_pos)
    forward = np.array(listing, np.int32)
    return (forward, np.argsort(forward).astype(np.int32))


def arrange(pieces, diag_count):
    leading = pieces.shape[:-3]
    tile_order = pieces.shape[-1]
    forward = diag_order(tile_order)[0]
    diagonal = pieces[..., :diag_count, :, :].reshape(
        leading + (diag_count, tile_order * tile_order)
    )
    diagonal = jnp.take(diagonal, forward, axis=-1).reshape(leading + (-1,))
    paired = pieces[..., diag_count:, :, :].reshape(leading + (-1, 2, tile_order, tile_order))
    paired = jnp.stack([paired[..., 0, :, :], jnp.swapaxes(paired[..., 1, :, :], -1, -2)], axis=-1)
    return jnp.concatenate([diagonal, paired.reshape(leading + (-1,))], axis=-1)


def unarrange(flattened, diag_count, tile_order):
    leading = flattened.shape[:-1]
    square = tile_order * tile_order
    inverse = diag_order(tile_order)[1]
    diagonal = flattened[..., : diag_count * square].reshape(leading + (diag_count, square))
    diagonal = jnp.take(diagonal, inverse, axis=-1).reshape(
        leading + (diag_count, tile_order, tile_order)
    )
    paired = flattened[..., diag_count * square :].reshape(
        leading + (-1, tile_order, tile_order, 2)
    )
    paired = jnp.stack([paired[..., 0], jnp.swapaxes(paired[..., 1], -1, -2)], axis=-3)
    paired = paired.reshape(leading + (-1, tile_order, tile_order))
    return jnp.concatenate([diagonal, paired], axis=-3)


def partner(flattened, diag_count, tile_order):
    size_last = flattened.shape[-1]
    square = tile_order * tile_order
    flipped = flattened.reshape(flattened.shape[:-1] + (size_last // 2, 2))[..., ::-1].reshape(
        flattened.shape
    )
    position = jnp.arange(size_last, dtype=jnp.int32)
    itself = (position < diag_count * square) & (position % square < tile_order)
    return jnp.where(itself, flattened, flipped)


def tables(rows_count, cols_count, length):
    phases = (
        jnp.arange(rows_count, dtype=jnp.int32)[:, None]
        * jnp.arange(cols_count, dtype=jnp.int32)[None, :]
        % length
    )
    angles = phases.astype(jnp.float32) * (2.0 * math.pi / length)
    return (jnp.cos(angles), jnp.sin(angles))


def apply_table(coeffs, values):
    return jnp.einsum("fe,keal->kfal", coeffs, values, precision=PRECISE)


def transform(series, cosine, sine, sign, factor):
    real_in = series[..., 0, :]
    imag_in = series[..., 1, :]
    real_out = apply_table(cosine, real_in) + sign * apply_table(sine, imag_in)
    imag_out = apply_table(cosine, imag_in) - sign * apply_table(sine, real_in)
    return jnp.stack([real_out, imag_out], axis=-2) * factor


def pair_prod(first, second):
    first_re = first[..., 0, :]
    first_im = first[..., 1, :]
    second_re = second[..., 0, :]
    second_im = second[..., 1, :]
    return jnp.stack(
        [first_re * second_re - first_im * second_im, first_re * second_im + first_im * second_re],
        axis=-2,
    )


def pair_mul(first, second):
    products = jnp.einsum("bsij,btjk->bstik", first, second, precision=PRECISE)
    return jnp.stack(
        [products[:, 0, 0] - products[:, 1, 1], products[:, 0, 1] + products[:, 1, 0]], axis=1
    )


def dagger(matrix):
    swapped = jnp.swapaxes(matrix, -1, -2)
    return jnp.stack([swapped[:, 0], -swapped[:, 1]], axis=1)


def newton(system, twice_eye):
    real_d = jnp.diagonal(system[:, 0], axis1=-2, axis2=-1)
    imag_d = jnp.diagonal(system[:, 1], axis1=-2, axis2=-1)
    denominator = real_d * real_d + imag_d * imag_d
    inverse_re = real_d / denominator
    inverse_im = -imag_d / denominator
    scaled_re = system[:, 0] * inverse_re[:, None, :] - system[:, 1] * inverse_im[:, None, :]
    scaled_im = system[:, 0] * inverse_im[:, None, :] + system[:, 1] * inverse_re[:, None, :]
    inner_re = twice_eye[:, 0] - scaled_re
    inner_im = -scaled_im
    approx = jnp.stack(
        [
            inverse_re[:, :, None] * inner_re - inverse_im[:, :, None] * inner_im,
            inverse_re[:, :, None] * inner_im + inverse_im[:, :, None] * inner_re,
        ],
        axis=1,
    )
    approx = pair_mul(approx, twice_eye - pair_mul(system, approx))
    return approx


def polar_terms(direct, mirrored, scale_p):
    reflected = jnp.concatenate([mirrored[:, :1], jnp.flip(mirrored[:, 1:], axis=1)], axis=1)
    correlated = pair_prod(direct, reflected[:, :, ::-1])
    return jnp.stack([correlated[..., 1, :], -correlated[..., 0, :]], axis=-2) * scale_p


def self_energy(direct, screened, out_cos, out_sin, length, scale_p):
    convolved = transform(pair_prod(direct, screened), out_cos, out_sin, -1.0, 1.0 / length)
    return jnp.stack([-convolved[..., 1, :], convolved[..., 0, :]], axis=-2) * (
        SIGMA_SCALE * scale_p
    )


def on_device(lesser_in, greater_in, h_diag, coupling, contact, coulomb, tiles):
    k_local = lesser_in.shape[0]
    e_local = lesser_in.shape[1]
    block_count = lesser_in.shape[2]
    order_n = lesser_in.shape[-1]
    tile_order = order_n // 4
    diag_count = 4 * block_count
    devices_e = lax.axis_size("ea")
    devices_k = lax.axis_size("ka")
    e_total = e_local * devices_e
    length = 2 * e_total
    ret_local = tiles.shape[0] * tile_order * tile_order // devices_e
    offset = lax.axis_index("ea") * ret_local
    k_total = k_local * devices_k
    scale_p = 1.0 / math.sqrt(e_total)

    def layout(blocks):
        return arrange(jnp.take(tiles_of(jnp.moveaxis(blocks, 3, 2)), tiles, axis=-3), diag_count)

    greens = jnp.stack([layout(lesser_in), layout(greater_in)], axis=2)
    fwd_cos, fwd_sin = tables(length, e_total, length)
    full_cos, full_sin = tables(length, length, length)
    out_cos, out_sin = tables(e_total, length, length)
    coulomb_flat = arrange(jnp.take(tiles_of(coulomb), tiles, axis=-3), diag_count)
    outgoing = jnp.concatenate([greens, partner(greens, diag_count, tile_order)], axis=2)
    spectra = transform(
        lax.all_to_all(outgoing, "ea", split_axis=4, concat_axis=1, tiled=True),
        fwd_cos,
        fwd_sin,
        1.0,
        1.0,
    )
    direct = spectra[:, :, :2]
    mirrored = spectra[:, :, 2:]
    turned = polar_terms(direct, mirrored, scale_p)
    weight = lax.dynamic_slice_in_dim(coulomb_flat, offset, ret_local) ** 2
    lags = transform(jnp.sum(turned, axis=0, keepdims=True), full_cos, full_sin, -1.0, 1.0 / length)
    summed = lax.psum(lags, "ka")
    screened = transform(summed * (weight / k_total), full_cos, full_sin, 1.0, 1.0)
    sigma = self_energy(direct, screened, out_cos, out_sin, length, scale_p)
    returned = lax.all_to_all(sigma, "ea", split_axis=1, concat_axis=4, tiled=True)
    pieces = unarrange(returned, diag_count, tile_order)
    empty = jnp.zeros(pieces.shape[:-3] + (block_count * 16, tile_order, tile_order), jnp.float32)
    sigma_blocks = blocks_of(empty.at[..., tiles, :, :].set(pieces), block_count)
    sigma_ret = 0.5 * (sigma_blocks[:, :, 1] - sigma_blocks[:, :, 0])
    sigma_less = sigma_blocks[:, :, 0]
    batch = k_local * e_local
    identity = jnp.eye(order_n, dtype=jnp.float32)
    energy_idx = lax.axis_index("ea") * e_local + jnp.arange(e_local, dtype=jnp.int32)
    energies = -SPREAD + 2.0 * SPREAD * (energy_idx.astype(jnp.float32) + 0.5) / e_total
    energies = energies[None, :].reshape(batch)
    shifted = jnp.stack(
        [
            energies[:, None, None] * identity,
            jnp.broadcast_to(BROADEN * identity, (batch, order_n, order_n)),
        ],
        axis=1,
    )
    twice_eye = jnp.broadcast_to(
        jnp.stack([2.0 * identity, 0.0 * identity]), (batch, 2, order_n, order_n)
    )

    def per_energy(array_k):
        return array_k[:, None].reshape((batch,) + array_k.shape[1:])

    forward_r = []
    forward_l = []
    for blk_no in range(block_count):
        system = (
            shifted
            - per_energy(h_diag[:, blk_no])
            - sigma_ret[:, :, :, blk_no].reshape(batch, 2, order_n, order_n)
        )
        source = sigma_less[:, :, :, blk_no].reshape(batch, 2, order_n, order_n)
        if blk_no == 0:
            source = source + contact[:, :, 0].reshape(batch, 2, order_n, order_n)
        if blk_no == block_count - 1:
            source = source + contact[:, :, 1].reshape(batch, 2, order_n, order_n)
        if blk_no > 0:
            link = per_energy(coupling[:, blk_no - 1])
            system = system - pair_mul(dagger(link), pair_mul(forward_r[-1], link))
            source = source + pair_mul(dagger(link), pair_mul(forward_l[-1], link))
        green_r = newton(system, twice_eye)
        forward_r.append(green_r)
        forward_l.append(pair_mul(pair_mul(green_r, source), dagger(green_r)))
    retarded_list = [forward_r[-1]]
    lesser_list = [forward_l[-1]]
    blk_no = 0
    green_r = forward_r[blk_no]
    green_l = forward_l[blk_no]
    link = per_energy(coupling[:, blk_no])
    right_op = pair_mul(green_r, link)
    middle = pair_mul(right_op, retarded_list[0])
    new_r = green_r + pair_mul(middle, pair_mul(dagger(link), green_r))
    cross = pair_mul(middle, pair_mul(dagger(link), green_l))
    new_l = (
        green_l
        + pair_mul(pair_mul(right_op, lesser_list[0]), dagger(right_op))
        - cross
        - dagger(cross)
    )
    retarded_list.insert(0, new_r)
    lesser_list.insert(0, new_l)
    lesser = jnp.stack(lesser_list, axis=1)
    greater = jnp.stack(
        [
            lesser_list[blk_no] + retarded_list[blk_no] - dagger(retarded_list[blk_no])
            for blk_no in range(block_count)
        ],
        axis=1,
    )
    out_shape = (k_local, e_local, block_count, 2, order_n, order_n)
    return (lesser.reshape(out_shape), greater.reshape(out_shape))


MESH = pl.DeviceIdType.MESH
VMEM = pl.BlockSpec(memory_space=pltpu.VMEM)
SMEM = pl.BlockSpec(memory_space=pltpu.SMEM)
HBM = pl.BlockSpec(memory_space=pltpu.HBM)


def rolled(rows, shift):
    return pltpu.roll(rows, shift, rows.ndim - 2)


def sublane(shape):
    return lax.broadcasted_iota(jnp.int32, shape, len(shape) - 2) % 8


def crossed_rows(four):
    row = sublane(four[0].shape)
    top, first = row < 4, row % 4 < 2
    a, b, c, d = four
    out = []
    for left, right in (
        (jnp.where(top, a, rolled(c, 4)), jnp.where(top, b, rolled(d, 4))),
        (jnp.where(top, rolled(a, 4), c), jnp.where(top, rolled(b, 4), d)),
    ):
        out.append(jnp.where(first, left, rolled(right, 2)))
        out.append(jnp.where(first, rolled(left, 6), right))
    return out


def tile_place(tiles_ref, slot):
    tile = tiles_ref[slot]
    return tile // 16, tile % 16 // 4, tile % 4


def pack_tiles(tiles_ref, load):
    group = lax.broadcasted_iota(jnp.int32, (32, 128), 1) // 32
    slabs = [[load(blk, 32 * pos) for pos in range(4)] for blk in range(2)]
    parts = []
    for blk in range(2):
        part = slabs[blk][0]
        for pos in range(1, 4):
            part = jnp.where(group == pos, slabs[blk][pos], part)
        parts.append(part)
    for half in range(2):
        part = None
        for pos in range(4):
            blk, row, col = tile_place(tiles_ref, 8 + 4 * half + pos)
            slab = slabs[0][0]
            for index in range(1, 8):
                found = blk * 4 + row == index
                slab = jnp.where(found, slabs[index // 4][index % 4], slab)
            turn = (pos + 4 - col) % 4
            slab = jnp.where(turn % 2 == 1, pltpu.roll(slab, 32, 1), slab)
            slab = jnp.where(turn >= 2, pltpu.roll(slab, 64, 1), slab)
            part = slab if part is None else jnp.where(group == pos, slab, part)
        parts.append(part)
    return jnp.concatenate(parts, axis=0).reshape(16, 8, 128)


def exchange_kernel(
    n_k,
    n_e,
    tiles_hbm,
    l_hbm,
    g_hbm,
    c_hbm,
    out_ref,
    tiles_ref,
    l_ref,
    g_ref,
    c_ref,
    gt_ref,
    ct_ref,
    packed,
    weight_ref,
    held,
    sigma,
    back,
    load_sem,
    send_a,
    recv_a,
    send_b,
    recv_b,
):
    count = n_k * n_e
    half = n_e // 2
    my_k = lax.axis_index("ka")
    my_e = lax.axis_index("ea")
    me = my_k * n_e + my_e
    side = my_e // half

    loads = [
        pltpu.make_async_copy(source, target, load_sem.at[index])
        for index, (source, target) in enumerate(
            ((tiles_hbm, tiles_ref), (g_hbm, g_ref), (l_hbm, l_ref), (c_hbm, c_ref))
        )
    ]
    for load in loads:
        load.start()

    k_list = [(my_k + step) % n_k for step in range(n_k)]
    near = [side * half + (my_e + step) % half for step in range(half)]
    far = [(1 - side) * half + (my_e + step) % half for step in range(half)]
    others = [(k, e) for k in k_list for e in far]
    others += [(k, e) for k in k_list for e in near][1:]

    def remote(source, target, send_sem, recv_sem, k, e):
        return pltpu.make_async_remote_copy(
            src_ref=source,
            dst_ref=target,
            send_sem=send_sem,
            recv_sem=recv_sem,
            device_id={"ka": k, "ea": e},
            device_id_type=MESH,
        )

    def all_of(ref, send_sem, recv_sem):
        every = ref.at[pl.ds(0, count - 1)]
        return remote(every, every, send_sem, recv_sem, *others[0])

    barrier = pltpu.get_barrier_semaphore()
    for k, e in others:
        pl.semaphore_signal(barrier, inc=1, device_id={"ka": k, "ea": e}, device_id_type=MESH)

    def spread(ref, pieces):
        for index, piece in enumerate(crossed_rows(pieces)):
            start = index % 2 * 16
            ref[index // 2, start : start + 16] = piece

    def pack(ref):
        return [
            pack_tiles(tiles_ref, lambda blk, row: ref[blk, part, pl.ds(row, 32), :])
            for part in range(2)
        ]

    loads[0].wait()
    loads[1].wait()
    for blk in range(2):
        for part in range(2):
            gt_ref[blk, part] = g_ref[blk, part].T
    greater_rows = pack(gt_ref)
    loads[2].wait()
    spread(packed, pack(l_ref) + greater_rows)
    pl.semaphore_wait(barrier, count - 1)
    for chunk in range(2):
        for k, e in others:
            source = packed.at[chunk, k * n_e + e]
            target = held.at[chunk, me]
            remote(source, target, send_a.at[chunk], recv_a.at[chunk], k, e).start()

    held[0, me] = packed[0, me]
    held[1, me] = packed[1, me]
    loads[3].wait()
    for blk in range(2):
        ct_ref[blk] = c_ref[blk].T
    for kind, ref in ((0, c_ref), (1, ct_ref)):
        bare = pack_tiles(tiles_ref, lambda blk, row: ref[blk, pl.ds(row, 32), :])
        spread(weight_ref.at[kind], [bare * bare * (SIGMA_SCALE / (n_e * n_k))] * 4)

    lags = 2 * n_e - 1
    row = sublane((8, 128))
    top, first_pair = row < 4, row % 4 < 2
    sign = jnp.where(first_pair, 1.0, -1.0)

    def swap(rows):
        return jnp.where(first_pair, rolled(rows, 6), rolled(rows, 2))

    def greens(chunk, pair):
        both = []
        for e in range(n_e):
            one = held[chunk, 2 * pair * n_e + e]
            two = held[chunk, (2 * pair + 1) * n_e + e]
            lesser = jnp.where(top, one, rolled(two, 4))
            both.append((lesser, jnp.where(top, rolled(one, 4), two)))
        return [piece[0] for piece in both], [piece[1] for piece in both]

    def work(chunk, carry):
        all_of(held.at[chunk], send_a.at[chunk], recv_a.at[chunk]).wait_recv()

        def correlate(pair, sums):
            plain, crossed = list(sums[0]), list(sums[1])
            lesser, greater = greens(chunk, pair)
            for e_two in range(n_e):
                swapped = swap(greater[e_two])
                for e_one in range(n_e):
                    lag = e_one - e_two + n_e - 1
                    plain[lag] = plain[lag] + lesser[e_one] * greater[e_two]
                    crossed[lag] = crossed[lag] + lesser[e_one] * swapped
            return tuple(plain), tuple(crossed)

        zero = jnp.zeros((8, 128), jnp.float32)
        plain, crossed = lax.fori_loop(
            0, n_k // 2, correlate, ((zero,) * lags, (zero,) * lags)
        )
        plain = [total + rolled(total, 4) for total in plain]
        crossed = [total + rolled(total, 4) for total in crossed]
        real = [sign * (total - rolled(total, 2)) for total in plain]
        imag = [-sign * (total + rolled(total, 2)) for total in crossed]
        weights = weight_ref[0, chunk, me], weight_ref[1, chunk, me]

        def convolve(turn, inner):
            pair = (my_k // 2 + turn) % (n_k // 2)
            results = []
            for kind, green in enumerate(greens(chunk, pair)):
                swapped = [swap(piece) for piece in green]
                for e_out in range(n_e):
                    total = None
                    for e_in in range(n_e):
                        lag = e_out - e_in if kind == 0 else e_in - e_out
                        lag = lag + n_e - 1
                        term = green[e_in] * real[lag] + swapped[e_in] * imag[lag]
                        total = term if total is None else total + term
                    results.append(total * weights[kind])
            for e in range(n_e):
                less, more = results[e], results[n_e + e]
                sigma[chunk, 2 * pair * n_e + e] = jnp.where(top, less, rolled(more, 4))
                sigma[chunk, (2 * pair + 1) * n_e + e] = jnp.where(top, rolled(less, 4), more)

            def send(k, e):
                source = sigma.at[chunk, k * n_e + e]
                target = back.at[chunk, me]
                remote(source, target, send_b.at[chunk], recv_b.at[chunk], k, e).start()

            for e in far + near[1:]:
                for k in (2 * pair, 2 * pair + 1):
                    send(k, e)
            for k in (2 * pair, 2 * pair + 1):

                @pl.when(k != my_k)
                def _():
                    send(k, my_e)

            return inner

        lax.fori_loop(0, n_k // 2, convolve, 0)
        back[chunk, me] = sigma[chunk, me]
        return carry

    lax.fori_loop(0, 2, work, 0)
    for chunk in range(2):
        all_of(held.at[chunk], send_a.at[chunk], recv_a.at[chunk]).wait_send()
        all_of(back.at[chunk], send_b.at[chunk], recv_b.at[chunk]).wait_send()
        all_of(back.at[chunk], send_b.at[chunk], recv_b.at[chunk]).wait_recv()
    out_ref[...] = back[...]


def split(value):
    high = value.astype(jnp.bfloat16)
    return high, (value - high.astype(jnp.float32)).astype(jnp.bfloat16)


def square_form(rows):
    real, imag = rows[:, :128], rows[:, 128:]
    return split(jnp.concatenate([rows, jnp.concatenate([-imag, real], axis=1)], axis=0))


def times(first, second, contract=0):
    dims = (((1,), (contract,)), ((), ()))

    def dot(left, right):
        return lax.dot_general(left, right, dims, preferred_element_type=jnp.float32)

    high, low = first
    both = dot(jnp.concatenate([high, low], axis=0), second[0])
    return both[:128] + (dot(high, second[1]) + both[128:])


def adjoint(rows):
    return jnp.concatenate([rows[:, :128].T, -rows[:, 128:].T], axis=1)


def first_step(system, eye):
    real_m, imag_m = system[:, :128], system[:, 128:]
    only_re = jnp.where(eye, real_m, 0.0)
    only_im = jnp.where(eye, imag_m, 0.0)

    def reciprocal(axis):
        real_d = jnp.sum(only_re, axis=axis, keepdims=True)
        imag_d = jnp.sum(only_im, axis=axis, keepdims=True)
        denominator = real_d * real_d + imag_d * imag_d
        return real_d / denominator, -imag_d / denominator

    row_re, row_im = reciprocal(0)
    col_re, col_im = reciprocal(1)
    twice = jnp.where(eye, 2.0, 0.0)
    inner_re = twice - (real_m * row_re - imag_m * row_im)
    inner_im = -(real_m * row_im + imag_m * row_re)
    return jnp.concatenate(
        [col_re * inner_re - col_im * inner_im, col_re * inner_im + col_im * inner_re], axis=1
    )


def sweep_kernel(
    tiles_hbm,
    energy_ref,
    sigma_ref,
    h_ref,
    link_ref,
    contact_ref,
    lesser_ref,
    greater_ref,
    blocks,
    tiles_ref,
    load_sem,
):
    load = pltpu.make_async_copy(tiles_hbm, tiles_ref, load_sem)
    load.start()
    group = lax.broadcasted_iota(jnp.int32, (32, 128), 1) // 32
    pieces = []
    parts = crossed_rows(
        [sigma_ref[index // 2, index % 2 * 16 : index % 2 * 16 + 16] for index in range(4)]
    )
    for kind in range(2):
        for part in range(2):
            packed = parts[2 * kind + part].reshape(128, 128)
            pieces.append((kind, part, packed[64:]))
            for blk in range(2):
                for pos in range(4):
                    blocks[kind, part, blk, 32 * pos : 32 * pos + 32, :] = jnp.where(
                        group == pos, packed[32 * blk : 32 * blk + 32], 0.0
                    )
    load.wait()
    for slot in range(8):
        blk, row, col = tile_place(tiles_ref, 8 + slot)
        start = 32 * (slot // 4)
        rows = pl.ds(pl.multiple_of(32 * row, 32), 32)
        for kind, part, packed in pieces:
            slab = pltpu.roll(packed[start : start + 32], (col + 4 - slot % 4) % 4 * 32, 1)
            blocks[kind, part, blk, rows, :] = jnp.where(
                group == col, slab, blocks[kind, part, blk, rows, :]
            )

    eye = lax.broadcasted_iota(jnp.int32, (128, 128), 0) == lax.broadcasted_iota(
        jnp.int32, (128, 128), 1
    )
    shift = jnp.concatenate(
        [jnp.where(eye, energy_ref[0], 0.0), jnp.where(eye, BROADEN, 0.0)], axis=1
    )

    def rows_of(ref, *index):
        return jnp.concatenate([ref[*index, 0], ref[*index, 1]], axis=1)

    def system_source(blk):
        less = jnp.concatenate([blocks[0, 0, blk], blocks[0, 1, blk]], axis=1)
        more = jnp.concatenate([blocks[1, 0, blk].T, blocks[1, 1, blk].T], axis=1)
        system = shift - rows_of(h_ref, blk) - 0.5 * (more - less)
        return system, less + rows_of(contact_ref, blk)

    twice = jnp.concatenate([jnp.where(eye, 2.0, 0.0), jnp.zeros((128, 128), jnp.float32)], axis=1)
    link = rows_of(link_ref, 0)
    link_square = square_form(link)
    link_adjoint = split(adjoint(link))

    system_0, source_0 = system_source(0)
    system_1, source_1 = system_source(1)
    x_0 = first_step(system_0, eye)
    x_0_square = square_form(x_0)
    product = times(split(system_0), x_0_square)
    left_x = split(times(link_adjoint, x_0_square))
    x_0 = split(x_0)
    through = square_form(2.0 * link - times(split(product), link_square))
    system_1 = system_1 - times(left_x, through)
    rest = square_form(twice - product)
    left_r = times(left_x, rest)
    gr_0 = times(x_0, rest)
    right_op = split(times(x_0, through))
    x_1 = first_step(system_1, eye)
    product = times(split(system_1), square_form(x_1))
    source_0_square = square_form(source_0)
    left_s = split(times(split(left_r), source_0_square))
    left_r = square_form(left_r)
    source_1 = square_form(source_1 + times(left_s, left_r, 1))
    gr_1 = times(split(x_1), square_form(twice - product))
    gr_0_square = square_form(gr_0)
    left_l = square_form(times(left_s, gr_0_square, 1))
    gl_0 = times(split(times(split(gr_0), source_0_square)), gr_0_square, 1)
    gr_1_square = square_form(gr_1)
    middle = times(right_op, gr_1_square)
    middle_rows = split(middle)
    carried = times(middle_rows, source_1)
    cross = times(middle_rows, left_l)
    gl_1 = times(split(times(split(gr_1), source_1)), gr_1_square, 1)
    inner = times(split(carried), square_form(middle), 1)
    full_r = gr_0 + times(middle_rows, left_r)
    full_l = gl_0 + inner - cross - adjoint(cross)
    for blk, retarded, lesser in ((1, gr_1, gl_1), (0, full_r, full_l)):
        greater = lesser + retarded - adjoint(retarded)
        for part in range(2):
            lesser_ref[blk, part] = lesser[:, 128 * part : 128 * part + 128]
            greater_ref[blk, part] = greater[:, 128 * part : 128 * part + 128]


def in_hbm(array):
    return pltpu.with_memory_space_constraint(array, pltpu.HBM)


def small_device(n_k, n_e, lesser_in, greater_in, h_diag, coupling, contact, coulomb, tiles):
    count = n_k * n_e
    f32 = jnp.float32
    limit = pltpu.CompilerParams(vmem_limit_bytes=32 * 1024 * 1024)
    slots = (2, count, 8, 128)
    blocks = pltpu.VMEM((2, 2, 128, 128), f32)
    plane = pltpu.VMEM((2, 128, 128), f32)
    sigma = pl.pallas_call(
        partial(exchange_kernel, n_k, n_e),
        out_shape=jax.ShapeDtypeStruct(slots, f32),
        in_specs=[HBM] * 4,
        out_specs=VMEM,
        scratch_shapes=[pltpu.SMEM((16,), jnp.int32), blocks, blocks, plane, blocks, plane]
        + [pltpu.VMEM(slots, f32), pltpu.VMEM((2,) + slots, f32)]
        + [pltpu.VMEM(slots, f32)] * 3
        + [pltpu.SemaphoreType.DMA((4,))]
        + [pltpu.SemaphoreType.DMA((2,))] * 4,
        compiler_params=pltpu.CompilerParams(
            collective_id=0, has_side_effects=True, vmem_limit_bytes=32 * 1024 * 1024
        ),
        name="exchange",
    )(*(in_hbm(array) for array in (tiles, lesser_in[0, 0], greater_in[0, 0], coulomb)))
    energy = -SPREAD + 2.0 * SPREAD * (lax.axis_index("ea").astype(f32) + 0.5) / n_e
    lesser, greater = pl.pallas_call(
        sweep_kernel,
        out_shape=(jax.ShapeDtypeStruct((2, 2, 128, 128), f32),) * 2,
        in_specs=[HBM, SMEM, VMEM, VMEM, VMEM, VMEM],
        out_specs=(VMEM, VMEM),
        scratch_shapes=[
            pltpu.VMEM((2, 2, 2, 128, 128), f32),
            pltpu.SMEM((16,), jnp.int32),
            pltpu.SemaphoreType.DMA,
        ],
        compiler_params=limit,
        name="sweep",
    )(
        in_hbm(tiles),
        energy.reshape(1),
        sigma,
        h_diag[0],
        coupling[0],
        contact[0, 0],
    )
    return lesser[None, None], greater[None, None]


def per_device(mesh, lesser_in, *rest):
    n_k, n_e = mesh.shape["ka"], mesh.shape["ea"]
    fits = n_k * n_e == 32 and lesser_in.shape == (1, 1, 2, 2, 128, 128) and rest[-1].shape == (16,)
    if fits:
        return small_device(n_k, n_e, lesser_in, *rest)
    return on_device(lesser_in, *rest)


def solution(mesh):
    in_specs = (
        P("ka", "ea", None, None, None, None),
        P("ka", "ea", None, None, None, None),
        P("ka", None, None, None, None),
        P("ka", None, None, None, None),
        P("ka", "ea", None, None, None, None),
        P(),
        P(),
    )
    out_specs = (P("ka", "ea", None, None, None, None), P("ka", "ea", None, None, None, None))
    return jax.shard_map(
        partial(per_device, mesh), mesh=mesh, in_specs=in_specs, out_specs=out_specs, check_vma=False
    )
```

```python
import math
from functools import partial

import jax
import jax.numpy as jnp
import numpy as np
from jax import lax
from jax.experimental import pallas as pl
from jax.experimental.pallas import tpu as pltpu
from jax.sharding import PartitionSpec as P

BROADEN = 0.3
SPREAD = 0.05
SIGMA_SCALE = 0.01
PRECISE = lax.Precision.HIGHEST


def tiles_of(blocks):
    leading = blocks.shape[:-3]
    lead_rank = len(leading)
    block_count = blocks.shape[-3]
    tile_order = blocks.shape[-1] // 4
    viewed = blocks.reshape(leading + (block_count, 4, tile_order, 4, tile_order))
    viewed = jnp.moveaxis(viewed, lead_rank + 3, lead_rank + 2)
    return viewed.reshape(leading + (block_count * 16, tile_order, tile_order))


def blocks_of(pieces, block_count):
    leading = pieces.shape[:-3]
    lead_rank = len(leading)
    tile_order = pieces.shape[-1]
    viewed = pieces.reshape(leading + (block_count, 4, 4, tile_order, tile_order))
    viewed = jnp.moveaxis(viewed, lead_rank + 2, lead_rank + 3)
    return viewed.reshape(leading + (block_count, 4 * tile_order, 4 * tile_order))


def diag_order(tile_order):
    listing = [row_pos * tile_order + row_pos for row_pos in range(tile_order)]
    for row_pos in range(tile_order):
        for col_pos in range(row_pos + 1, tile_order):
            listing.append(row_pos * tile_order + col_pos)
            listing.append(col_pos * tile_order + row_pos)
    forward = np.array(listing, np.int32)
    return (forward, np.argsort(forward).astype(np.int32))


def arrange(pieces, diag_count):
    leading = pieces.shape[:-3]
    tile_order = pieces.shape[-1]
    forward = diag_order(tile_order)[0]
    diagonal = pieces[..., :diag_count, :, :].reshape(
        leading + (diag_count, tile_order * tile_order)
    )
    diagonal = jnp.take(diagonal, forward, axis=-1).reshape(leading + (-1,))
    paired = pieces[..., diag_count:, :, :].reshape(leading + (-1, 2, tile_order, tile_order))
    paired = jnp.stack([paired[..., 0, :, :], jnp.swapaxes(paired[..., 1, :, :], -1, -2)], axis=-1)
    return jnp.concatenate([diagonal, paired.reshape(leading + (-1,))], axis=-1)


def unarrange(flattened, diag_count, tile_order):
    leading = flattened.shape[:-1]
    square = tile_order * tile_order
    inverse = diag_order(tile_order)[1]
    diagonal = flattened[..., : diag_count * square].reshape(leading + (diag_count, square))
    diagonal = jnp.take(diagonal, inverse, axis=-1).reshape(
        leading + (diag_count, tile_order, tile_order)
    )
    paired = flattened[..., diag_count * square :].reshape(
        leading + (-1, tile_order, tile_order, 2)
    )
    paired = jnp.stack([paired[..., 0], jnp.swapaxes(paired[..., 1], -1, -2)], axis=-3)
    paired = paired.reshape(leading + (-1, tile_order, tile_order))
    return jnp.concatenate([diagonal, paired], axis=-3)


def partner(flattened, diag_count, tile_order):
    size_last = flattened.shape[-1]
    square = tile_order * tile_order
    flipped = flattened.reshape(flattened.shape[:-1] + (size_last // 2, 2))[..., ::-1].reshape(
        flattened.shape
    )
    position = jnp.arange(size_last, dtype=jnp.int32)
    itself = (position < diag_count * square) & (position % square < tile_order)
    return jnp.where(itself, flattened, flipped)


def tables(rows_count, cols_count, length):
    phases = (
        jnp.arange(rows_count, dtype=jnp.int32)[:, None]
        * jnp.arange(cols_count, dtype=jnp.int32)[None, :]
        % length
    )
    angles = phases.astype(jnp.float32) * (2.0 * math.pi / length)
    return (jnp.cos(angles), jnp.sin(angles))


def apply_table(coeffs, values):
    return jnp.einsum("fe,keal->kfal", coeffs, values, precision=PRECISE)


def transform(series, cosine, sine, sign, factor):
    real_in = series[..., 0, :]
    imag_in = series[..., 1, :]
    real_out = apply_table(cosine, real_in) + sign * apply_table(sine, imag_in)
    imag_out = apply_table(cosine, imag_in) - sign * apply_table(sine, real_in)
    return jnp.stack([real_out, imag_out], axis=-2) * factor


def pair_prod(first, second):
    first_re = first[..., 0, :]
    first_im = first[..., 1, :]
    second_re = second[..., 0, :]
    second_im = second[..., 1, :]
    return jnp.stack(
        [first_re * second_re - first_im * second_im, first_re * second_im + first_im * second_re],
        axis=-2,
    )


def pair_mul(first, second):
    products = jnp.einsum("bsij,btjk->bstik", first, second, precision=PRECISE)
    return jnp.stack(
        [products[:, 0, 0] - products[:, 1, 1], products[:, 0, 1] + products[:, 1, 0]], axis=1
    )


def dagger(matrix):
    swapped = jnp.swapaxes(matrix, -1, -2)
    return jnp.stack([swapped[:, 0], -swapped[:, 1]], axis=1)


def newton(system, twice_eye):
    real_d = jnp.diagonal(system[:, 0], axis1=-2, axis2=-1)
    imag_d = jnp.diagonal(system[:, 1], axis1=-2, axis2=-1)
    denominator = real_d * real_d + imag_d * imag_d
    inverse_re = real_d / denominator
    inverse_im = -imag_d / denominator
    scaled_re = system[:, 0] * inverse_re[:, None, :] - system[:, 1] * inverse_im[:, None, :]
    scaled_im = system[:, 0] * inverse_im[:, None, :] + system[:, 1] * inverse_re[:, None, :]
    inner_re = twice_eye[:, 0] - scaled_re
    inner_im = -scaled_im
    approx = jnp.stack(
        [
            inverse_re[:, :, None] * inner_re - inverse_im[:, :, None] * inner_im,
            inverse_re[:, :, None] * inner_im + inverse_im[:, :, None] * inner_re,
        ],
        axis=1,
    )
    approx = pair_mul(approx, twice_eye - pair_mul(system, approx))
    return approx


def polar_terms(direct, mirrored, scale_p):
    reflected = jnp.concatenate([mirrored[:, :1], jnp.flip(mirrored[:, 1:], axis=1)], axis=1)
    correlated = pair_prod(direct, reflected[:, :, ::-1])
    return jnp.stack([correlated[..., 1, :], -correlated[..., 0, :]], axis=-2) * scale_p


def self_energy(direct, screened, out_cos, out_sin, length, scale_p):
    convolved = transform(pair_prod(direct, screened), out_cos, out_sin, -1.0, 1.0 / length)
    return jnp.stack([-convolved[..., 1, :], convolved[..., 0, :]], axis=-2) * (
        SIGMA_SCALE * scale_p
    )


def on_device(lesser_in, greater_in, h_diag, coupling, contact, coulomb, tiles):
    k_local = lesser_in.shape[0]
    e_local = lesser_in.shape[1]
    block_count = lesser_in.shape[2]
    order_n = lesser_in.shape[-1]
    tile_order = order_n // 4
    diag_count = 4 * block_count
    devices_e = lax.axis_size("ea")
    devices_k = lax.axis_size("ka")
    e_total = e_local * devices_e
    length = 2 * e_total
    ret_local = tiles.shape[0] * tile_order * tile_order // devices_e
    offset = lax.axis_index("ea") * ret_local
    k_total = k_local * devices_k
    scale_p = 1.0 / math.sqrt(e_total)

    def layout(blocks):
        return arrange(jnp.take(tiles_of(jnp.moveaxis(blocks, 3, 2)), tiles, axis=-3), diag_count)

    greens = jnp.stack([layout(lesser_in), layout(greater_in)], axis=2)
    fwd_cos, fwd_sin = tables(length, e_total, length)
    full_cos, full_sin = tables(length, length, length)
    out_cos, out_sin = tables(e_total, length, length)
    coulomb_flat = arrange(jnp.take(tiles_of(coulomb), tiles, axis=-3), diag_count)
    outgoing = jnp.concatenate([greens, partner(greens, diag_count, tile_order)], axis=2)
    spectra = transform(
        lax.all_to_all(outgoing, "ea", split_axis=4, concat_axis=1, tiled=True),
        fwd_cos,
        fwd_sin,
        1.0,
        1.0,
    )
    direct = spectra[:, :, :2]
    mirrored = spectra[:, :, 2:]
    turned = polar_terms(direct, mirrored, scale_p)
    weight = lax.dynamic_slice_in_dim(coulomb_flat, offset, ret_local) ** 2
    lags = transform(jnp.sum(turned, axis=0, keepdims=True), full_cos, full_sin, -1.0, 1.0 / length)
    summed = lax.psum(lags, "ka")
    screened = transform(summed * (weight / k_total), full_cos, full_sin, 1.0, 1.0)
    sigma = self_energy(direct, screened, out_cos, out_sin, length, scale_p)
    returned = lax.all_to_all(sigma, "ea", split_axis=1, concat_axis=4, tiled=True)
    pieces = unarrange(returned, diag_count, tile_order)
    empty = jnp.zeros(pieces.shape[:-3] + (block_count * 16, tile_order, tile_order), jnp.float32)
    sigma_blocks = blocks_of(empty.at[..., tiles, :, :].set(pieces), block_count)
    sigma_ret = 0.5 * (sigma_blocks[:, :, 1] - sigma_blocks[:, :, 0])
    sigma_less = sigma_blocks[:, :, 0]
    batch = k_local * e_local
    identity = jnp.eye(order_n, dtype=jnp.float32)
    energy_idx = lax.axis_index("ea") * e_local + jnp.arange(e_local, dtype=jnp.int32)
    energies = -SPREAD + 2.0 * SPREAD * (energy_idx.astype(jnp.float32) + 0.5) / e_total
    energies = energies[None, :].reshape(batch)
    shifted = jnp.stack(
        [
            energies[:, None, None] * identity,
            jnp.broadcast_to(BROADEN * identity, (batch, order_n, order_n)),
        ],
        axis=1,
    )
    twice_eye = jnp.broadcast_to(
        jnp.stack([2.0 * identity, 0.0 * identity]), (batch, 2, order_n, order_n)
    )

    def per_energy(array_k):
        return array_k[:, None].reshape((batch,) + array_k.shape[1:])

    forward_r = []
    forward_l = []
    for blk_no in range(block_count):
        system = (
            shifted
            - per_energy(h_diag[:, blk_no])
            - sigma_ret[:, :, :, blk_no].reshape(batch, 2, order_n, order_n)
        )
        source = sigma_less[:, :, :, blk_no].reshape(batch, 2, order_n, order_n)
        if blk_no == 0:
            source = source + contact[:, :, 0].reshape(batch, 2, order_n, order_n)
        if blk_no == block_count - 1:
            source = source + contact[:, :, 1].reshape(batch, 2, order_n, order_n)
        if blk_no > 0:
            link = per_energy(coupling[:, blk_no - 1])
            system = system - pair_mul(dagger(link), pair_mul(forward_r[-1], link))
            source = source + pair_mul(dagger(link), pair_mul(forward_l[-1], link))
        green_r = newton(system, twice_eye)
        forward_r.append(green_r)
        forward_l.append(pair_mul(pair_mul(green_r, source), dagger(green_r)))
    retarded_list = [forward_r[-1]]
    lesser_list = [forward_l[-1]]
    blk_no = 0
    green_r = forward_r[blk_no]
    green_l = forward_l[blk_no]
    link = per_energy(coupling[:, blk_no])
    right_op = pair_mul(green_r, link)
    middle = pair_mul(right_op, retarded_list[0])
    new_r = green_r + pair_mul(middle, pair_mul(dagger(link), green_r))
    cross = pair_mul(middle, pair_mul(dagger(link), green_l))
    new_l = (
        green_l
        + pair_mul(pair_mul(right_op, lesser_list[0]), dagger(right_op))
        - cross
        - dagger(cross)
    )
    retarded_list.insert(0, new_r)
    lesser_list.insert(0, new_l)
    lesser = jnp.stack(lesser_list, axis=1)
    greater = jnp.stack(
        [
            lesser_list[blk_no] + retarded_list[blk_no] - dagger(retarded_list[blk_no])
            for blk_no in range(block_count)
        ],
        axis=1,
    )
    out_shape = (k_local, e_local, block_count, 2, order_n, order_n)
    return (lesser.reshape(out_shape), greater.reshape(out_shape))


MESH = pl.DeviceIdType.MESH
VMEM = pl.BlockSpec(memory_space=pltpu.VMEM)
SMEM = pl.BlockSpec(memory_space=pltpu.SMEM)
HBM = pl.BlockSpec(memory_space=pltpu.HBM)


def rolled(rows, shift):
    return pltpu.roll(rows, shift, rows.ndim - 2)


def sublane(shape):
    return lax.broadcasted_iota(jnp.int32, shape, len(shape) - 2) % 8


def crossed_rows(four):
    row = sublane(four[0].shape)
    top, first = row < 4, row % 4 < 2
    a, b, c, d = four
    out = []
    for left, right in (
        (jnp.where(top, a, rolled(c, 4)), jnp.where(top, b, rolled(d, 4))),
        (jnp.where(top, rolled(a, 4), c), jnp.where(top, rolled(b, 4), d)),
    ):
        out.append(jnp.where(first, left, rolled(right, 2)))
        out.append(jnp.where(first, rolled(left, 6), right))
    return out


def tile_place(tiles_ref, slot):
    tile = tiles_ref[slot]
    return tile // 16, tile % 16 // 4, tile % 4


def pack_tiles(tiles_ref, load):
    group = lax.broadcasted_iota(jnp.int32, (32, 128), 1) // 32
    slabs = [[load(blk, 32 * pos) for pos in range(4)] for blk in range(2)]
    parts = []
    for blk in range(2):
        part = slabs[blk][0]
        for pos in range(1, 4):
            part = jnp.where(group == pos, slabs[blk][pos], part)
        parts.append(part)
    for half in range(2):
        part = None
        for pos in range(4):
            blk, row, col = tile_place(tiles_ref, 8 + 4 * half + pos)
            slab = slabs[0][0]
            for index in range(1, 8):
                found = blk * 4 + row == index
                slab = jnp.where(found, slabs[index // 4][index % 4], slab)
            turn = (pos + 4 - col) % 4
            slab = jnp.where(turn % 2 == 1, pltpu.roll(slab, 32, 1), slab)
            slab = jnp.where(turn >= 2, pltpu.roll(slab, 64, 1), slab)
            part = slab if part is None else jnp.where(group == pos, slab, part)
        parts.append(part)
    return jnp.concatenate(parts, axis=0).reshape(16, 8, 128)


def exchange_kernel(
    n_k,
    n_e,
    tiles_hbm,
    l_hbm,
    g_hbm,
    c_hbm,
    out_ref,
    tiles_ref,
    l_ref,
    g_ref,
    c_ref,
    gt_ref,
    ct_ref,
    packed,
    weight_ref,
    held,
    sigma,
    back,
    load_sem,
    send_a,
    recv_a,
    send_b,
    recv_b,
):
    count = n_k * n_e
    half = n_e // 2
    my_k = lax.axis_index("ka")
    my_e = lax.axis_index("ea")
    me = my_k * n_e + my_e
    side = my_e // half

    loads = [
        pltpu.make_async_copy(source, target, load_sem.at[index])
        for index, (source, target) in enumerate(
            ((tiles_hbm, tiles_ref), (g_hbm, g_ref), (l_hbm, l_ref), (c_hbm, c_ref))
        )
    ]
    for load in loads:
        load.start()

    k_list = [(my_k + step) % n_k for step in range(n_k)]
    near = [side * half + (my_e + step) % half for step in range(half)]
    far = [(1 - side) * half + (my_e + step) % half for step in range(half)]
    others = [(k, e) for k in k_list for e in far]
    others += [(k, e) for k in k_list for e in near][1:]

    def remote(source, target, send_sem, recv_sem, k, e):
        return pltpu.make_async_remote_copy(
            src_ref=source,
            dst_ref=target,
            send_sem=send_sem,
            recv_sem=recv_sem,
            device_id={"ka": k, "ea": e},
            device_id_type=MESH,
        )

    def all_of(ref, send_sem, recv_sem):
        every = ref.at[pl.ds(0, count - 1)]
        return remote(every, every, send_sem, recv_sem, *others[0])

    barrier = pltpu.get_barrier_semaphore()
    for k, e in others:
        pl.semaphore_signal(barrier, inc=1, device_id={"ka": k, "ea": e}, device_id_type=MESH)

    def spread(ref, pieces):
        for index, piece in enumerate(crossed_rows(pieces)):
            start = index % 2 * 16
            ref[index // 2, start : start + 16] = piece

    def pack(ref):
        return [
            pack_tiles(tiles_ref, lambda blk, row: ref[blk, part, pl.ds(row, 32), :])
            for part in range(2)
        ]

    loads[0].wait()
    loads[1].wait()
    for blk in range(2):
        for part in range(2):
            gt_ref[blk, part] = g_ref[blk, part].T
    greater_rows = pack(gt_ref)
    loads[2].wait()
    spread(packed, pack(l_ref) + greater_rows)
    pl.semaphore_wait(barrier, count - 1)
    for chunk in range(2):
        for k, e in others:
            source = packed.at[chunk, k * n_e + e]
            target = held.at[chunk, me]
            remote(source, target, send_a.at[chunk], recv_a.at[chunk], k, e).start()

    held[0, me] = packed[0, me]
    held[1, me] = packed[1, me]
    loads[3].wait()
    for blk in range(2):
        ct_ref[blk] = c_ref[blk].T
    for kind, ref in ((0, c_ref), (1, ct_ref)):
        bare = pack_tiles(tiles_ref, lambda blk, row: ref[blk, pl.ds(row, 32), :])
        spread(weight_ref.at[kind], [bare * bare * (SIGMA_SCALE / (n_e * n_k))] * 4)

    lags = 2 * n_e - 1
    row = sublane((8, 128))
    top, first_pair = row < 4, row % 4 < 2
    sign = jnp.where(first_pair, 1.0, -1.0)

    def swap(rows):
        return jnp.where(first_pair, rolled(rows, 6), rolled(rows, 2))

    def greens(chunk, pair):
        both = []
        for e in range(n_e):
            one = held[chunk, 2 * pair * n_e + e]
            two = held[chunk, (2 * pair + 1) * n_e + e]
            lesser = jnp.where(top, one, rolled(two, 4))
            both.append((lesser, jnp.where(top, rolled(one, 4), two)))
        return [piece[0] for piece in both], [piece[1] for piece in both]

    def work(chunk, carry):
        all_of(held.at[chunk], send_a.at[chunk], recv_a.at[chunk]).wait_recv()

        def correlate(pair, sums):
            plain, crossed = list(sums[0]), list(sums[1])
            lesser, greater = greens(chunk, pair)
            for e_two in range(n_e):
                swapped = swap(greater[e_two])
                for e_one in range(n_e):
                    lag = e_one - e_two + n_e - 1
                    plain[lag] = plain[lag] + lesser[e_one] * greater[e_two]
                    crossed[lag] = crossed[lag] + lesser[e_one] * swapped
            return tuple(plain), tuple(crossed)

        zero = jnp.zeros((8, 128), jnp.float32)
        plain, crossed = lax.fori_loop(
            0, n_k // 2, correlate, ((zero,) * lags, (zero,) * lags)
        )
        plain = [total + rolled(total, 4) for total in plain]
        crossed = [total + rolled(total, 4) for total in crossed]
        real = [sign * (total - rolled(total, 2)) for total in plain]
        imag = [-sign * (total + rolled(total, 2)) for total in crossed]
        weights = weight_ref[0, chunk, me], weight_ref[1, chunk, me]

        def convolve(turn, inner):
            pair = (my_k // 2 + turn) % (n_k // 2)
            results = []
            for kind, green in enumerate(greens(chunk, pair)):
                swapped = [swap(piece) for piece in green]
                for e_out in range(n_e):
                    total = None
                    for e_in in range(n_e):
                        lag = e_out - e_in if kind == 0 else e_in - e_out
                        lag = lag + n_e - 1
                        term = green[e_in] * real[lag] + swapped[e_in] * imag[lag]
                        total = term if total is None else total + term
                    results.append(total * weights[kind])
            for e in range(n_e):
                less, more = results[e], results[n_e + e]
                sigma[chunk, 2 * pair * n_e + e] = jnp.where(top, less, rolled(more, 4))
                sigma[chunk, (2 * pair + 1) * n_e + e] = jnp.where(top, rolled(less, 4), more)

            def send(k, e):
                source = sigma.at[chunk, k * n_e + e]
                target = back.at[chunk, me]
                remote(source, target, send_b.at[chunk], recv_b.at[chunk], k, e).start()

            for e in far + near[1:]:
                for k in (2 * pair, 2 * pair + 1):
                    send(k, e)
            for k in (2 * pair, 2 * pair + 1):

                @pl.when(k != my_k)
                def _():
                    send(k, my_e)

            return inner

        lax.fori_loop(0, n_k // 2, convolve, 0)
        back[chunk, me] = sigma[chunk, me]
        return carry

    lax.fori_loop(0, 2, work, 0)
    for chunk in range(2):
        all_of(held.at[chunk], send_a.at[chunk], recv_a.at[chunk]).wait_send()
        all_of(back.at[chunk], send_b.at[chunk], recv_b.at[chunk]).wait_send()
        all_of(back.at[chunk], send_b.at[chunk], recv_b.at[chunk]).wait_recv()
    out_ref[...] = back[...]


def split(value):
    high = value.astype(jnp.bfloat16)
    return high, (value - high.astype(jnp.float32)).astype(jnp.bfloat16)


def square_form(rows):
    real, imag = rows[:, :128], rows[:, 128:]
    return split(jnp.concatenate([rows, jnp.concatenate([-imag, real], axis=1)], axis=0))


def times(first, second, contract=0):
    dims = (((1,), (contract,)), ((), ()))

    def dot(left, right):
        return lax.dot_general(left, right, dims, preferred_element_type=jnp.float32)

    high, low = first
    both = dot(jnp.concatenate([high, low], axis=0), second[0])
    return both[:128] + (dot(high, second[1]) + both[128:])


def adjoint(rows):
    return jnp.concatenate([rows[:, :128].T, -rows[:, 128:].T], axis=1)


def scaled(rows, factor):
    real, imag = rows[:, :128], rows[:, 128:]
    return jnp.concatenate(
        [real * factor[0] - imag * factor[1], real * factor[1] + imag * factor[0]], axis=1
    )


def diagonal_inverse(system, eye):
    only_re = jnp.where(eye, system[:, :128], 0.0)
    only_im = jnp.where(eye, system[:, 128:], 0.0)
    pair = []
    for axis in range(2):
        real_d = jnp.sum(only_re, axis=axis, keepdims=True)
        imag_d = jnp.sum(only_im, axis=axis, keepdims=True)
        denominator = real_d * real_d + imag_d * imag_d
        pair.append((real_d / denominator, -imag_d / denominator))
    return pair


def sweep_kernel(
    tiles_hbm,
    energy_ref,
    sigma_ref,
    h_ref,
    link_ref,
    contact_ref,
    lesser_ref,
    greater_ref,
    blocks,
    tiles_ref,
    load_sem,
):
    load = pltpu.make_async_copy(tiles_hbm, tiles_ref, load_sem)
    load.start()
    group = lax.broadcasted_iota(jnp.int32, (32, 128), 1) // 32
    pieces = []
    parts = crossed_rows(
        [sigma_ref[index // 2, index % 2 * 16 : index % 2 * 16 + 16] for index in range(4)]
    )
    for kind in range(2):
        for part in range(2):
            packed = parts[2 * kind + part].reshape(128, 128)
            pieces.append((kind, part, packed[64:]))
            for blk in range(2):
                for pos in range(4):
                    blocks[kind, part, blk, 32 * pos : 32 * pos + 32, :] = jnp.where(
                        group == pos, packed[32 * blk : 32 * blk + 32], 0.0
                    )
    load.wait()
    for slot in range(8):
        blk, row, col = tile_place(tiles_ref, 8 + slot)
        start = 32 * (slot // 4)
        rows = pl.ds(pl.multiple_of(32 * row, 32), 32)
        for kind, part, packed in pieces:
            slab = pltpu.roll(packed[start : start + 32], (col + 4 - slot % 4) % 4 * 32, 1)
            blocks[kind, part, blk, rows, :] = jnp.where(
                group == col, slab, blocks[kind, part, blk, rows, :]
            )

    eye = lax.broadcasted_iota(jnp.int32, (128, 128), 0) == lax.broadcasted_iota(
        jnp.int32, (128, 128), 1
    )
    shift = jnp.concatenate(
        [jnp.where(eye, energy_ref[0], 0.0), jnp.where(eye, BROADEN, 0.0)], axis=1
    )

    def rows_of(ref, *index):
        return jnp.concatenate([ref[*index, 0], ref[*index, 1]], axis=1)

    def system_source(blk):
        less = jnp.concatenate([blocks[0, 0, blk], blocks[0, 1, blk]], axis=1)
        more = jnp.concatenate([blocks[1, 0, blk].T, blocks[1, 1, blk].T], axis=1)
        system = shift - rows_of(h_ref, blk) - 0.5 * (more - less)
        return system, less + rows_of(contact_ref, blk)

    twice = jnp.concatenate([jnp.where(eye, 2.0, 0.0), jnp.zeros((128, 128), jnp.float32)], axis=1)
    link = rows_of(link_ref, 0)
    link_square = square_form(link)

    system_0, source_0 = system_source(0)
    system_1, source_1 = system_source(1)
    system_0_square = square_form(system_0)
    row_0, col_0 = diagonal_inverse(system_0, eye)
    x_0 = scaled(twice - scaled(system_0, row_0), col_0)
    link_d = scaled(adjoint(link), row_0)
    left_u = 2.0 * link_d - scaled(times(split(link_d), system_0_square), row_0)
    left_rows = split(left_u)
    left_m = split(times(left_rows, system_0_square))
    x_0_rows, x_0_square = split(x_0), square_form(x_0)
    x_link = square_form(times(x_0_rows, link_square))
    system_1 = system_1 - (2.0 * times(left_rows, link_square) - times(left_m, x_link))
    system_1_square = square_form(system_1)
    row_1, col_1 = diagonal_inverse(system_1, eye)
    x_1 = scaled(twice - scaled(system_1, row_1), col_1)
    rest = split(twice - times(x_0_rows, system_0_square))
    right_op = split(times(rest, x_link))
    x_1_rows, x_1_square = split(x_1), square_form(x_1)
    right_x = times(right_op, x_1_square)
    right_m = times(split(right_x), system_1_square)
    product = times(x_1_rows, system_1_square)
    gr_0 = times(rest, x_0_square)
    left_r = 2.0 * left_u - times(left_m, x_0_square)
    source_0_square = square_form(source_0)
    left_s = split(times(split(left_r), source_0_square))
    left_r = square_form(left_r)
    source_1 = square_form(source_1 + times(left_s, left_r, 1))
    middle = 2.0 * right_x - times(split(right_m), x_1_square)
    gr_1 = times(split(twice - product), x_1_square)
    gr_0_square = square_form(gr_0)
    left_l = square_form(times(left_s, gr_0_square, 1))
    gl_0 = times(split(times(split(gr_0), source_0_square)), gr_0_square, 1)
    gr_1_square = square_form(gr_1)
    middle_rows = split(middle)
    carried = times(middle_rows, source_1)
    cross = times(middle_rows, left_l)
    gl_1 = times(split(times(split(gr_1), source_1)), gr_1_square, 1)
    inner = times(split(carried), square_form(middle), 1)
    full_r = gr_0 + times(middle_rows, left_r)
    full_l = gl_0 + inner - cross - adjoint(cross)
    for blk, retarded, lesser in ((1, gr_1, gl_1), (0, full_r, full_l)):
        greater = lesser + retarded - adjoint(retarded)
        for part in range(2):
            lesser_ref[blk, part] = lesser[:, 128 * part : 128 * part + 128]
            greater_ref[blk, part] = greater[:, 128 * part : 128 * part + 128]


def in_hbm(array):
    return pltpu.with_memory_space_constraint(array, pltpu.HBM)


def small_device(n_k, n_e, lesser_in, greater_in, h_diag, coupling, contact, coulomb, tiles):
    count = n_k * n_e
    f32 = jnp.float32
    limit = pltpu.CompilerParams(vmem_limit_bytes=32 * 1024 * 1024)
    slots = (2, count, 8, 128)
    blocks = pltpu.VMEM((2, 2, 128, 128), f32)
    plane = pltpu.VMEM((2, 128, 128), f32)
    sigma = pl.pallas_call(
        partial(exchange_kernel, n_k, n_e),
        out_shape=jax.ShapeDtypeStruct(slots, f32),
        in_specs=[HBM] * 4,
        out_specs=VMEM,
        scratch_shapes=[pltpu.SMEM((16,), jnp.int32), blocks, blocks, plane, blocks, plane]
        + [pltpu.VMEM(slots, f32), pltpu.VMEM((2,) + slots, f32)]
        + [pltpu.VMEM(slots, f32)] * 3
        + [pltpu.SemaphoreType.DMA((4,))]
        + [pltpu.SemaphoreType.DMA((2,))] * 4,
        compiler_params=pltpu.CompilerParams(
            collective_id=0, has_side_effects=True, vmem_limit_bytes=32 * 1024 * 1024
        ),
        name="exchange",
    )(*(in_hbm(array) for array in (tiles, lesser_in[0, 0], greater_in[0, 0], coulomb)))
    energy = -SPREAD + 2.0 * SPREAD * (lax.axis_index("ea").astype(f32) + 0.5) / n_e
    lesser, greater = pl.pallas_call(
        sweep_kernel,
        out_shape=(jax.ShapeDtypeStruct((2, 2, 128, 128), f32),) * 2,
        in_specs=[HBM, SMEM, VMEM, VMEM, VMEM, VMEM],
        out_specs=(VMEM, VMEM),
        scratch_shapes=[
            pltpu.VMEM((2, 2, 2, 128, 128), f32),
            pltpu.SMEM((16,), jnp.int32),
            pltpu.SemaphoreType.DMA,
        ],
        compiler_params=limit,
        name="sweep",
    )(
        in_hbm(tiles),
        energy.reshape(1),
        sigma,
        h_diag[0],
        coupling[0],
        contact[0, 0],
    )
    return lesser[None, None], greater[None, None]


def per_device(mesh, lesser_in, *rest):
    n_k, n_e = mesh.shape["ka"], mesh.shape["ea"]
    fits = n_k * n_e == 32 and lesser_in.shape == (1, 1, 2, 2, 128, 128) and rest[-1].shape == (16,)
    if fits:
        return small_device(n_k, n_e, lesser_in, *rest)
    return on_device(lesser_in, *rest)


def solution(mesh):
    in_specs = (
        P("ka", "ea", None, None, None, None),
        P("ka", "ea", None, None, None, None),
        P("ka", None, None, None, None),
        P("ka", None, None, None, None),
        P("ka", "ea", None, None, None, None),
        P(),
        P(),
    )
    out_specs = (P("ka", "ea", None, None, None, None), P("ka", "ea", None, None, None, None))
    return jax.shard_map(
        partial(per_device, mesh), mesh=mesh, in_specs=in_specs, out_specs=out_specs, check_vma=False
    )
```

```python
import math
from functools import partial

import jax
import jax.numpy as jnp
import numpy as np
from jax import lax
from jax.experimental import pallas as pl
from jax.experimental.pallas import tpu as pltpu
from jax.sharding import PartitionSpec as P

BROADEN = 0.3
SPREAD = 0.05
SIGMA_SCALE = 0.01
PRECISE = lax.Precision.HIGHEST


def tiles_of(blocks):
    leading = blocks.shape[:-3]
    lead_rank = len(leading)
    block_count = blocks.shape[-3]
    tile_order = blocks.shape[-1] // 4
    viewed = blocks.reshape(leading + (block_count, 4, tile_order, 4, tile_order))
    viewed = jnp.moveaxis(viewed, lead_rank + 3, lead_rank + 2)
    return viewed.reshape(leading + (block_count * 16, tile_order, tile_order))


def blocks_of(pieces, block_count):
    leading = pieces.shape[:-3]
    lead_rank = len(leading)
    tile_order = pieces.shape[-1]
    viewed = pieces.reshape(leading + (block_count, 4, 4, tile_order, tile_order))
    viewed = jnp.moveaxis(viewed, lead_rank + 2, lead_rank + 3)
    return viewed.reshape(leading + (block_count, 4 * tile_order, 4 * tile_order))


def diag_order(tile_order):
    listing = [row_pos * tile_order + row_pos for row_pos in range(tile_order)]
    for row_pos in range(tile_order):
        for col_pos in range(row_pos + 1, tile_order):
            listing.append(row_pos * tile_order + col_pos)
            listing.append(col_pos * tile_order + row_pos)
    forward = np.array(listing, np.int32)
    return (forward, np.argsort(forward).astype(np.int32))


def arrange(pieces, diag_count):
    leading = pieces.shape[:-3]
    tile_order = pieces.shape[-1]
    forward = diag_order(tile_order)[0]
    diagonal = pieces[..., :diag_count, :, :].reshape(
        leading + (diag_count, tile_order * tile_order)
    )
    diagonal = jnp.take(diagonal, forward, axis=-1).reshape(leading + (-1,))
    paired = pieces[..., diag_count:, :, :].reshape(leading + (-1, 2, tile_order, tile_order))
    paired = jnp.stack([paired[..., 0, :, :], jnp.swapaxes(paired[..., 1, :, :], -1, -2)], axis=-1)
    return jnp.concatenate([diagonal, paired.reshape(leading + (-1,))], axis=-1)


def unarrange(flattened, diag_count, tile_order):
    leading = flattened.shape[:-1]
    square = tile_order * tile_order
    inverse = diag_order(tile_order)[1]
    diagonal = flattened[..., : diag_count * square].reshape(leading + (diag_count, square))
    diagonal = jnp.take(diagonal, inverse, axis=-1).reshape(
        leading + (diag_count, tile_order, tile_order)
    )
    paired = flattened[..., diag_count * square :].reshape(
        leading + (-1, tile_order, tile_order, 2)
    )
    paired = jnp.stack([paired[..., 0], jnp.swapaxes(paired[..., 1], -1, -2)], axis=-3)
    paired = paired.reshape(leading + (-1, tile_order, tile_order))
    return jnp.concatenate([diagonal, paired], axis=-3)


def partner(flattened, diag_count, tile_order):
    size_last = flattened.shape[-1]
    square = tile_order * tile_order
    flipped = flattened.reshape(flattened.shape[:-1] + (size_last // 2, 2))[..., ::-1].reshape(
        flattened.shape
    )
    position = jnp.arange(size_last, dtype=jnp.int32)
    itself = (position < diag_count * square) & (position % square < tile_order)
    return jnp.where(itself, flattened, flipped)


def tables(rows_count, cols_count, length):
    phases = (
        jnp.arange(rows_count, dtype=jnp.int32)[:, None]
        * jnp.arange(cols_count, dtype=jnp.int32)[None, :]
        % length
    )
    angles = phases.astype(jnp.float32) * (2.0 * math.pi / length)
    return (jnp.cos(angles), jnp.sin(angles))


def apply_table(coeffs, values):
    return jnp.einsum("fe,keal->kfal", coeffs, values, precision=PRECISE)


def transform(series, cosine, sine, sign, factor):
    real_in = series[..., 0, :]
    imag_in = series[..., 1, :]
    real_out = apply_table(cosine, real_in) + sign * apply_table(sine, imag_in)
    imag_out = apply_table(cosine, imag_in) - sign * apply_table(sine, real_in)
    return jnp.stack([real_out, imag_out], axis=-2) * factor


def pair_prod(first, second):
    first_re = first[..., 0, :]
    first_im = first[..., 1, :]
    second_re = second[..., 0, :]
    second_im = second[..., 1, :]
    return jnp.stack(
        [first_re * second_re - first_im * second_im, first_re * second_im + first_im * second_re],
        axis=-2,
    )


def pair_mul(first, second):
    products = jnp.einsum("bsij,btjk->bstik", first, second, precision=PRECISE)
    return jnp.stack(
        [products[:, 0, 0] - products[:, 1, 1], products[:, 0, 1] + products[:, 1, 0]], axis=1
    )


def dagger(matrix):
    swapped = jnp.swapaxes(matrix, -1, -2)
    return jnp.stack([swapped[:, 0], -swapped[:, 1]], axis=1)


def newton(system, twice_eye):
    real_d = jnp.diagonal(system[:, 0], axis1=-2, axis2=-1)
    imag_d = jnp.diagonal(system[:, 1], axis1=-2, axis2=-1)
    denominator = real_d * real_d + imag_d * imag_d
    inverse_re = real_d / denominator
    inverse_im = -imag_d / denominator
    scaled_re = system[:, 0] * inverse_re[:, None, :] - system[:, 1] * inverse_im[:, None, :]
    scaled_im = system[:, 0] * inverse_im[:, None, :] + system[:, 1] * inverse_re[:, None, :]
    inner_re = twice_eye[:, 0] - scaled_re
    inner_im = -scaled_im
    approx = jnp.stack(
        [
            inverse_re[:, :, None] * inner_re - inverse_im[:, :, None] * inner_im,
            inverse_re[:, :, None] * inner_im + inverse_im[:, :, None] * inner_re,
        ],
        axis=1,
    )
    approx = pair_mul(approx, twice_eye - pair_mul(system, approx))
    return approx


def polar_terms(direct, mirrored, scale_p):
    reflected = jnp.concatenate([mirrored[:, :1], jnp.flip(mirrored[:, 1:], axis=1)], axis=1)
    correlated = pair_prod(direct, reflected[:, :, ::-1])
    return jnp.stack([correlated[..., 1, :], -correlated[..., 0, :]], axis=-2) * scale_p


def self_energy(direct, screened, out_cos, out_sin, length, scale_p):
    convolved = transform(pair_prod(direct, screened), out_cos, out_sin, -1.0, 1.0 / length)
    return jnp.stack([-convolved[..., 1, :], convolved[..., 0, :]], axis=-2) * (
        SIGMA_SCALE * scale_p
    )


def on_device(lesser_in, greater_in, h_diag, coupling, contact, coulomb, tiles):
    k_local = lesser_in.shape[0]
    e_local = lesser_in.shape[1]
    block_count = lesser_in.shape[2]
    order_n = lesser_in.shape[-1]
    tile_order = order_n // 4
    diag_count = 4 * block_count
    devices_e = lax.axis_size("ea")
    devices_k = lax.axis_size("ka")
    e_total = e_local * devices_e
    length = 2 * e_total
    ret_local = tiles.shape[0] * tile_order * tile_order // devices_e
    offset = lax.axis_index("ea") * ret_local
    k_total = k_local * devices_k
    scale_p = 1.0 / math.sqrt(e_total)

    def layout(blocks):
        return arrange(jnp.take(tiles_of(jnp.moveaxis(blocks, 3, 2)), tiles, axis=-3), diag_count)

    greens = jnp.stack([layout(lesser_in), layout(greater_in)], axis=2)
    fwd_cos, fwd_sin = tables(length, e_total, length)
    full_cos, full_sin = tables(length, length, length)
    out_cos, out_sin = tables(e_total, length, length)
    coulomb_flat = arrange(jnp.take(tiles_of(coulomb), tiles, axis=-3), diag_count)
    outgoing = jnp.concatenate([greens, partner(greens, diag_count, tile_order)], axis=2)
    spectra = transform(
        lax.all_to_all(outgoing, "ea", split_axis=4, concat_axis=1, tiled=True),
        fwd_cos,
        fwd_sin,
        1.0,
        1.0,
    )
    direct = spectra[:, :, :2]
    mirrored = spectra[:, :, 2:]
    turned = polar_terms(direct, mirrored, scale_p)
    weight = lax.dynamic_slice_in_dim(coulomb_flat, offset, ret_local) ** 2
    lags = transform(jnp.sum(turned, axis=0, keepdims=True), full_cos, full_sin, -1.0, 1.0 / length)
    summed = lax.psum(lags, "ka")
    screened = transform(summed * (weight / k_total), full_cos, full_sin, 1.0, 1.0)
    sigma = self_energy(direct, screened, out_cos, out_sin, length, scale_p)
    returned = lax.all_to_all(sigma, "ea", split_axis=1, concat_axis=4, tiled=True)
    pieces = unarrange(returned, diag_count, tile_order)
    empty = jnp.zeros(pieces.shape[:-3] + (block_count * 16, tile_order, tile_order), jnp.float32)
    sigma_blocks = blocks_of(empty.at[..., tiles, :, :].set(pieces), block_count)
    sigma_ret = 0.5 * (sigma_blocks[:, :, 1] - sigma_blocks[:, :, 0])
    sigma_less = sigma_blocks[:, :, 0]
    batch = k_local * e_local
    identity = jnp.eye(order_n, dtype=jnp.float32)
    energy_idx = lax.axis_index("ea") * e_local + jnp.arange(e_local, dtype=jnp.int32)
    energies = -SPREAD + 2.0 * SPREAD * (energy_idx.astype(jnp.float32) + 0.5) / e_total
    energies = energies[None, :].reshape(batch)
    shifted = jnp.stack(
        [
            energies[:, None, None] * identity,
            jnp.broadcast_to(BROADEN * identity, (batch, order_n, order_n)),
        ],
        axis=1,
    )
    twice_eye = jnp.broadcast_to(
        jnp.stack([2.0 * identity, 0.0 * identity]), (batch, 2, order_n, order_n)
    )

    def per_energy(array_k):
        return array_k[:, None].reshape((batch,) + array_k.shape[1:])

    forward_r = []
    forward_l = []
    for blk_no in range(block_count):
        system = (
            shifted
            - per_energy(h_diag[:, blk_no])
            - sigma_ret[:, :, :, blk_no].reshape(batch, 2, order_n, order_n)
        )
        source = sigma_less[:, :, :, blk_no].reshape(batch, 2, order_n, order_n)
        if blk_no == 0:
            source = source + contact[:, :, 0].reshape(batch, 2, order_n, order_n)
        if blk_no == block_count - 1:
            source = source + contact[:, :, 1].reshape(batch, 2, order_n, order_n)
        if blk_no > 0:
            link = per_energy(coupling[:, blk_no - 1])
            system = system - pair_mul(dagger(link), pair_mul(forward_r[-1], link))
            source = source + pair_mul(dagger(link), pair_mul(forward_l[-1], link))
        green_r = newton(system, twice_eye)
        forward_r.append(green_r)
        forward_l.append(pair_mul(pair_mul(green_r, source), dagger(green_r)))
    retarded_list = [forward_r[-1]]
    lesser_list = [forward_l[-1]]
    blk_no = 0
    green_r = forward_r[blk_no]
    green_l = forward_l[blk_no]
    link = per_energy(coupling[:, blk_no])
    right_op = pair_mul(green_r, link)
    middle = pair_mul(right_op, retarded_list[0])
    new_r = green_r + pair_mul(middle, pair_mul(dagger(link), green_r))
    cross = pair_mul(middle, pair_mul(dagger(link), green_l))
    new_l = (
        green_l
        + pair_mul(pair_mul(right_op, lesser_list[0]), dagger(right_op))
        - cross
        - dagger(cross)
    )
    retarded_list.insert(0, new_r)
    lesser_list.insert(0, new_l)
    lesser = jnp.stack(lesser_list, axis=1)
    greater = jnp.stack(
        [
            lesser_list[blk_no] + retarded_list[blk_no] - dagger(retarded_list[blk_no])
            for blk_no in range(block_count)
        ],
        axis=1,
    )
    out_shape = (k_local, e_local, block_count, 2, order_n, order_n)
    return (lesser.reshape(out_shape), greater.reshape(out_shape))


MESH = pl.DeviceIdType.MESH
VMEM = pl.BlockSpec(memory_space=pltpu.VMEM)
SMEM = pl.BlockSpec(memory_space=pltpu.SMEM)
HBM = pl.BlockSpec(memory_space=pltpu.HBM)


def rolled(rows, shift):
    return pltpu.roll(rows, shift, rows.ndim - 2)


def sublane(shape):
    return lax.broadcasted_iota(jnp.int32, shape, len(shape) - 2) % 8


def crossed_rows(four):
    row = sublane(four[0].shape)
    top, first = row < 4, row % 4 < 2
    a, b, c, d = four
    out = []
    for left, right in (
        (jnp.where(top, a, rolled(c, 4)), jnp.where(top, b, rolled(d, 4))),
        (jnp.where(top, rolled(a, 4), c), jnp.where(top, rolled(b, 4), d)),
    ):
        out.append(jnp.where(first, left, rolled(right, 2)))
        out.append(jnp.where(first, rolled(left, 6), right))
    return out


def tile_place(tiles_ref, slot):
    tile = tiles_ref[slot]
    return tile // 16, tile % 16 // 4, tile % 4


def pack_tiles(tiles_ref, load):
    group = lax.broadcasted_iota(jnp.int32, (32, 128), 1) // 32
    slabs = [[load(blk, 32 * pos) for pos in range(4)] for blk in range(2)]
    parts = []
    for blk in range(2):
        part = slabs[blk][0]
        for pos in range(1, 4):
            part = jnp.where(group == pos, slabs[blk][pos], part)
        parts.append(part)
    for half in range(2):
        part = None
        for pos in range(4):
            blk, row, col = tile_place(tiles_ref, 8 + 4 * half + pos)
            slab = slabs[0][0]
            for index in range(1, 8):
                found = blk * 4 + row == index
                slab = jnp.where(found, slabs[index // 4][index % 4], slab)
            turn = (pos + 4 - col) % 4
            slab = jnp.where(turn % 2 == 1, pltpu.roll(slab, 32, 1), slab)
            slab = jnp.where(turn >= 2, pltpu.roll(slab, 64, 1), slab)
            part = slab if part is None else jnp.where(group == pos, slab, part)
        parts.append(part)
    return jnp.concatenate(parts, axis=0).reshape(16, 8, 128)


def exchange_kernel(
    n_k,
    n_e,
    tiles_hbm,
    l_hbm,
    g_hbm,
    c_hbm,
    out_ref,
    tiles_ref,
    l_ref,
    g_ref,
    c_ref,
    gt_ref,
    ct_ref,
    packed,
    weight_ref,
    held,
    sigma,
    back,
    load_sem,
    send_a,
    recv_a,
    send_b,
    recv_b,
):
    count = n_k * n_e
    half = n_e // 2
    my_k = lax.axis_index("ka")
    my_e = lax.axis_index("ea")
    me = my_k * n_e + my_e
    side = my_e // half

    loads = [
        pltpu.make_async_copy(source, target, load_sem.at[index])
        for index, (source, target) in enumerate(
            ((tiles_hbm, tiles_ref), (g_hbm, g_ref), (l_hbm, l_ref), (c_hbm, c_ref))
        )
    ]
    for load in loads:
        load.start()

    k_list = [(my_k + step) % n_k for step in range(n_k)]
    near = [side * half + (my_e + step) % half for step in range(half)]
    far = [(1 - side) * half + (my_e + step) % half for step in range(half)]
    others = [(k, e) for k in k_list for e in far]
    others += [(k, e) for k in k_list for e in near][1:]

    def remote(source, target, send_sem, recv_sem, k, e):
        return pltpu.make_async_remote_copy(
            src_ref=source,
            dst_ref=target,
            send_sem=send_sem,
            recv_sem=recv_sem,
            device_id={"ka": k, "ea": e},
            device_id_type=MESH,
        )

    def all_of(ref, send_sem, recv_sem):
        every = ref.at[pl.ds(0, count - 1)]
        return remote(every, every, send_sem, recv_sem, *others[0])

    barrier = pltpu.get_barrier_semaphore()
    for k, e in others:
        pl.semaphore_signal(barrier, inc=1, device_id={"ka": k, "ea": e}, device_id_type=MESH)

    def spread(ref, pieces):
        for index, piece in enumerate(crossed_rows(pieces)):
            start = index % 2 * 16
            ref[index // 2, start : start + 16] = piece

    def pack(ref):
        return [
            pack_tiles(tiles_ref, lambda blk, row: ref[blk, part, pl.ds(row, 32), :])
            for part in range(2)
        ]

    loads[0].wait()
    loads[1].wait()
    for blk in range(2):
        for part in range(2):
            gt_ref[blk, part] = g_ref[blk, part].T
    greater_rows = pack(gt_ref)
    loads[2].wait()
    spread(packed, pack(l_ref) + greater_rows)
    pl.semaphore_wait(barrier, count - 1)
    for chunk in range(2):
        for k, e in others:
            source = packed.at[chunk, k * n_e + e]
            target = held.at[chunk, me]
            remote(source, target, send_a.at[chunk], recv_a.at[chunk], k, e).start()

    held[0, me] = packed[0, me]
    held[1, me] = packed[1, me]
    loads[3].wait()
    for blk in range(2):
        ct_ref[blk] = c_ref[blk].T
    for kind, ref in ((0, c_ref), (1, ct_ref)):
        bare = pack_tiles(tiles_ref, lambda blk, row: ref[blk, pl.ds(row, 32), :])
        spread(weight_ref.at[kind], [bare * bare * (SIGMA_SCALE / (n_e * n_k))] * 4)

    lags = 2 * n_e - 1
    row = sublane((8, 128))
    top, first_pair = row < 4, row % 4 < 2
    sign = jnp.where(first_pair, 1.0, -1.0)

    def swap(rows):
        return jnp.where(first_pair, rolled(rows, 6), rolled(rows, 2))

    def greens(chunk, pair):
        both = []
        for e in range(n_e):
            one = held[chunk, 2 * pair * n_e + e]
            two = held[chunk, (2 * pair + 1) * n_e + e]
            lesser = jnp.where(top, one, rolled(two, 4))
            both.append((lesser, jnp.where(top, rolled(one, 4), two)))
        return [piece[0] for piece in both], [piece[1] for piece in both]

    def work(chunk, carry):
        all_of(held.at[chunk], send_a.at[chunk], recv_a.at[chunk]).wait_recv()

        def correlate(pair, sums):
            plain, crossed = list(sums[0]), list(sums[1])
            lesser, greater = greens(chunk, pair)
            for e_two in range(n_e):
                swapped = swap(greater[e_two])
                for e_one in range(n_e):
                    lag = e_one - e_two + n_e - 1
                    plain[lag] = plain[lag] + lesser[e_one] * greater[e_two]
                    crossed[lag] = crossed[lag] + lesser[e_one] * swapped
            return tuple(plain), tuple(crossed)

        zero = jnp.zeros((8, 128), jnp.float32)
        plain, crossed = (zero,) * lags, (zero,) * lags
        for pair in range(n_k // 2):
            plain, crossed = correlate(pair, (plain, crossed))
        plain = [total + rolled(total, 4) for total in plain]
        crossed = [total + rolled(total, 4) for total in crossed]
        real = [sign * (total - rolled(total, 2)) for total in plain]
        imag = [-sign * (total + rolled(total, 2)) for total in crossed]
        weights = weight_ref[0, chunk, me], weight_ref[1, chunk, me]

        def convolve(turn, inner):
            pair = (my_k // 2 + turn) % (n_k // 2)
            results = []
            for kind, green in enumerate(greens(chunk, pair)):
                swapped = [swap(piece) for piece in green]
                for e_out in range(n_e):
                    total = None
                    for e_in in range(n_e):
                        lag = e_out - e_in if kind == 0 else e_in - e_out
                        lag = lag + n_e - 1
                        term = green[e_in] * real[lag] + swapped[e_in] * imag[lag]
                        total = term if total is None else total + term
                    results.append(total * weights[kind])
            for e in range(n_e):
                less, more = results[e], results[n_e + e]
                sigma[chunk, 2 * pair * n_e + e] = jnp.where(top, less, rolled(more, 4))
                sigma[chunk, (2 * pair + 1) * n_e + e] = jnp.where(top, rolled(less, 4), more)

            def send(k, e):
                source = sigma.at[chunk, k * n_e + e]
                target = back.at[chunk, me]
                remote(source, target, send_b.at[chunk], recv_b.at[chunk], k, e).start()

            for e in far + near[1:]:
                for k in (2 * pair, 2 * pair + 1):
                    send(k, e)
            for k in (2 * pair, 2 * pair + 1):

                @pl.when(k != my_k)
                def _():
                    send(k, my_e)

            return inner

        lax.fori_loop(0, n_k // 2, convolve, 0)
        back[chunk, me] = sigma[chunk, me]
        return carry

    lax.fori_loop(0, 2, work, 0)
    for chunk in range(2):
        all_of(back.at[chunk], send_b.at[chunk], recv_b.at[chunk]).wait_recv()
        out_ref[chunk] = back[chunk]
    for chunk in range(2):
        all_of(held.at[chunk], send_a.at[chunk], recv_a.at[chunk]).wait_send()
        all_of(back.at[chunk], send_b.at[chunk], recv_b.at[chunk]).wait_send()


def split(value):
    high = value.astype(jnp.bfloat16)
    return high, (value - high.astype(jnp.float32)).astype(jnp.bfloat16)


def square_form(rows):
    real, imag = rows[:, :128], rows[:, 128:]
    return split(jnp.concatenate([rows, jnp.concatenate([-imag, real], axis=1)], axis=0))


def times(first, second, contract=0):
    dims = (((1,), (contract,)), ((), ()))

    def dot(left, right):
        return lax.dot_general(left, right, dims, preferred_element_type=jnp.float32)

    high, low = first
    both = dot(jnp.concatenate([high, low], axis=0), second[0])
    return both[:128] + (dot(high, second[1]) + both[128:])


def adjoint(rows):
    return jnp.concatenate([rows[:, :128].T, -rows[:, 128:].T], axis=1)


def first_step(system, eye):
    real_m, imag_m = system[:, :128], system[:, 128:]
    only_re = jnp.where(eye, real_m, 0.0)
    only_im = jnp.where(eye, imag_m, 0.0)

    def reciprocal(axis):
        real_d = jnp.sum(only_re, axis=axis, keepdims=True)
        imag_d = jnp.sum(only_im, axis=axis, keepdims=True)
        denominator = real_d * real_d + imag_d * imag_d
        return real_d / denominator, -imag_d / denominator

    row_re, row_im = reciprocal(0)
    col_re, col_im = reciprocal(1)
    twice = jnp.where(eye, 2.0, 0.0)
    inner_re = twice - (real_m * row_re - imag_m * row_im)
    inner_im = -(real_m * row_im + imag_m * row_re)
    return jnp.concatenate(
        [col_re * inner_re - col_im * inner_im, col_re * inner_im + col_im * inner_re], axis=1
    )


def sweep_kernel(
    tiles_hbm,
    energy_ref,
    sigma_ref,
    h_ref,
    link_ref,
    contact_ref,
    lesser_ref,
    greater_ref,
    blocks,
    tiles_ref,
    load_sem,
):
    load = pltpu.make_async_copy(tiles_hbm, tiles_ref, load_sem)
    load.start()
    group = lax.broadcasted_iota(jnp.int32, (32, 128), 1) // 32
    pieces = []
    parts = crossed_rows(
        [sigma_ref[index // 2, index % 2 * 16 : index % 2 * 16 + 16] for index in range(4)]
    )
    for kind in range(2):
        for part in range(2):
            packed = parts[2 * kind + part].reshape(128, 128)
            pieces.append((kind, part, packed[64:]))
            for blk in range(2):
                for pos in range(4):
                    blocks[kind, part, blk, 32 * pos : 32 * pos + 32, :] = jnp.where(
                        group == pos, packed[32 * blk : 32 * blk + 32], 0.0
                    )
    load.wait()
    for slot in range(8):
        blk, row, col = tile_place(tiles_ref, 8 + slot)
        start = 32 * (slot // 4)
        rows = pl.ds(pl.multiple_of(32 * row, 32), 32)
        for kind, part, packed in pieces:
            slab = pltpu.roll(packed[start : start + 32], (col + 4 - slot % 4) % 4 * 32, 1)
            blocks[kind, part, blk, rows, :] = jnp.where(
                group == col, slab, blocks[kind, part, blk, rows, :]
            )

    eye = lax.broadcasted_iota(jnp.int32, (128, 128), 0) == lax.broadcasted_iota(
        jnp.int32, (128, 128), 1
    )
    shift = jnp.concatenate(
        [jnp.where(eye, energy_ref[0], 0.0), jnp.where(eye, BROADEN, 0.0)], axis=1
    )

    def rows_of(ref, *index):
        return jnp.concatenate([ref[*index, 0], ref[*index, 1]], axis=1)

    def system_source(blk):
        less = jnp.concatenate([blocks[0, 0, blk], blocks[0, 1, blk]], axis=1)
        more = jnp.concatenate([blocks[1, 0, blk].T, blocks[1, 1, blk].T], axis=1)
        system = shift - rows_of(h_ref, blk) - 0.5 * (more - less)
        return system, less + rows_of(contact_ref, blk)

    twice = jnp.concatenate([jnp.where(eye, 2.0, 0.0), jnp.zeros((128, 128), jnp.float32)], axis=1)
    link = rows_of(link_ref, 0)
    link_square = square_form(link)
    link_adjoint = split(adjoint(link))

    system_0, source_0 = system_source(0)
    system_1, source_1 = system_source(1)
    x_0 = first_step(system_0, eye)
    x_0_square = square_form(x_0)
    product = times(split(system_0), x_0_square)
    left_x = split(times(link_adjoint, x_0_square))
    x_0 = split(x_0)
    through = square_form(2.0 * link - times(split(product), link_square))
    system_1 = system_1 - times(left_x, through)
    rest = square_form(twice - product)
    left_r = times(left_x, rest)
    gr_0 = times(x_0, rest)
    right_op = split(times(x_0, through))
    x_1 = first_step(system_1, eye)
    product = times(split(x_1), square_form(system_1))
    source_0_square = square_form(source_0)
    left_s = split(times(split(left_r), source_0_square))
    left_r = square_form(left_r)
    source_1 = square_form(source_1 + times(left_s, left_r, 1))
    gr_1 = times(split(twice - product), square_form(x_1))
    gr_0_square = square_form(gr_0)
    left_l = square_form(times(left_s, gr_0_square, 1))
    gl_0 = times(split(times(split(gr_0), source_0_square)), gr_0_square, 1)
    gr_1_square = square_form(gr_1)
    middle = times(right_op, gr_1_square)
    middle_rows = split(middle)
    carried = times(middle_rows, source_1)
    cross = times(middle_rows, left_l)
    gl_1 = times(split(times(split(gr_1), source_1)), gr_1_square, 1)
    inner = times(split(carried), square_form(middle), 1)
    full_r = gr_0 + times(middle_rows, left_r)
    full_l = gl_0 + inner - cross - adjoint(cross)
    for blk, retarded, lesser in ((1, gr_1, gl_1), (0, full_r, full_l)):
        greater = lesser + retarded - adjoint(retarded)
        for part in range(2):
            lesser_ref[blk, part] = lesser[:, 128 * part : 128 * part + 128]
            greater_ref[blk, part] = greater[:, 128 * part : 128 * part + 128]


def in_hbm(array):
    return pltpu.with_memory_space_constraint(array, pltpu.HBM)


def small_device(n_k, n_e, lesser_in, greater_in, h_diag, coupling, contact, coulomb, tiles):
    count = n_k * n_e
    f32 = jnp.float32
    limit = pltpu.CompilerParams(vmem_limit_bytes=32 * 1024 * 1024)
    slots = (2, count, 8, 128)
    blocks = pltpu.VMEM((2, 2, 128, 128), f32)
    plane = pltpu.VMEM((2, 128, 128), f32)
    sigma = pl.pallas_call(
        partial(exchange_kernel, n_k, n_e),
        out_shape=jax.ShapeDtypeStruct(slots, f32),
        in_specs=[HBM] * 4,
        out_specs=VMEM,
        scratch_shapes=[pltpu.SMEM((16,), jnp.int32), blocks, blocks, plane, blocks, plane]
        + [pltpu.VMEM(slots, f32), pltpu.VMEM((2,) + slots, f32)]
        + [pltpu.VMEM(slots, f32)] * 3
        + [pltpu.SemaphoreType.DMA((4,))]
        + [pltpu.SemaphoreType.DMA((2,))] * 4,
        compiler_params=pltpu.CompilerParams(
            collective_id=0, has_side_effects=True, vmem_limit_bytes=32 * 1024 * 1024
        ),
        name="exchange",
    )(*(in_hbm(array) for array in (tiles, lesser_in[0, 0], greater_in[0, 0], coulomb)))
    energy = -SPREAD + 2.0 * SPREAD * (lax.axis_index("ea").astype(f32) + 0.5) / n_e
    lesser, greater = pl.pallas_call(
        sweep_kernel,
        out_shape=(jax.ShapeDtypeStruct((2, 2, 128, 128), f32),) * 2,
        in_specs=[HBM, SMEM, VMEM, VMEM, VMEM, VMEM],
        out_specs=(VMEM, VMEM),
        scratch_shapes=[
            pltpu.VMEM((2, 2, 2, 128, 128), f32),
            pltpu.SMEM((16,), jnp.int32),
            pltpu.SemaphoreType.DMA,
        ],
        compiler_params=limit,
        name="sweep",
    )(
        in_hbm(tiles),
        energy.reshape(1),
        sigma,
        h_diag[0],
        coupling[0],
        contact[0, 0],
    )
    return lesser[None, None], greater[None, None]


def per_device(mesh, lesser_in, *rest):
    n_k, n_e = mesh.shape["ka"], mesh.shape["ea"]
    fits = n_k * n_e == 32 and lesser_in.shape == (1, 1, 2, 2, 128, 128) and rest[-1].shape == (16,)
    if fits:
        return small_device(n_k, n_e, lesser_in, *rest)
    return on_device(lesser_in, *rest)


def solution(mesh):
    in_specs = (
        P("ka", "ea", None, None, None, None),
        P("ka", "ea", None, None, None, None),
        P("ka", None, None, None, None),
        P("ka", None, None, None, None),
        P("ka", "ea", None, None, None, None),
        P(),
        P(),
    )
    out_specs = (P("ka", "ea", None, None, None, None), P("ka", "ea", None, None, None, None))
    return jax.shard_map(
        partial(per_device, mesh), mesh=mesh, in_specs=in_specs, out_specs=out_specs, check_vma=False
    )
```
